32 devices in a mesh: ctx: 2 (over x), chan: 4 (over z), dp: 4 (over y, core).
Axes of the slice: x: 2, y: 2, z: 4, core: 2. Of those that a mesh axis runs over, the one named last changes fastest.
Arguments:
- projected: bfloat16 [3, 1024, 8192], P(None, ('dp', 'ctx'), 'chan'), parts along dimension 1, may hold values from -6 to 6
- short_weight: float32 [7, 3, 8192], P(None, None, 'chan'), may hold values from -2 to 2
- pos_in: float32 [33, 64], replicated, may hold values from -1 to 1
- pos_bias: float32 [64], replicated, may hold values from -4 to 4
- sine_freq: float32 [64], replicated, may hold values from 1.5 to 3
- pos_mid: float32 [64, 64], replicated, may hold values from -0.75 to 0.75
- pos_out: float32 [64, 8192], P(None, 'chan'), may hold values from -0.75 to 0.75
- decay_rate: float32 [8192], P('chan'), may hold values from 0.000390625 to 0.05
- skip_gain: float32 [8192], P('chan'), may hold values from -4 to 4
Outputs:
- mixed: bfloat16 [1024, 8192], P(('dp', 'ctx'), 'chan'), parts along dimension 0
The draws below stay inside these ranges and needn't reach their ends.
There are 4 independent parts, one for each index of `dp`. The reference program is written for one: setup_inputs(seed, part) draws one part's arguments, and reference() takes and returns one part's arrays. A program takes and returns all parts, laid end to end along the dimension named above; an argument that names none is the same for every part. Nothing has to cross between parts.
All inputs are finite; a program needn't handle non-finite values.
Results may differ from the reference program's by a relative error of at most 0.001.
Values may be sent and summed in bfloat16 or wider, within the bound.
No kernel may reach another device: no remote copies, remote signals or barrier semaphores. Data moves between devices by JAX's collectives and lax.ppermute only.
A program may use at most 128 MiB of HBM per device.

```python
import math
import jax
import jax.numpy as jnp
from jax import lax

D = 8192
ORDER = 64
BANDS = 16
TAPS = 7
FEAT = 33
LEN = 256


def draw_decay_rate(key, part):
    level_key = jax.random.fold_in(key, 0)
    lowest = jnp.log(jnp.float32(0.1 / LEN))
    highest = jnp.log(jnp.float32(0.05))
    levels = jax.random.uniform(level_key, (D,), jnp.float32)
    return jnp.exp(lowest + levels * (highest - lowest))


def shard_levels(stream_key, dims, cuts, low, largest):
    gain = 1.0
    for axis_at, parts in cuts:
        heights = jax.random.uniform(jax.random.fold_in(jax.random.fold_in(stream_key, 6), axis_at), (parts,), jnp.float32, low / len(cuts), largest / len(cuts))
        gain = gain * jnp.repeat(jnp.exp(heights), dims[axis_at] // parts).reshape((-1,) + (1,) * (len(dims) - 1 - axis_at))
    return gain


def centred(stream_key, shape, deviation, reach, cuts=(), held_as=jnp.bfloat16):
    loudness = shard_levels(stream_key, shape, cuts, -0.22, 0.18) if cuts else 1.0
    drawn = jax.random.normal(stream_key, shape, jnp.float32) * deviation * loudness
    return jnp.minimum(jnp.maximum(drawn, -reach), reach).astype(held_as)


def setup_inputs(seed: int = 0, part: int = 0) -> dict:
    seeds = jax.random.split(jax.random.key(seed), 10)
    part_splits = jax.random.split(jax.random.fold_in(seeds[9], part), 10)
    projected = centred(part_splits[0], (3, LEN, D), 1.0, 6.0, ((1, 2), (2, 4)))
    short_weight = centred(seeds[1], (TAPS, 3, D), TAPS ** -0.5, 2.0, ((2, 4),), jnp.float32)
    pos_in = jnp.clip(jax.random.uniform(seeds[2], (FEAT, ORDER), jnp.float32, -1.0, 1.0), -1.0, 1.0)
    pos_bias = centred(seeds[3], (ORDER,), 1.0, 4.0, (), jnp.float32)
    sine_freq = jnp.clip(jax.random.uniform(seeds[4], (ORDER,), jnp.float32, 1.5, 3.0), 1.5, 3.0)
    pos_mid = jnp.clip(jax.random.uniform(seeds[5], (ORDER, ORDER), jnp.float32, -0.75, 0.75), -0.75, 0.75)
    pos_out = centred(seeds[6], (ORDER, D), ORDER ** -0.5, 0.75, ((1, 4),), jnp.float32)
    decay_rate = draw_decay_rate(jax.random.fold_in(seeds[9], 71), part)
    skip_gain = centred(seeds[8], (D,), 1.0, 4.0, ((0, 4),), jnp.float32)
    return {"projected": projected, "short_weight": short_weight, "pos_in": pos_in, "pos_bias": pos_bias, "sine_freq": sine_freq, "pos_mid": pos_mid, "pos_out": pos_out, "decay_rate": decay_rate, "skip_gain": skip_gain}


def features(positions, total_len):
    band_ids = jnp.arange(1, BANDS + 1, dtype=jnp.float32)
    angles = positions[:, None] * band_ids[None, :] * (2.0 * math.pi / total_len)
    return jnp.concatenate([positions[:, None] / total_len, jnp.cos(angles), jnp.sin(angles)], axis=1)

def filter_rows(positions, total_len, pos_in, pos_bias, sine_freq, pos_mid, pos_out, decay_rate):
    highest = lax.Precision.HIGHEST
    inputs = features(positions, total_len)
    first_layer = jnp.sin(sine_freq * (jnp.dot(inputs, pos_in, precision=highest, preferred_element_type=jnp.float32) + pos_bias))
    second_layer = jnp.sin(sine_freq * jnp.dot(first_layer, pos_mid, precision=highest, preferred_element_type=jnp.float32))
    raw_filter = jnp.dot(second_layer, pos_out, precision=highest, preferred_element_type=jnp.float32)
    return raw_filter * jnp.exp(-decay_rate[None, :] * positions[:, None])

def short_conv(projected, short_weight):
    padded = jnp.pad(projected.astype(jnp.float32), ((0, 0), (TAPS - 1, 0), (0, 0)))
    summed = jnp.zeros(projected.shape, jnp.float32)
    for tap_index in range(TAPS):
        offset = TAPS - 1 - tap_index
        summed = summed + short_weight[tap_index][:, None, :] * padded[:, offset:offset + LEN, :]
    return summed

def causal_conv(normed, driven):
    channel_count = normed.shape[1]
    block_width = math.gcd(channel_count, 512)
    block_count = channel_count // block_width

    def one_block(block_index):
        offset = block_index * block_width
        filter_part = lax.dynamic_slice_in_dim(normed, offset, block_width, 1)
        signal_part = lax.dynamic_slice_in_dim(driven, offset, block_width, 1)
        signal_spec = jnp.fft.rfft(signal_part, n=2 * LEN, axis=0)
        filter_spec = jnp.fft.rfft(filter_part, n=2 * LEN, axis=0)
        return jnp.fft.irfft(signal_spec * filter_spec, n=2 * LEN, axis=0)[:LEN].astype(jnp.float32)
    results = lax.map(one_block, jnp.arange(block_count, dtype=jnp.int32))
    return jnp.moveaxis(results, 0, 1).reshape(LEN, channel_count)

def reference(projected, short_weight, pos_in, pos_bias, sine_freq, pos_mid, pos_out, decay_rate, skip_gain):
    short_out = short_conv(projected, short_weight)
    left_gate, right_gate, value_stream = (short_out[0], short_out[1], short_out[2])
    driven = left_gate * value_stream
    positions = jnp.arange(LEN, dtype=jnp.float32)
    long_filter = filter_rows(positions, LEN, pos_in, pos_bias, sine_freq, pos_mid, pos_out, decay_rate)
    normed = long_filter / jnp.sqrt(lax.optimization_barrier(jnp.sum(long_filter * long_filter, axis=0)) + 1e-05)
    long_conv = causal_conv(normed, driven)
    return (right_gate * (long_conv + skip_gain[None, :] * driven)).astype(jnp.bfloat16)
```

```python
import functools
import math

import jax
import jax.numpy as jnp
import numpy as np
from jax import lax
from jax.experimental import pallas as pl
from jax.experimental.pallas import tpu as pltpu
from jax.sharding import PartitionSpec as P

BANDS = 16
TAPS = 7
SPAN = 250.0
TINY = 1e-30

HIGHEST = lax.Precision.HIGHEST


def shifted(x, axis, by):
    size = lax.axis_size(axis)
    pairs = [(i, i + by) for i in range(size) if 0 <= i + by < size]
    return lax.ppermute(x, axis, pairs)


def features(positions, total_len):
    band_ids = jnp.arange(1, BANDS + 1, dtype=jnp.float32)
    angles = positions[:, None] * band_ids[None, :] * (2.0 * math.pi / total_len)
    return jnp.concatenate(
        [positions[:, None] / total_len, jnp.cos(angles), jnp.sin(angles)], axis=1
    )


def second_rows(positions, total_len, pos_in, pos_bias, sine_freq, pos_mid):
    inputs = features(positions, total_len)
    first_layer = jnp.sin(
        sine_freq
        * (
            jnp.dot(inputs, pos_in, precision=HIGHEST, preferred_element_type=jnp.float32)
            + pos_bias
        )
    )
    return jnp.sin(
        sine_freq
        * jnp.dot(first_layer, pos_mid, precision=HIGHEST, preferred_element_type=jnp.float32)
    )


def filter_rows(positions, total_len, pos_in, pos_bias, sine_freq, pos_mid, pos_out, decay_rate):
    second_layer = second_rows(positions, total_len, pos_in, pos_bias, sine_freq, pos_mid)
    raw_filter = jnp.dot(
        second_layer, pos_out, precision=HIGHEST, preferred_element_type=jnp.float32
    )
    return raw_filter * jnp.exp(-decay_rate[None, :] * positions[:, None])


def halves(x):
    high = x.astype(jnp.bfloat16)
    low = (x - high.astype(jnp.float32)).astype(jnp.bfloat16)
    return high, low


def table_columns(table):
    high = table.astype(jnp.bfloat16)
    low = (table - high.astype(np.float32)).astype(jnp.bfloat16)
    return np.concatenate([high, high, low], axis=1)


def spread(x):
    high, low = halves(x)
    return jnp.concatenate([high, low, high], axis=0)


def product(table, x):
    return jnp.dot(table, spread(x), preferred_element_type=jnp.float32)


def odd_tables(rows):
    turns = (2 * np.arange(rows)[:, None] + 1) * np.arange(rows)[None, :] % (4 * rows)
    angles = turns * (np.pi / (2 * rows))
    forward = np.concatenate([np.cos(angles), -np.sin(angles)], axis=0)
    backward = forward.T / rows
    return table_columns(forward.astype(np.float32)), table_columns(backward.astype(np.float32))


def short_sum(rim, rows, taps):
    x = jnp.concatenate([rim, rows], axis=0)
    before = pltpu.roll(x, 1, 0)
    total = taps[6] * x
    for at in (4, 2, 0):
        total = taps[at] * x + taps[at + 1] * before + pltpu.roll(total, 2, 0)
    return total[8:]


def encode_kernel(left_ref, right_ref, stream_ref, taps_ref, coded_ref, side_ref):
    @pl.when(lax.axis_index("ctx") == 0)
    def _():
        count = coded_ref.shape[1] // 128
        for lane in range(count):
            cols = pl.ds(lane * 128, 128)
            left = left_ref[0, :, cols].astype(jnp.float32)
            stream = stream_ref[0, :, cols].astype(jnp.float32)
            nothing = jnp.zeros((8, 128), jnp.float32)
            left_taps = [taps_ref[k, 0:1, cols] for k in range(TAPS)]
            stream_taps = [taps_ref[k, 2:3, cols] for k in range(TAPS)]
            driven = short_sum(nothing, left, left_taps) * short_sum(nothing, stream, stream_taps)
            size = jnp.abs(driven)
            level = jnp.maximum(jnp.max(size, axis=0, keepdims=True), TINY)
            level = level.astype(jnp.bfloat16).astype(jnp.float32)
            coded = jnp.exp2(size * (SPAN / level) - SPAN / 2)
            coded_ref[:, cols] = jnp.where(driven < 0, -coded, coded).astype(jnp.bfloat16)
            place = lax.broadcasted_iota(jnp.int32, (8, 128), 0)
            rims = [left[-8:], right_ref[0, :, cols].astype(jnp.float32)[-8:], stream[-8:]]
            rims = [jnp.where(place < 2, level, rim) for rim in rims]
            side_ref[:, cols] = jnp.concatenate(rims, axis=0).astype(jnp.bfloat16)


def filter_kernel(second_ref, out_ref, decay_ref, forward_ref, near_ref, far_ref):
    rows = near_ref.shape[0] // 2
    width = near_ref.shape[1]
    second_high, second_low = halves(second_ref[...])
    second = jnp.concatenate([second_high, second_high, second_low], axis=1)
    raw = jnp.dot(second, spread(out_ref[...]), preferred_element_type=jnp.float32)
    places = lax.broadcasted_iota(jnp.int32, (2 * rows, width), 0).astype(jnp.float32)
    taps = raw * jnp.exp(-decay_ref[...] * places)
    taps = taps * (1.0 / jnp.sqrt(jnp.sum(taps * taps, axis=0, keepdims=True) + 1e-05))
    forward = forward_ref[...]
    low = product(forward, taps[:rows])
    high = product(forward, taps[rows:])
    near_ref[...] = low
    odd = lax.broadcasted_iota(jnp.int32, (rows, width), 0) % 2 == 1
    real, imag = low[:rows], low[rows:]
    far_ref[:rows] = high[:rows] + jnp.where(odd, imag, -imag)
    far_ref[rows:] = high[rows:] + jnp.where(odd, -real, real)


def spectrum_product(one_real, one_imag, two_real, two_imag):
    return one_real * two_real - one_imag * two_imag, one_real * two_imag + one_imag * two_real


def own_kernel(
    projected_ref, side_ref, taps_ref, skip_ref, near_ref, forward_ref, backward_ref, base_ref, right_ref,
    driven_ref,
):
    rows, width = base_ref.shape
    for lane in range(width // 128):
        cols = pl.ds(lane * 128, 128)
        sums = []
        for at in range(3):
            rim = side_ref[8 * at : 8 * at + 8, cols].astype(jnp.float32)
            stream = projected_ref[at, :, cols].astype(jnp.float32)
            sums.append(short_sum(rim, stream, [taps_ref[k, at : at + 1, cols] for k in range(TAPS)]))
        driven_ref[:, cols] = sums[0] * sums[2]
        right_ref[:, cols] = sums[1]
    driven = driven_ref[...]
    spec = product(forward_ref[...], driven)
    real, imag = spectrum_product(spec[:rows], spec[rows:], near_ref[:rows], near_ref[rows:])
    conv = product(backward_ref[...], jnp.concatenate([real, imag], axis=0))
    base_ref[...] = conv + skip_ref[...] * driven


def join_kernel(
    coded_ref, side_ref, far_ref, base_ref, right_ref, forward_ref, backward_ref, earlier_ref, mixed_ref
):
    rows, width = base_ref.shape
    place = lax.axis_index("ctx")

    @pl.when(place == 0)
    def _():
        mixed_ref[...] = (right_ref[...] * base_ref[...]).astype(jnp.bfloat16)

    @pl.when(place != 0)
    def _():
        coded = coded_ref[...].astype(jnp.float32)
        level = side_ref[0:1].astype(jnp.float32)
        size = (jnp.log(jnp.abs(coded)) * (1.0 / math.log(2.0)) + SPAN / 2) * (level / SPAN)
        earlier = jnp.where(coded < 0, -size, size)
        spec = product(forward_ref[...], earlier)
        real, imag = spectrum_product(spec[:rows], spec[rows:], far_ref[:rows], far_ref[rows:])
        conv = product(backward_ref[...], jnp.concatenate([real, imag], axis=0))
        mixed_ref[...] = (right_ref[...] * (conv + base_ref[...])).astype(jnp.bfloat16)


def params(mib=40):
    return pltpu.CompilerParams(vmem_limit_bytes=mib * 1024 * 1024)


def cost(us):
    return pl.CostEstimate(flops=int(us * 1e9), bytes_accessed=int(us * 3e6), transcendentals=0)


def one_way(
    projected, short_weight, pos_in, pos_bias, sine_freq, pos_mid, pos_out, decay_rate, skip_gain
):
    _, rows, width = projected.shape
    total_len = 2 * rows
    block = math.gcd(width, 512)
    steps = width // block
    half = width // 2
    forward, backward = odd_tables(rows)
    decay_row = decay_rate[None, :]
    skip_row = skip_gain[None, :]

    def cols(*lead, first=0):
        fixed = (0,) * len(lead)
        return pl.BlockSpec(tuple(lead) + (block,), lambda j: fixed + (j + first,))

    def whole(array):
        return pl.BlockSpec(array.shape, lambda j: (0,) * array.ndim)

    last = rows // 16 - 1
    coded, side = pl.pallas_call(
        encode_kernel,
        grid=(steps,),
        in_specs=[
            pl.BlockSpec((1, rows, block), lambda j: (0, 0, j)),
            pl.BlockSpec((1, 16, block), lambda j: (1, last, j)),
            pl.BlockSpec((1, rows, block), lambda j: (2, 0, j)),
            cols(TAPS, 3),
        ],
        out_specs=[cols(rows), cols(24)],
        out_shape=[
            jax.ShapeDtypeStruct((rows, width), jnp.bfloat16),
            jax.ShapeDtypeStruct((24, width), jnp.bfloat16),
        ],
        compiler_params=params(),
        cost_estimate=cost(2),
        name="encode",
    )(projected, projected, projected, short_weight)
    side = lax.ppermute(side, "ctx", [(0, 1)])
    coded = lax.ppermute(coded, "ctx", [(0, 1)])

    positions = jnp.arange(total_len, dtype=jnp.int32).astype(jnp.float32)
    second = second_rows(positions, total_len, pos_in, pos_bias, sine_freq, pos_mid)
    near, far = pl.pallas_call(
        filter_kernel,
        grid=(steps,),
        in_specs=[whole(second), cols(pos_out.shape[0]), cols(1), whole(forward)],
        out_specs=[cols(total_len), cols(total_len)],
        out_shape=[jax.ShapeDtypeStruct((total_len, width), jnp.float32)] * 2,
        compiler_params=params(),
        cost_estimate=cost(3),
        name="filter",
    )(second, pos_out, decay_row, forward)
    base, right = pl.pallas_call(
        own_kernel,
        grid=(steps,),
        in_specs=[
            cols(3, rows), cols(24), cols(TAPS, 3), cols(1), cols(total_len), whole(forward), whole(backward),
        ],
        out_specs=[cols(rows), cols(rows)],
        out_shape=[jax.ShapeDtypeStruct((rows, width), jnp.float32)] * 2,
        scratch_shapes=[pltpu.VMEM((rows, block), jnp.float32)],
        compiler_params=params(),
        cost_estimate=cost(3),
        name="own",
    )(projected, side, short_weight, skip_row, near, forward, backward)
    mixed = pl.pallas_call(
        functools.partial(lambda *refs: join_kernel(*refs[:7], None, refs[7])),
        grid=(steps,),
        in_specs=[
            cols(rows), cols(24), cols(total_len), cols(rows), cols(rows), whole(forward), whole(backward),
        ],
        out_specs=cols(rows),
        out_shape=jax.ShapeDtypeStruct((rows, width), jnp.bfloat16),
        compiler_params=params(),
        cost_estimate=cost(2),
        name="join",
    )(coded, side, far, base, right, forward, backward)
    return mixed


def turn_table(outer_ids, inner_ids, modulus):
    product_grid = outer_ids[:, None] * inner_ids[None, :] % modulus
    angles = product_grid.astype(jnp.float32) * (2.0 * math.pi / modulus)
    return (jnp.cos(angles), jnp.sin(angles))


def section_outer(table, data):
    return jnp.einsum(
        "ka,cab->ckb", table, data, precision=HIGHEST, preferred_element_type=jnp.float32
    )


def section_inner(table, data):
    return jnp.einsum(
        "ckb,bj->ckj", data, table, precision=HIGHEST, preferred_element_type=jnp.float32
    )


def padded_spectrum(signal, outer_count, inner_count, tables):
    cos_half, sin_half, cos_twist, sin_twist, cos_inner, sin_inner = tables
    shaped = signal.reshape(signal.shape[0], outer_count // 2, inner_count)
    real_one = section_outer(cos_half, shaped)
    imag_one = -section_outer(sin_half, shaped)
    real_two = real_one * cos_twist + imag_one * sin_twist
    imag_two = imag_one * cos_twist - real_one * sin_twist
    spec_real = section_inner(cos_inner, real_two) + section_inner(sin_inner, imag_two)
    spec_imag = section_inner(cos_inner, imag_two) - section_inner(sin_inner, real_two)
    return (spec_real, spec_imag)


def causal_local(driven_cols, normed_cols, total_len):
    full_len = 2 * total_len
    inner_count = math.gcd(total_len, 128)
    outer_count = full_len // inner_count
    outer_full = jnp.arange(outer_count, dtype=jnp.int32)
    outer_half = jnp.arange(outer_count // 2, dtype=jnp.int32)
    inner_ids = jnp.arange(inner_count, dtype=jnp.int32)
    cos_half, sin_half = turn_table(outer_full, outer_half, outer_count)
    cos_twist, sin_twist = turn_table(outer_full, inner_ids, full_len)
    cos_inner, sin_inner = turn_table(inner_ids, inner_ids, inner_count)
    tables = (cos_half, sin_half, cos_twist, sin_twist, cos_inner, sin_inner)
    sig_real, sig_imag = padded_spectrum(driven_cols, outer_count, inner_count, tables)
    fil_real, fil_imag = padded_spectrum(normed_cols, outer_count, inner_count, tables)
    prod_real = sig_real * fil_real - sig_imag * fil_imag
    prod_imag = sig_real * fil_imag + sig_imag * fil_real
    back_real = section_inner(cos_inner, prod_real) - section_inner(sin_inner, prod_imag)
    back_imag = section_inner(sin_inner, prod_real) + section_inner(cos_inner, prod_imag)
    turned_real = back_real * cos_twist - back_imag * sin_twist
    turned_imag = back_real * sin_twist + back_imag * cos_twist
    cos_last, sin_last = turn_table(outer_half, outer_full, outer_count)
    result = (
        section_outer(cos_last, turned_real) - section_outer(sin_last, turned_imag)
    ) / full_len
    return result.reshape(driven_cols.shape[0], total_len)


def exchanged(
    projected, short_weight, pos_in, pos_bias, sine_freq, pos_mid, pos_out, decay_rate, skip_gain
):
    ctx_count = lax.axis_size("ctx")
    ctx_place = lax.axis_index("ctx")
    block_rows = projected.shape[1]
    total_len = block_rows * ctx_count
    rim_rows = shifted(projected[:, block_rows - (TAPS - 1) :, :], "ctx", 1)
    extended = jnp.concatenate([rim_rows, projected], axis=1)
    short_out = jnp.zeros(projected.shape, jnp.float32)
    for tap_index in range(TAPS):
        offset = TAPS - 1 - tap_index
        short_out = short_out + short_weight[tap_index][:, None, :] * extended[
            :, offset : offset + block_rows, :
        ].astype(jnp.float32)
    left_gate, right_gate, value_stream = (short_out[0], short_out[1], short_out[2])
    driven = left_gate * value_stream
    own_width = driven.shape[1] // ctx_count
    driven_cols = lax.all_to_all(driven.T, "ctx", split_axis=0, concat_axis=1, tiled=True)
    own_out = lax.dynamic_slice_in_dim(pos_out, ctx_place * own_width, own_width, 1)
    own_decay = lax.dynamic_slice_in_dim(decay_rate, ctx_place * own_width, own_width, 0)
    positions = jnp.arange(total_len, dtype=jnp.int32).astype(jnp.float32)
    long_filter = filter_rows(
        positions, total_len, pos_in, pos_bias, sine_freq, pos_mid, own_out, own_decay
    )
    normed = long_filter / jnp.sqrt(jnp.sum(long_filter * long_filter, axis=0) + 1e-05)
    conv_cols = causal_local(driven_cols, normed.T, total_len)
    long_conv = lax.all_to_all(conv_cols, "ctx", split_axis=1, concat_axis=0, tiled=True).T
    return (right_gate * (long_conv + skip_gain[None, :] * driven)).astype(jnp.bfloat16)


def body(projected, *others):
    if lax.axis_size("ctx") == 2:
        return one_way(projected, *others)
    return exchanged(projected, *others)


def solution(mesh):
    placed = (
        P(None, ("dp", "ctx"), "chan"),
        P(None, None, "chan"),
        P(),
        P(),
        P(),
        P(),
        P(None, "chan"),
        P("chan"),
        P("chan"),
    )
    return jax.shard_map(
        body, mesh=mesh, in_specs=placed, out_specs=P(("dp", "ctx"), "chan"), check_vma=False
    )
```

```python
import functools
import math

import jax
import jax.numpy as jnp
import numpy as np
from jax import lax
from jax.experimental import pallas as pl
from jax.experimental.pallas import tpu as pltpu
from jax.sharding import PartitionSpec as P

BANDS = 16
TAPS = 7
SPAN = 250.0
TINY = 1e-30

HIGHEST = lax.Precision.HIGHEST


def shifted(x, axis, by):
    size = lax.axis_size(axis)
    pairs = [(i, i + by) for i in range(size) if 0 <= i + by < size]
    return lax.ppermute(x, axis, pairs)


def features(positions, total_len):
    band_ids = jnp.arange(1, BANDS + 1, dtype=jnp.float32)
    angles = positions[:, None] * band_ids[None, :] * (2.0 * math.pi / total_len)
    return jnp.concatenate(
        [positions[:, None] / total_len, jnp.cos(angles), jnp.sin(angles)], axis=1
    )


def second_rows(positions, total_len, pos_in, pos_bias, sine_freq, pos_mid):
    inputs = features(positions, total_len)
    first_layer = jnp.sin(
        sine_freq
        * (
            jnp.dot(inputs, pos_in, precision=HIGHEST, preferred_element_type=jnp.float32)
            + pos_bias
        )
    )
    return jnp.sin(
        sine_freq
        * jnp.dot(first_layer, pos_mid, precision=HIGHEST, preferred_element_type=jnp.float32)
    )


def filter_rows(positions, total_len, pos_in, pos_bias, sine_freq, pos_mid, pos_out, decay_rate):
    second_layer = second_rows(positions, total_len, pos_in, pos_bias, sine_freq, pos_mid)
    raw_filter = jnp.dot(
        second_layer, pos_out, precision=HIGHEST, preferred_element_type=jnp.float32
    )
    return raw_filter * jnp.exp(-decay_rate[None, :] * positions[:, None])


def halves(x):
    high = x.astype(jnp.bfloat16)
    low = (x - high.astype(jnp.float32)).astype(jnp.bfloat16)
    return high, low


def table_columns(table):
    high = table.astype(jnp.bfloat16)
    low = (table - high.astype(np.float32)).astype(jnp.bfloat16)
    return np.concatenate([high, high, low], axis=1)


def spread(x):
    high, low = halves(x)
    return jnp.concatenate([high, low, high], axis=0)


def product(table, x):
    return jnp.dot(table, spread(x), preferred_element_type=jnp.float32)


def strided_order(rows):
    place = np.arange(rows)
    return place % 8 * (rows // 8) + place // 8


def odd_tables(rows):
    turns = (2 * np.arange(rows)[:, None] + 1) * np.arange(rows)[None, :] % (4 * rows)
    angles = turns * (np.pi / (2 * rows))
    forward = np.concatenate([np.cos(angles), -np.sin(angles)], axis=0)
    backward = forward.T / rows
    strided = forward[:, strided_order(rows)]
    return tuple(table_columns(table.astype(np.float32)) for table in (forward, strided, backward))


def strided_rows(values, buf):
    buf[...] = values.astype(jnp.float32)
    count = buf.shape[0] // 8
    return [buf[pl.ds(v, 8, stride=count), :] for v in range(count)]


def short_sum(parts, rim, taps_ref, at, cols):
    top = lax.broadcasted_iota(jnp.int32, (8, 128), 0) == 0
    before = {}
    for back in range(1, TAPS):
        edge = 0.0 if rim is None else rim[8 - back : 9 - back]
        before[-back] = jnp.where(top, edge, pltpu.roll(parts[-back], 1, 0))
    taps = [jnp.broadcast_to(taps_ref[at, k : k + 1, cols], (8, 128)) for k in range(TAPS)]
    sums = []
    for v in range(len(parts)):
        terms = [taps[k] * (parts[v - k] if v >= k else before[v - k]) for k in range(TAPS)]
        sums.append(((terms[0] + terms[1]) + (terms[2] + terms[3])) + ((terms[4] + terms[5]) + terms[6]))
    return sums


def lanes(first, size=128):
    return pl.ds(pl.multiple_of(first, 128), size)


def paired(values):
    return [jnp.concatenate(values[i : i + 2], axis=0) for i in range(0, len(values), 2)]


def encode_kernel(projected_ref, taps_ref, *refs):
    *coded_refs, side_ref, rows_buf, rim_buf, taps_buf, strided_buf, sems = refs
    width = projected_ref.shape[2]
    block = strided_buf.shape[1] * 128

    @pl.when(lax.axis_index("ctx") == 0)
    def _():
        last = projected_ref.shape[1] - 16
        small = [
            pltpu.make_async_copy(taps_ref, taps_buf, sems.at[width // block, 0]),
            pltpu.make_async_copy(projected_ref.at[1, pl.ds(last, 16)], rim_buf, sems.at[width // block, 1]),
        ]

        def large(at, way):
            cols = lanes(at * block, block)
            return pltpu.make_async_copy(
                projected_ref.at[2 * way, :, cols], rows_buf.at[way, :, cols], sems.at[at, way]
            )

        small[0].start()
        for at in range(width // block):
            large(at, 0).start()
            large(at, 1).start()
            if at == 0:
                small[1].start()
        small[0].wait()
        small[1].wait()
        first = 0
        for coded_ref in coded_refs:

            def one_block(at, _, coded_ref=coded_ref, first=first):
                large(at, 0).wait()
                large(at, 1).wait()
                for number in range(block // 128):
                    cols = lanes(at * block + number * 128)
                    left = rows_buf[0, :, cols]
                    stream = rows_buf[1, :, cols]
                    left_sums = short_sum(strided_rows(left, strided_buf.at[0, number]), None, taps_buf, 0, cols)
                    stream_sums = short_sum(
                        strided_rows(stream, strided_buf.at[1, number]), None, taps_buf, 2, cols
                    )
                    driven = [one * two for one, two in zip(left_sums, stream_sums)]
                    sizes = [jnp.abs(value) for value in driven]
                    level = functools.reduce(jnp.maximum, sizes)
                    level = jnp.maximum(jnp.max(level, axis=0, keepdims=True), TINY)
                    level = level.astype(jnp.bfloat16).astype(jnp.float32)
                    gain = jnp.broadcast_to(SPAN / level, (8, 128))
                    coded = [jnp.exp2(size * gain - SPAN / 2) for size in sizes]
                    coded = [jnp.where(value < 0, -code, code) for value, code in zip(driven, coded)]
                    there = lanes(at * block + number * 128 - first)
                    for pair, rows in enumerate(paired(coded)):
                        coded_ref[16 * pair : 16 * pair + 16, there] = rows.astype(jnp.bfloat16)
                    place = lax.broadcasted_iota(jnp.int32, (8, 128), 0)
                    rims = [left[-16:], rim_buf[:, cols], stream[-16:]]
                    rims = [jnp.where(place < 2, level, rim.astype(jnp.float32)[8:]) for rim in rims]
                    side_ref[:, cols] = jnp.concatenate(rims, axis=0).astype(jnp.bfloat16)
                return 0

            lax.fori_loop(first // block, (first + coded_ref.shape[1]) // block, one_block, 0)
            first += coded_ref.shape[1]


def filter_kernel(second_ref, out_ref, decay_ref, skip_ref, forward_ref, near_ref, far_ref):
    rows = near_ref.shape[0] // 2
    width = near_ref.shape[1]
    second_high, second_low = halves(second_ref[...])
    second = jnp.concatenate([second_high, second_high, second_low], axis=1)
    raw = jnp.dot(second, spread(out_ref[...]), preferred_element_type=jnp.float32)
    places = lax.broadcasted_iota(jnp.int32, (2 * rows, width), 0).astype(jnp.float32)
    taps = raw * jnp.exp(-decay_ref[...] * places)
    taps = taps * (1.0 / jnp.sqrt(jnp.sum(taps * taps, axis=0, keepdims=True) + 1e-05))
    forward = forward_ref[...]
    low = product(forward, taps[:rows])
    high = product(forward, taps[rows:])
    odd = lax.broadcasted_iota(jnp.int32, (rows, width), 0) % 2 == 1
    real, imag = low[:rows], low[rows:]
    near_ref[:rows] = real + skip_ref[...]
    near_ref[rows:] = imag
    far_ref[:rows] = high[:rows] + jnp.where(odd, imag, -imag)
    far_ref[rows:] = high[rows:] + jnp.where(odd, -real, real)


def convolved(spec, filter_ref, cols, backward):
    rows = spec.shape[0] // 2
    real, imag = spec[:rows], spec[rows:]
    filter_real, filter_imag = filter_ref[:rows, cols], filter_ref[rows:, cols]
    both = [real * filter_real - imag * filter_imag, real * filter_imag + imag * filter_real]
    return product(backward, jnp.concatenate(both, axis=0))


def own_kernel(
    projected_ref, side_ref, taps_ref, near_ref, strided_ref, backward_ref, base_ref, right_ref, mixed_ref,
    strided_buf, mixed_buf, sems,
):
    rows, width = base_ref.shape
    block = strided_buf.shape[0] * 128
    strided, backward = strided_ref[...], backward_ref[...]

    def driven_rows(first, bufs):
        blocks = []
        for number in range(2):
            cols = lanes(first + number * 128)
            sums = []
            for at in range(3):
                buf = bufs.at[number, at]
                rim = side_ref[8 * at : 8 * at + 8, cols].astype(jnp.float32)
                sums.append(
                    short_sum(strided_rows(projected_ref[at, :, cols], buf), rim, taps_ref, at, cols)
                )
            back = bufs.at[number, 3]
            for v, value in enumerate(sums[1]):
                back[pl.ds(v, 8, stride=rows // 8), :] = value
            right_ref[:, cols] = back[...]
            blocks.append(jnp.concatenate([one * two for one, two in zip(sums[0], sums[2])], axis=0))
        return jnp.concatenate(blocks, axis=1)

    def finish(first, spec):
        cols = lanes(first, 256)
        base = convolved(spec, near_ref, cols, backward)
        base_ref[:, cols] = base
        mixed_buf[:, cols] = (right_ref[:, cols] * base).astype(jnp.bfloat16)

    def one_block(at, _):
        first = at * block
        specs = []
        for piece in range(block // 256):
            driven = driven_rows(first + piece * 256, strided_buf.at[pl.ds(piece * 2, 2)])
            specs.append(product(strided, driven))
        for piece, spec in enumerate(specs):
            finish(first + piece * 256, spec)
        return 0

    lax.fori_loop(0, width // block, one_block, 0)

    @pl.when(lax.axis_index("ctx") == 0)
    def _():
        copy = pltpu.make_async_copy(mixed_buf, mixed_ref, sems.at[0])
        copy.start()
        copy.wait()


def join_kernel(
    first, coded_ref, side_ref, far_ref, base_ref, right_ref, strided_ref, backward_ref, sofar_ref, mixed_ref,
    buf, sems,
):
    rows, width = coded_ref.shape
    block = math.gcd(width, 512)

    @pl.when(lax.axis_index("ctx") != 0)
    def _():
        strided, backward = strided_ref[...], backward_ref[...]

        def spectrum(at):
            coded = coded_ref[:, lanes(at, 256)].astype(jnp.float32)
            level = side_ref[0:1, lanes(first + at, 256)].astype(jnp.float32)
            size = jnp.log(jnp.abs(coded)) * (level * (1.0 / (math.log(2.0) * SPAN))) + level / 2
            return product(strided, jnp.where(coded < 0, -size, size))

        def finish(at, spec):
            cols = lanes(first + at, 256)
            conv = convolved(spec, far_ref, cols, backward)
            buf[:, lanes(at, 256)] = (right_ref[:, cols] * (conv + base_ref[:, cols])).astype(jnp.bfloat16)

        def copy(at):
            return pltpu.make_async_copy(
                buf.at[:, lanes(at * block, block)], mixed_ref.at[:, lanes(first + at * block, block)], sems.at[at]
            )

        def one_block(at, _):
            specs = [spectrum(at * block + piece) for piece in range(0, block, 256)]
            for piece, spec in enumerate(specs):
                finish(at * block + piece * 256, spec)
            copy(at).start()
            return 0

        def one_wait(at, _):
            copy(at).wait()
            return 0

        lax.fori_loop(0, width // block, one_block, 0)
        lax.fori_loop(0, width // block, one_wait, 0)


def params(mib=40):
    return pltpu.CompilerParams(vmem_limit_bytes=mib * 1024 * 1024)


def cost(us):
    return pl.CostEstimate(flops=int(us * 1e9), bytes_accessed=int(us * 3e6), transcendentals=0)


def one_way(
    projected, short_weight, pos_in, pos_bias, sine_freq, pos_mid, pos_out, decay_rate, skip_gain
):
    _, rows, width = projected.shape
    total_len = 2 * rows
    block = math.gcd(width, 512)
    steps = width // block
    parts = [width * 3 // 4, width // 4]
    forward, strided, backward = odd_tables(rows)
    decay_row = decay_rate[None, :]
    skip_row = skip_gain[None, :]
    taps = jnp.transpose(short_weight, (1, 0, 2))
    in_vmem = pl.BlockSpec(memory_space=pltpu.VMEM)
    in_hbm = pl.BlockSpec(memory_space=pltpu.HBM)

    *coded, side = pl.pallas_call(
        encode_kernel,
        in_specs=[in_hbm, in_hbm],
        out_specs=[in_vmem] * (len(parts) + 1),
        out_shape=[jax.ShapeDtypeStruct((rows, part), jnp.bfloat16) for part in parts]
        + [jax.ShapeDtypeStruct((24, width), jnp.bfloat16)],
        scratch_shapes=[
            pltpu.VMEM((2, rows, width), jnp.bfloat16),
            pltpu.VMEM((16, width), jnp.bfloat16),
            pltpu.VMEM(taps.shape, jnp.float32),
            pltpu.VMEM((2, 2, rows, 128), jnp.float32),
            pltpu.SemaphoreType.DMA((width // 256 + 1, 2)),
        ],
        compiler_params=params(),
        cost_estimate=cost(2),
        name="encode",
    )(
        pltpu.with_memory_space_constraint(projected, pltpu.HBM),
        pltpu.with_memory_space_constraint(taps, pltpu.HBM),
    )
    pairs = [(0, 1)]
    side = lax.ppermute(side, "ctx", pairs)
    coded[0] = lax.ppermute(coded[0], "ctx", pairs)
    side, *late = lax.optimization_barrier((side, *coded[1:]))
    coded[1:] = [lax.ppermute(part, "ctx", pairs) for part in late]

    positions = jnp.arange(total_len, dtype=jnp.int32).astype(jnp.float32)
    second = second_rows(positions, total_len, pos_in, pos_bias, sine_freq, pos_mid)

    def cols(lead):
        return pl.BlockSpec((lead, block), lambda j: (0, j))

    def whole(array):
        return pl.BlockSpec(array.shape, lambda j: (0,) * array.ndim)

    near, far = pl.pallas_call(
        filter_kernel,
        grid=(steps,),
        in_specs=[whole(second), cols(pos_out.shape[0]), cols(1), cols(1), whole(forward)],
        out_specs=[cols(total_len), cols(total_len)],
        out_shape=[jax.ShapeDtypeStruct((total_len, width), jnp.float32)] * 2,
        compiler_params=params(),
        cost_estimate=cost(3),
        name="filter",
    )(second, pos_out, decay_row, skip_row, forward)
    base, right, mixed = pl.pallas_call(
        own_kernel,
        in_specs=[in_vmem] * 6,
        out_specs=[in_vmem, in_vmem, in_hbm],
        out_shape=[jax.ShapeDtypeStruct((rows, width), jnp.float32)] * 2
        + [jax.ShapeDtypeStruct((rows, width), jnp.bfloat16)],
        scratch_shapes=[
            pltpu.VMEM((block // 128, 4, rows, 128), jnp.float32),
            pltpu.VMEM((rows, width), jnp.bfloat16),
            pltpu.SemaphoreType.DMA((1,)),
        ],
        compiler_params=params(),
        cost_estimate=cost(3),
        name="own",
    )(projected, side, taps, near, strided, backward)
    first = 0
    for part, values in zip(parts, coded):
        mixed = pl.pallas_call(
            functools.partial(join_kernel, first),
            in_specs=[in_vmem] * 7 + [in_hbm],
            out_specs=in_hbm,
            out_shape=jax.ShapeDtypeStruct((rows, width), jnp.bfloat16),
            input_output_aliases={7: 0},
            scratch_shapes=[
                pltpu.VMEM((rows, part), jnp.bfloat16),
                pltpu.SemaphoreType.DMA((part // math.gcd(part, 512),)),
            ],
            compiler_params=params(),
            cost_estimate=cost(1),
            name="join",
        )(values, side, far, base, right, strided, backward, mixed)
        first += part
    return mixed


def turn_table(outer_ids, inner_ids, modulus):
    product_grid = outer_ids[:, None] * inner_ids[None, :] % modulus
    angles = product_grid.astype(jnp.float32) * (2.0 * math.pi / modulus)
    return (jnp.cos(angles), jnp.sin(angles))


def section_outer(table, data):
    return jnp.einsum(
        "ka,cab->ckb", table, data, precision=HIGHEST, preferred_element_type=jnp.float32
    )


def section_inner(table, data):
    return jnp.einsum(
        "ckb,bj->ckj", data, table, precision=HIGHEST, preferred_element_type=jnp.float32
    )


def padded_spectrum(signal, outer_count, inner_count, tables):
    cos_half, sin_half, cos_twist, sin_twist, cos_inner, sin_inner = tables
    shaped = signal.reshape(signal.shape[0], outer_count // 2, inner_count)
    real_one = section_outer(cos_half, shaped)
    imag_one = -section_outer(sin_half, shaped)
    real_two = real_one * cos_twist + imag_one * sin_twist
    imag_two = imag_one * cos_twist - real_one * sin_twist
    spec_real = section_inner(cos_inner, real_two) + section_inner(sin_inner, imag_two)
    spec_imag = section_inner(cos_inner, imag_two) - section_inner(sin_inner, real_two)
    return (spec_real, spec_imag)


def causal_local(driven_cols, normed_cols, total_len):
    full_len = 2 * total_len
    inner_count = math.gcd(total_len, 128)
    outer_count = full_len // inner_count
    outer_full = jnp.arange(outer_count, dtype=jnp.int32)
    outer_half = jnp.arange(outer_count // 2, dtype=jnp.int32)
    inner_ids = jnp.arange(inner_count, dtype=jnp.int32)
    cos_half, sin_half = turn_table(outer_full, outer_half, outer_count)
    cos_twist, sin_twist = turn_table(outer_full, inner_ids, full_len)
    cos_inner, sin_inner = turn_table(inner_ids, inner_ids, inner_count)
    tables = (cos_half, sin_half, cos_twist, sin_twist, cos_inner, sin_inner)
    sig_real, sig_imag = padded_spectrum(driven_cols, outer_count, inner_count, tables)
    fil_real, fil_imag = padded_spectrum(normed_cols, outer_count, inner_count, tables)
    prod_real = sig_real * fil_real - sig_imag * fil_imag
    prod_imag = sig_real * fil_imag + sig_imag * fil_real
    back_real = section_inner(cos_inner, prod_real) - section_inner(sin_inner, prod_imag)
    back_imag = section_inner(sin_inner, prod_real) + section_inner(cos_inner, prod_imag)
    turned_real = back_real * cos_twist - back_imag * sin_twist
    turned_imag = back_real * sin_twist + back_imag * cos_twist
    cos_last, sin_last = turn_table(outer_half, outer_full, outer_count)
    result = (
        section_outer(cos_last, turned_real) - section_outer(sin_last, turned_imag)
    ) / full_len
    return result.reshape(driven_cols.shape[0], total_len)


def exchanged(
    projected, short_weight, pos_in, pos_bias, sine_freq, pos_mid, pos_out, decay_rate, skip_gain
):
    ctx_count = lax.axis_size("ctx")
    ctx_place = lax.axis_index("ctx")
    block_rows = projected.shape[1]
    total_len = block_rows * ctx_count
    rim_rows = shifted(projected[:, block_rows - (TAPS - 1) :, :], "ctx", 1)
    extended = jnp.concatenate([rim_rows, projected], axis=1)
    short_out = jnp.zeros(projected.shape, jnp.float32)
    for tap_index in range(TAPS):
        offset = TAPS - 1 - tap_index
        short_out = short_out + short_weight[tap_index][:, None, :] * extended[
            :, offset : offset + block_rows, :
        ].astype(jnp.float32)
    left_gate, right_gate, value_stream = (short_out[0], short_out[1], short_out[2])
    driven = left_gate * value_stream
    own_width = driven.shape[1] // ctx_count
    driven_cols = lax.all_to_all(driven.T, "ctx", split_axis=0, concat_axis=1, tiled=True)
    own_out = lax.dynamic_slice_in_dim(pos_out, ctx_place * own_width, own_width, 1)
    own_decay = lax.dynamic_slice_in_dim(decay_rate, ctx_place * own_width, own_width, 0)
    positions = jnp.arange(total_len, dtype=jnp.int32).astype(jnp.float32)
    long_filter = filter_rows(
        positions, total_len, pos_in, pos_bias, sine_freq, pos_mid, own_out, own_decay
    )
    normed = long_filter / jnp.sqrt(jnp.sum(long_filter * long_filter, axis=0) + 1e-05)
    conv_cols = causal_local(driven_cols, normed.T, total_len)
    long_conv = lax.all_to_all(conv_cols, "ctx", split_axis=1, concat_axis=0, tiled=True).T
    return (right_gate * (long_conv + skip_gain[None, :] * driven)).astype(jnp.bfloat16)


def body(projected, *others):
    if lax.axis_size("ctx") == 2:
        return one_way(projected, *others)
    return exchanged(projected, *others)


def solution(mesh):
    placed = (
        P(None, ("dp", "ctx"), "chan"),
        P(None, None, "chan"),
        P(),
        P(),
        P(),
        P(),
        P(None, "chan"),
        P("chan"),
        P("chan"),
    )
    return jax.shard_map(
        body, mesh=mesh, in_specs=placed, out_specs=P(("dp", "ctx"), "chan"), check_vma=False
    )
```

```python
import functools
import math

import jax
import jax.numpy as jnp
import numpy as np
from jax import lax
from jax.experimental import pallas as pl
from jax.experimental.pallas import tpu as pltpu
from jax.sharding import PartitionSpec as P

BANDS = 16
TAPS = 7
SPAN = 250.0
TINY = 1e-30

HIGHEST = lax.Precision.HIGHEST


def shifted(x, axis, by):
    size = lax.axis_size(axis)
    pairs = [(i, i + by) for i in range(size) if 0 <= i + by < size]
    return lax.ppermute(x, axis, pairs)


def features(positions, total_len):
    band_ids = jnp.arange(1, BANDS + 1, dtype=jnp.float32)
    angles = positions[:, None] * band_ids[None, :] * (2.0 * math.pi / total_len)
    return jnp.concatenate(
        [positions[:, None] / total_len, jnp.cos(angles), jnp.sin(angles)], axis=1
    )


def second_rows(positions, total_len, pos_in, pos_bias, sine_freq, pos_mid):
    inputs = features(positions, total_len)
    first_layer = jnp.sin(
        sine_freq
        * (
            jnp.dot(inputs, pos_in, precision=HIGHEST, preferred_element_type=jnp.float32)
            + pos_bias
        )
    )
    return jnp.sin(
        sine_freq
        * jnp.dot(first_layer, pos_mid, precision=HIGHEST, preferred_element_type=jnp.float32)
    )


def filter_rows(positions, total_len, pos_in, pos_bias, sine_freq, pos_mid, pos_out, decay_rate):
    second_layer = second_rows(positions, total_len, pos_in, pos_bias, sine_freq, pos_mid)
    raw_filter = jnp.dot(
        second_layer, pos_out, precision=HIGHEST, preferred_element_type=jnp.float32
    )
    return raw_filter * jnp.exp(-decay_rate[None, :] * positions[:, None])


def halves(x):
    high = x.astype(jnp.bfloat16)
    low = (x - high.astype(jnp.float32)).astype(jnp.bfloat16)
    return high, low


def parity_order(rows):
    place = np.arange(rows)
    parity, inner = place // (rows // 2), place % (rows // 2)
    return rows // 8 * (inner % 8) + inner // 8 * 2 + parity


def table_columns(table):
    high = table.astype(jnp.bfloat16)
    low = (table - high.astype(np.float32)).astype(jnp.bfloat16)
    return np.concatenate([high, high, low], axis=1)


def odd_tables(rows):
    half = rows // 2
    order = np.concatenate([np.arange(0, half, 2), np.arange(1, half, 2)])
    turns = (2 * order[:, None] + 1) * parity_order(rows)[None, :] % (4 * rows)
    angles = turns * (np.pi / (2 * rows))
    forward = np.concatenate([np.cos(angles), -np.sin(angles)], axis=0).astype(np.float32)
    pieces = [forward[:, :half], forward[:, half:]]
    return (
        np.concatenate([table_columns(piece) for piece in pieces], axis=0),
        np.concatenate([table_columns(piece.T / np.float32(rows)) for piece in pieces], axis=0),
    )


def each_tile(tiles, unroll, action):
    count = math.gcd(tiles, unroll)

    def step(at, _):
        for number in range(count):
            action(at * count + number, number)
        return 0

    if tiles == count:
        step(0, 0)
    else:
        lax.fori_loop(0, tiles // count, step, 0)


def put_halves(ref, parity, row, cols, value):
    size = ref.shape[1] // 2
    high, low = halves(value)
    count = value.shape[0]
    ref[parity, row : row + count, cols] = high
    ref[parity, size + row : size + row + count, cols] = low


def three_pass(table, ref, parity):
    size = ref.shape[1] // 2
    both = jnp.concatenate([ref[parity], ref[parity, :size]], axis=0)
    return jnp.dot(table, both, preferred_element_type=jnp.float32)


def forward_dots(forward_ref, parts_ref, spec_ref):
    rows = spec_ref.shape[1]
    for parity in range(2):
        spec_ref[parity] = three_pass(forward_ref[parity * rows : (parity + 1) * rows], parts_ref, parity)


def backward_dots(backward_ref, bins_ref, conv_ref):
    half = conv_ref.shape[0] // 2
    for parity in range(2):
        rows = slice(parity * half, (parity + 1) * half)
        conv_ref[rows] = three_pass(backward_ref[rows], bins_ref, parity)


def unfolded(spec_ref, row, cols):
    half = spec_ref.shape[1] // 2
    even_cos, odd_cos = spec_ref[0, row : row + 16, cols], spec_ref[1, row : row + 16, cols]
    sine = slice(half + row, half + row + 16)
    even_sin, odd_sin = spec_ref[0, sine, cols], spec_ref[1, sine, cols]
    return even_cos + odd_cos, even_sin + odd_sin, even_cos - odd_cos, odd_sin - even_sin


def filtered(spec_ref, filter_ref, bins_ref, cols, filter_cols):
    half = spec_ref.shape[1] // 2
    for row in range(0, half, 16):
        real, imag, real_far, imag_far = unfolded(spec_ref, row, cols)
        taps = [filter_ref[at * half + row : at * half + row + 16, filter_cols] for at in range(4)]
        out_real, out_imag = real * taps[0] - imag * taps[1], real * taps[1] + imag * taps[0]
        far_real = real_far * taps[2] - imag_far * taps[3]
        far_imag = real_far * taps[3] + imag_far * taps[2]
        put_halves(bins_ref, 0, row, cols, out_real + far_real)
        put_halves(bins_ref, 0, half + row, cols, out_imag - far_imag)
        put_halves(bins_ref, 1, row, cols, out_real - far_real)
        put_halves(bins_ref, 1, half + row, cols, out_imag + far_imag)


def strided_rows(values, buf):
    buf[...] = values.astype(jnp.float32)
    count = buf.shape[0] // 8
    return [buf[pl.ds(v, 8, stride=count), :] for v in range(count)]


def short_sum(parts, rim, taps_ref, at, cols):
    top = lax.broadcasted_iota(jnp.int32, (8, 128), 0) == 0
    before = {}
    for back in range(1, TAPS):
        edge = 0.0 if rim is None else rim[8 - back : 9 - back]
        before[-back] = jnp.where(top, edge, pltpu.roll(parts[-back], 1, 0))
    taps = [jnp.broadcast_to(taps_ref[at, k : k + 1, cols], (8, 128)) for k in range(TAPS)]
    sums = []
    for v in range(len(parts)):
        terms = [taps[k] * (parts[v - k] if v >= k else before[v - k]) for k in range(TAPS)]
        sums.append(((terms[0] + terms[1]) + (terms[2] + terms[3])) + ((terms[4] + terms[5]) + terms[6]))
    return sums


def parity_rows(parts):
    ordered = parts[0::2] + parts[1::2]
    return [jnp.concatenate(ordered[i : i + 2], axis=0) for i in range(0, len(ordered), 2)]


def natural_rows(ref_rows, buf):
    count = buf.shape[0] // 8
    for at, value in enumerate(ref_rows):
        for piece in range(2):
            number = 2 * at + piece
            v = number % (count // 2) * 2 + number // (count // 2)
            buf[pl.ds(v, 8, stride=count), :] = value[8 * piece : 8 * piece + 8]
    return buf[...]


def tile_lanes(tile, first=0):
    return pl.ds(pl.multiple_of(first + tile * 128, 128), 128)


def tile_rows(tile, row, count=16):
    return pl.ds(pl.multiple_of(tile * 128 + row, 16), count)


def place_level(peak, tile, peak_buf, levels_buf):
    for step in (1, 2, 4):
        peak = jnp.maximum(peak, pltpu.roll(peak, step, 0))
    level = jnp.maximum(peak, TINY)
    wide = level * 65537.0
    level = wide - (wide - level)
    peak_buf[:, tile_lanes(tile)] = SPAN / level
    levels_buf[pl.ds(tile, 1), :] = level[0:1]


def put_coded(coded_ref, tile, row, value, gain):
    coded = jnp.exp2(jnp.abs(value) * gain - SPAN / 2)
    coded_ref[tile_rows(tile, row), :] = jnp.where(value < 0, -coded, coded).astype(jnp.bfloat16)


def decoder(levels_buf, tile):
    level = levels_buf[pl.ds(tile, 1), :]
    slope = jnp.broadcast_to(level * (1.0 / (math.log(2.0) * SPAN)), (16, 128))
    middle = jnp.broadcast_to(level / 2, (16, 128))

    def decode(coded):
        coded = coded.astype(jnp.float32)
        size = jnp.log(jnp.abs(coded)) * slope + middle
        return jnp.where(coded < 0, -size, size)

    return decode


def encode_kernel(
    first, projected_ref, taps_ref, coded_ref, driven_ref, rows_buf, rim_buf, taps_buf, strided_buf, peak_buf,
    levels_buf, sems,
):
    rows, size = rows_buf.shape[1:]
    tiles = size // 128
    span = pl.ds(first, size)
    with_rims = coded_ref.shape[0] > tiles * rows + 16

    @pl.when(lax.axis_index("ctx") == 0)
    def _():
        copies = [
            pltpu.make_async_copy(taps_ref.at[:, :, span], taps_buf, sems.at[0]),
            pltpu.make_async_copy(projected_ref.at[0, :, span], rows_buf.at[0], sems.at[1]),
            pltpu.make_async_copy(projected_ref.at[2, :, span], rows_buf.at[1], sems.at[2]),
        ]
        if with_rims:
            copies.append(pltpu.make_async_copy(projected_ref.at[:, pl.ds(rows - 16, 16)], rim_buf, sems.at[3]))
        for copy in copies:
            copy.start()
        for copy in copies:
            copy.wait()

        def drive(tile, number):
            cols = tile_lanes(tile)
            sums = [
                short_sum(
                    strided_rows(rows_buf[way, :, cols], strided_buf.at[number, way]), None, taps_buf, 2 * way, cols
                )
                for way in range(2)
            ]
            driven = [one * two for one, two in zip(*sums)]
            for row, value in enumerate(parity_rows(driven)):
                driven_ref[16 * row : 16 * row + 16, cols] = value
            peak_buf[:, cols] = functools.reduce(jnp.maximum, [jnp.abs(value) for value in driven])

        each_tile(tiles, strided_buf.shape[0], drive)
        each_tile(
            tiles, 4, lambda tile, _: place_level(peak_buf[:, tile_lanes(tile)], tile, peak_buf, levels_buf)
        )
        coded_ref[tiles * rows : tiles * rows + 16] = levels_buf[...].astype(jnp.bfloat16)

        def code(tile, _):
            cols = tile_lanes(tile)
            gain = peak_buf[:, cols]
            gain = jnp.concatenate([gain, gain], axis=0)
            for row in range(0, rows, 16):
                put_coded(coded_ref, tile, row, driven_ref[row : row + 16, cols], gain)

        each_tile(tiles, 4, code)
        if with_rims:

            def rims(pair, _):
                for at in range(3):
                    values = [
                        rim_buf[at, :, tile_lanes(2 * pair + way)].astype(jnp.float32)[8:] for way in range(2)
                    ]
                    there = pl.ds(pl.multiple_of(tiles * rows + 16 + pair * 48 + at * 16, 16), 16)
                    coded_ref[there, :] = jnp.concatenate(values, axis=0).astype(jnp.bfloat16)

            each_tile(rim_buf.shape[2] // 256, 4, rims)


def filter_kernel(
    second_ref, out_ref, decay_ref, skip_ref, places_ref, forward_ref, near_ref, far_ref, raw_buf, parts_buf, spec_buf,
    scale_buf,
):
    rows, width = near_ref.shape[0] // 2, near_ref.shape[1]
    half = rows // 2
    second_high, second_low = halves(second_ref[...])
    second = jnp.concatenate([second_high, second_high, second_low], axis=1)
    out_high, out_low = halves(out_ref[...])
    raw_buf[...] = jnp.dot(
        second, jnp.concatenate([out_high, out_low, out_high], axis=0), preferred_element_type=jnp.float32
    )

    def decay(tile, _):
        cols = tile_lanes(tile)
        fall = -decay_ref[:, cols]
        total = jnp.zeros((8, 128), jnp.float32)
        for row in range(0, 2 * rows, 16):
            taps = raw_buf[row : row + 16, cols] * jnp.exp(fall * places_ref[row : row + 16])
            total = total + (taps[:8] * taps[:8] + taps[8:] * taps[8:])
            parity = row % rows // half
            put_halves(parts_buf, parity, row % half, tile_lanes(tile, row // rows * width), taps)
        for step in (1, 2, 4):
            total = total + pltpu.roll(total, step, 0)
        scale_buf[:, cols] = 1.0 / jnp.sqrt(total + 1e-05)

    each_tile(width // 128, 4, decay)
    forward_dots(forward_ref, parts_buf, spec_buf)

    def shape(tile, _):
        cols = tile_lanes(tile)
        scale = scale_buf[:, cols]
        scale = jnp.concatenate([scale, scale], axis=0)
        skip = skip_ref[:, cols]
        for row in range(0, half, 16):
            low = [value * scale for value in unfolded(spec_buf, row, cols)]
            high = [value * scale for value in unfolded(spec_buf, row, tile_lanes(tile, width))]
            sign = 1 if row < half // 2 else -1
            turned = [-sign * low[1], sign * low[0], sign * low[3], -sign * low[2]]
            low = [low[0] + skip, low[1], low[2] + skip, low[3]]
            for at in range(4):
                near_ref[at * half + row : at * half + row + 16, cols] = low[at]
                far_ref[at * half + row : at * half + row + 16, cols] = high[at] + turned[at]

    each_tile(width // 128, 4, shape)


def own_kernel(
    first, send, projected_ref, rims_ref, taps_ref, near_ref, far_ref, forward_ref, backward_ref, *refs
):
    if send:
        base_ref, right_ref, mixed_ref, coded_ref, *bufs = refs
    else:
        *driven_refs, _, base_ref, right_ref, mixed_ref = refs[:6]
        bufs = refs[6:]
    strided_buf, parts_buf, spec_buf, bins_buf, mixed_buf, sems = bufs[:6]
    rows, width = base_ref.shape
    half = rows // 2
    tiles = width // 128
    first_tile = first // 128
    rims_at = rims_ref.shape[0] - projected_ref.shape[2] // 128 * 24
    place = lax.axis_index("ctx")

    def sums_of(tile, number, ats):
        cols = tile_lanes(tile, first)
        far_tile = tile + first_tile
        sums = []
        for at in ats:
            pair = pl.ds(pl.multiple_of(rims_at + far_tile // 2 * 48 + at * 16, 16), 16)
            rim = rims_ref[pair, :].astype(jnp.float32)
            rim = jnp.where(far_tile % 2 == 0, rim[:8], rim[8:])
            parts = strided_rows(projected_ref[at, :, cols], strided_buf.at[number, at])
            sums.append(short_sum(parts, rim, taps_ref, at, cols))
        return sums

    def put_right(tile, values):
        for at, value in enumerate(parity_rows(values)):
            right_ref[16 * at : 16 * at + 16, tile_lanes(tile)] = value

    def drive(tile, number):
        sums = sums_of(tile, number, range(3))
        put_right(tile, sums[1])
        driven = [one * two for one, two in zip(sums[0], sums[2])]
        for at, value in enumerate(parity_rows(driven)):
            put_halves(parts_buf, 16 * at // half, 16 * at % half, tile_lanes(tile), value)

    if send:
        each_tile(tiles, strided_buf.shape[0], drive)
    else:

        @pl.when(place != 0)
        def _():
            each_tile(tiles, strided_buf.shape[0], drive)

        @pl.when(place == 0)
        def _():
            each_tile(tiles, strided_buf.shape[0], lambda tile, number: put_right(tile, sums_of(tile, number, [1])[0]))
            start = 0
            for ref in driven_refs:

                def recall(tile, _, ref=ref, start=start):
                    for row in range(0, rows, 16):
                        value = ref[row : row + 16, tile_lanes(tile)]
                        put_halves(parts_buf, row // half, row % half, tile_lanes(tile, start), value)

                each_tile(ref.shape[1] // 128, 4, recall)
                start += ref.shape[1]

    forward_dots(forward_ref, parts_buf, spec_buf)
    if send:
        conv_buf, peak_buf, levels_buf = bufs[6:]

        @pl.when(place == 0)
        def _():
            each_tile(
                tiles, 4,
                lambda tile, _: filtered(spec_buf, far_ref, bins_buf, tile_lanes(tile), tile_lanes(tile, first)),
            )
            backward_dots(backward_ref, bins_buf, conv_buf)

            def peaks(tile, _):
                cols = tile_lanes(tile)
                peak = functools.reduce(
                    jnp.maximum, [jnp.abs(conv_buf[row : row + 8, cols]) for row in range(0, rows, 8)]
                )
                place_level(peak, tile, peak_buf, levels_buf)

            each_tile(tiles, 4, peaks)
            coded_ref[tiles * rows : tiles * rows + 16] = levels_buf[...].astype(jnp.bfloat16)

            def code(tile, _):
                cols = tile_lanes(tile)
                gain = peak_buf[:, cols]
                gain = jnp.concatenate([gain, gain], axis=0)
                for row in range(0, rows, 16):
                    put_coded(coded_ref, tile, row, conv_buf[row : row + 16, cols], gain)

            each_tile(tiles, 4, code)

    each_tile(
        tiles, 4, lambda tile, _: filtered(spec_buf, near_ref, bins_buf, tile_lanes(tile), tile_lanes(tile, first))
    )
    backward_dots(backward_ref, bins_buf, base_ref)

    @pl.when(place == 0)
    def _():
        def mix(tile, number):
            cols = tile_lanes(tile)
            values = [right_ref[at : at + 16, cols] * base_ref[at : at + 16, cols] for at in range(0, rows, 16)]
            mixed_buf[:, cols] = natural_rows(values, strided_buf.at[number, 0]).astype(jnp.bfloat16)

        each_tile(tiles, strided_buf.shape[0], mix)
        copy = pltpu.make_async_copy(mixed_buf, mixed_ref.at[:, pl.ds(first, width)], sems.at[0])
        copy.start()
        copy.wait()


def read_levels(coded_ref, levels_buf, tiles, rows):
    levels_buf[...] = coded_ref[tiles * rows : tiles * rows + 16].astype(jnp.float32)


def join_kernel(
    one_ref, two_ref, far_ref, base_ref, right_ref, forward_ref, backward_ref, sofar_ref, mixed_ref,
    parts_buf, spec_buf, bins_buf, conv_buf, strided_buf, buf, levels_buf, sems,
):
    rows, width = base_ref.shape
    half = rows // 2
    tiles = width // 128
    later = (two_ref.shape[0] - 16) // rows
    counts = [tiles - later, later]

    @pl.when(lax.axis_index("ctx") != 0)
    def _():
        start = 0
        for at, ref in enumerate((one_ref, two_ref)):
            read_levels(ref, levels_buf.at[at], counts[at], rows)

            def spread_out(tile, _, ref=ref, at=at, start=start):
                decode = decoder(levels_buf.at[at], tile)
                for row in range(0, rows, 16):
                    value = decode(ref[tile_rows(tile, row), :])
                    put_halves(parts_buf, row // half, row % half, tile_lanes(tile, start), value)

            each_tile(counts[at], 4, spread_out)
            start += counts[at] * 128
        forward_dots(forward_ref, parts_buf, spec_buf)
        each_tile(
            tiles, 4, lambda tile, _: filtered(spec_buf, far_ref, bins_buf, tile_lanes(tile), tile_lanes(tile))
        )
        backward_dots(backward_ref, bins_buf, conv_buf)

        def mix(tile, number):
            cols = tile_lanes(tile)
            values = [
                right_ref[at : at + 16, cols] * (conv_buf[at : at + 16, cols] + base_ref[at : at + 16, cols])
                for at in range(0, rows, 16)
            ]
            buf[:, cols] = natural_rows(values, strided_buf.at[number]).astype(jnp.bfloat16)

        each_tile(tiles, strided_buf.shape[0], mix)
        copy = pltpu.make_async_copy(buf, mixed_ref.at[:, pl.ds(0, width)], sems.at[0])
        copy.start()
        copy.wait()


def last_kernel(
    first, coded_ref, base_ref, right_ref, sofar_ref, mixed_ref, strided_buf, buf, levels_buf, sems
):
    rows, width = base_ref.shape
    tiles = width // 128

    @pl.when(lax.axis_index("ctx") != 0)
    def _():
        read_levels(coded_ref, levels_buf, tiles, rows)

        def mix(tile, number):
            cols = tile_lanes(tile)
            decode = decoder(levels_buf, tile)
            values = [
                right_ref[at : at + 16, cols] * (decode(coded_ref[tile_rows(tile, at), :]) + base_ref[at : at + 16, cols])
                for at in range(0, rows, 16)
            ]
            buf[:, cols] = natural_rows(values, strided_buf.at[number]).astype(jnp.bfloat16)

        each_tile(tiles, strided_buf.shape[0], mix)
        copy = pltpu.make_async_copy(buf, mixed_ref.at[:, pl.ds(first, width)], sems.at[0])
        copy.start()
        copy.wait()


def params(mib=40):
    return pltpu.CompilerParams(vmem_limit_bytes=mib * 1024 * 1024)


def cost(us):
    return pl.CostEstimate(flops=int(us * 1e9), bytes_accessed=int(us * 3e6), transcendentals=0)


def one_way(
    projected, short_weight, pos_in, pos_bias, sine_freq, pos_mid, pos_out, decay_rate, skip_gain
):
    _, rows, width = projected.shape
    half = rows // 2
    total_len = 2 * rows
    ahead = [width // 8, width * 5 // 8]
    middle = sum(ahead)
    behind = width - middle
    forward, backward = odd_tables(rows)
    taps = jnp.transpose(short_weight, (1, 0, 2))
    in_vmem = pl.BlockSpec(memory_space=pltpu.VMEM)
    in_hbm = pl.BlockSpec(memory_space=pltpu.HBM)
    floats, shorts = functools.partial(pltpu.VMEM, dtype=jnp.float32), functools.partial(pltpu.VMEM, dtype=jnp.bfloat16)
    pairs = [(0, 1)]

    def arrays(*shapes, dtype=jnp.float32):
        return [jax.ShapeDtypeStruct(shape, dtype) for shape in shapes]

    def message(size, more=0):
        return arrays((size // 128 * rows + 16 + more, 128), dtype=jnp.bfloat16)

    coded, driven = [], []
    for at, size in enumerate(ahead):
        code, signal = pl.pallas_call(
            functools.partial(encode_kernel, sum(ahead[:at])),
            in_specs=[in_hbm, in_hbm],
            out_specs=[in_vmem] * 2,
            out_shape=message(size, width // 128 * 24 if at == 0 else 0) + arrays((rows, size)),
            scratch_shapes=[
                shorts((2, rows, size)),
                shorts((3, 16, width)),
                floats((3, TAPS, size)),
                floats((2, 2, rows, 128)),
                floats((8, size)),
                floats((16, 128)),
                pltpu.SemaphoreType.DMA((4,)),
            ],
            compiler_params=params(),
            cost_estimate=cost(1),
            name="encode",
        )(
            pltpu.with_memory_space_constraint(projected, pltpu.HBM),
            pltpu.with_memory_space_constraint(taps, pltpu.HBM),
        )
        coded.append(lax.ppermute(code, "ctx", pairs))
        driven.append(signal)

    order = parity_order(rows)
    places = np.concatenate([order, order + rows]).astype(np.float32)
    second = second_rows(jnp.asarray(places), total_len, pos_in, pos_bias, sine_freq, pos_mid)
    near, far = pl.pallas_call(
        filter_kernel,
        in_specs=[in_vmem] * 6,
        out_specs=[in_vmem] * 2,
        out_shape=arrays((total_len, width), (total_len, width)),
        scratch_shapes=[
            floats((total_len, width)),
            shorts((2, rows, 2 * width)),
            floats((2, rows, 2 * width)),
            floats((8, width)),
        ],
        compiler_params=params(),
        cost_estimate=cost(3),
        name="filter",
    )(second, pos_out, decay_rate[None, :], skip_gain[None, :], jnp.asarray(np.repeat(places[:, None], 128, 1)), forward)

    def own(first, size, send, *more):
        return pl.pallas_call(
            functools.partial(own_kernel, first, send),
            in_specs=[in_vmem] * 7 + [in_vmem, in_vmem, in_hbm][: len(more)],
            out_specs=[in_vmem, in_vmem, in_hbm] + [in_vmem] * send,
            out_shape=arrays((rows, size), (rows, size))
            + arrays((rows, width), dtype=jnp.bfloat16)
            + message(size) * send,
            input_output_aliases={} if send else {9: 2},
            scratch_shapes=[
                floats((2, 3, rows, 128)),
                shorts((2, rows, size)),
                floats((2, rows, size)),
                shorts((2, 2 * rows, size)),
                shorts((rows, size)),
                pltpu.SemaphoreType.DMA((1,)),
            ]
            + [floats((rows, size)), floats((8, size)), floats((16, 128))] * send,
            compiler_params=params(),
            cost_estimate=cost(2),
            name="own",
        )(projected, coded[0], taps, near, far, forward, backward, *more)

    last_base, last_right, mixed, code = own(middle, behind, True)
    last_code = lax.ppermute(code, "ctx", pairs)
    base, right, mixed = own(0, middle, False, *driven, mixed)
    mixed = pl.pallas_call(
        join_kernel,
        in_specs=[in_vmem] * 7 + [in_hbm],
        out_specs=in_hbm,
        out_shape=jax.ShapeDtypeStruct((rows, width), jnp.bfloat16),
        input_output_aliases={7: 0},
        scratch_shapes=[
            shorts((2, rows, middle)),
            floats((2, rows, middle)),
            shorts((2, 2 * rows, middle)),
            floats((rows, middle)),
            floats((4, rows, 128)),
            shorts((rows, middle)),
            floats((2, 16, 128)),
            pltpu.SemaphoreType.DMA((1,)),
        ],
        compiler_params=params(),
        cost_estimate=cost(2),
        name="join",
    )(*coded, far, base, right, forward, backward, mixed)
    return pl.pallas_call(
        functools.partial(last_kernel, middle),
        in_specs=[in_vmem] * 3 + [in_hbm],
        out_specs=in_hbm,
        out_shape=jax.ShapeDtypeStruct((rows, width), jnp.bfloat16),
        input_output_aliases={3: 0},
        scratch_shapes=[
            floats((4, rows, 128)),
            shorts((rows, behind)),
            floats((16, 128)),
            pltpu.SemaphoreType.DMA((1,)),
        ],
        compiler_params=params(),
        cost_estimate=cost(1),
        name="last",
    )(last_code, last_base, last_right, mixed)


def turn_table(outer_ids, inner_ids, modulus):
    product_grid = outer_ids[:, None] * inner_ids[None, :] % modulus
    angles = product_grid.astype(jnp.float32) * (2.0 * math.pi / modulus)
    return (jnp.cos(angles), jnp.sin(angles))


def section_outer(table, data):
    return jnp.einsum(
        "ka,cab->ckb", table, data, precision=HIGHEST, preferred_element_type=jnp.float32
    )


def section_inner(table, data):
    return jnp.einsum(
        "ckb,bj->ckj", data, table, precision=HIGHEST, preferred_element_type=jnp.float32
    )


def padded_spectrum(signal, outer_count, inner_count, tables):
    cos_half, sin_half, cos_twist, sin_twist, cos_inner, sin_inner = tables
    shaped = signal.reshape(signal.shape[0], outer_count // 2, inner_count)
    real_one = section_outer(cos_half, shaped)
    imag_one = -section_outer(sin_half, shaped)
    real_two = real_one * cos_twist + imag_one * sin_twist
    imag_two = imag_one * cos_twist - real_one * sin_twist
    spec_real = section_inner(cos_inner, real_two) + section_inner(sin_inner, imag_two)
    spec_imag = section_inner(cos_inner, imag_two) - section_inner(sin_inner, real_two)
    return (spec_real, spec_imag)


def causal_local(driven_cols, normed_cols, total_len):
    full_len = 2 * total_len
    inner_count = math.gcd(total_len, 128)
    outer_count = full_len // inner_count
    outer_full = jnp.arange(outer_count, dtype=jnp.int32)
    outer_half = jnp.arange(outer_count // 2, dtype=jnp.int32)
    inner_ids = jnp.arange(inner_count, dtype=jnp.int32)
    cos_half, sin_half = turn_table(outer_full, outer_half, outer_count)
    cos_twist, sin_twist = turn_table(outer_full, inner_ids, full_len)
    cos_inner, sin_inner = turn_table(inner_ids, inner_ids, inner_count)
    tables = (cos_half, sin_half, cos_twist, sin_twist, cos_inner, sin_inner)
    sig_real, sig_imag = padded_spectrum(driven_cols, outer_count, inner_count, tables)
    fil_real, fil_imag = padded_spectrum(normed_cols, outer_count, inner_count, tables)
    prod_real = sig_real * fil_real - sig_imag * fil_imag
    prod_imag = sig_real * fil_imag + sig_imag * fil_real
    back_real = section_inner(cos_inner, prod_real) - section_inner(sin_inner, prod_imag)
    back_imag = section_inner(sin_inner, prod_real) + section_inner(cos_inner, prod_imag)
    turned_real = back_real * cos_twist - back_imag * sin_twist
    turned_imag = back_real * sin_twist + back_imag * cos_twist
    cos_last, sin_last = turn_table(outer_half, outer_full, outer_count)
    result = (
        section_outer(cos_last, turned_real) - section_outer(sin_last, turned_imag)
    ) / full_len
    return result.reshape(driven_cols.shape[0], total_len)


def exchanged(
    projected, short_weight, pos_in, pos_bias, sine_freq, pos_mid, pos_out, decay_rate, skip_gain
):
    ctx_count = lax.axis_size("ctx")
    ctx_place = lax.axis_index("ctx")
    block_rows = projected.shape[1]
    total_len = block_rows * ctx_count
    rim_rows = shifted(projected[:, block_rows - (TAPS - 1) :, :], "ctx", 1)
    extended = jnp.concatenate([rim_rows, projected], axis=1)
    short_out = jnp.zeros(projected.shape, jnp.float32)
    for tap_index in range(TAPS):
        offset = TAPS - 1 - tap_index
        short_out = short_out + short_weight[tap_index][:, None, :] * extended[
            :, offset : offset + block_rows, :
        ].astype(jnp.float32)
    left_gate, right_gate, value_stream = (short_out[0], short_out[1], short_out[2])
    driven = left_gate * value_stream
    own_width = driven.shape[1] // ctx_count
    driven_cols = lax.all_to_all(driven.T, "ctx", split_axis=0, concat_axis=1, tiled=True)
    own_out = lax.dynamic_slice_in_dim(pos_out, ctx_place * own_width, own_width, 1)
    own_decay = lax.dynamic_slice_in_dim(decay_rate, ctx_place * own_width, own_width, 0)
    positions = jnp.arange(total_len, dtype=jnp.int32).astype(jnp.float32)
    long_filter = filter_rows(
        positions, total_len, pos_in, pos_bias, sine_freq, pos_mid, own_out, own_decay
    )
    normed = long_filter / jnp.sqrt(jnp.sum(long_filter * long_filter, axis=0) + 1e-05)
    conv_cols = causal_local(driven_cols, normed.T, total_len)
    long_conv = lax.all_to_all(conv_cols, "ctx", split_axis=1, concat_axis=0, tiled=True).T
    return (right_gate * (long_conv + skip_gain[None, :] * driven)).astype(jnp.bfloat16)


def body(projected, *others):
    if lax.axis_size("ctx") == 2:
        return one_way(projected, *others)
    return exchanged(projected, *others)


def solution(mesh):
    placed = (
        P(None, ("dp", "ctx"), "chan"),
        P(None, None, "chan"),
        P(),
        P(),
        P(),
        P(),
        P(None, "chan"),
        P("chan"),
        P("chan"),
    )
    return jax.shard_map(
        body, mesh=mesh, in_specs=placed, out_specs=P(("dp", "ctx"), "chan"), check_vma=False
    )
```

```python
import functools
import math

import jax
import jax.numpy as jnp
import numpy as np
from jax import lax
from jax.experimental import pallas as pl
from jax.experimental.pallas import tpu as pltpu
from jax.sharding import PartitionSpec as P

BANDS = 16
TAPS = 7
SPAN = 250.0
TINY = 1e-30

HIGHEST = lax.Precision.HIGHEST


def shifted(x, axis, by):
    size = lax.axis_size(axis)
    pairs = [(i, i + by) for i in range(size) if 0 <= i + by < size]
    return lax.ppermute(x, axis, pairs)


def features(positions, total_len):
    band_ids = jnp.arange(1, BANDS + 1, dtype=jnp.float32)
    angles = positions[:, None] * band_ids[None, :] * (2.0 * math.pi / total_len)
    return jnp.concatenate(
        [positions[:, None] / total_len, jnp.cos(angles), jnp.sin(angles)], axis=1
    )


def second_rows(positions, total_len, pos_in, pos_bias, sine_freq, pos_mid):
    inputs = features(positions, total_len)
    first_layer = jnp.sin(
        sine_freq
        * (
            jnp.dot(inputs, pos_in, precision=HIGHEST, preferred_element_type=jnp.float32)
            + pos_bias
        )
    )
    return jnp.sin(
        sine_freq
        * jnp.dot(first_layer, pos_mid, precision=HIGHEST, preferred_element_type=jnp.float32)
    )


def filter_rows(positions, total_len, pos_in, pos_bias, sine_freq, pos_mid, pos_out, decay_rate):
    second_layer = second_rows(positions, total_len, pos_in, pos_bias, sine_freq, pos_mid)
    raw_filter = jnp.dot(
        second_layer, pos_out, precision=HIGHEST, preferred_element_type=jnp.float32
    )
    return raw_filter * jnp.exp(-decay_rate[None, :] * positions[:, None])


def halves(x):
    high = x.astype(jnp.bfloat16)
    low = (x - high.astype(jnp.float32)).astype(jnp.bfloat16)
    return high, low


def feature_table(places, total_len):
    bands = np.arange(1, BANDS + 1, dtype=np.float32)
    angles = places[:, None] * bands[None, :] * np.float32(2.0 * math.pi / total_len)
    first = places[:, None] / np.float32(total_len)
    table = np.concatenate([first, np.cos(angles), np.sin(angles), np.ones_like(first)], axis=1)
    spare = np.zeros((places.shape[0], -table.shape[1] % 8))
    return np.concatenate([table, spare], axis=1).astype(np.float32).T.copy()


def parity_order(rows):
    place = np.arange(rows)
    parity, inner = place // (rows // 2), place % (rows // 2)
    return rows // 8 * (inner % 8) + inner // 8 * 2 + parity


def table_columns(table):
    high = table.astype(jnp.bfloat16)
    low = (table - high.astype(np.float32)).astype(jnp.bfloat16)
    return np.concatenate([high, high, low], axis=1)


def odd_tables(rows):
    half = rows // 2
    order = np.concatenate([np.arange(0, half, 2), np.arange(1, half, 2)])
    turns = (2 * order[:, None] + 1) * parity_order(rows)[None, :] % (4 * rows)
    angles = turns * (np.pi / (2 * rows))
    forward = np.concatenate([np.cos(angles), -np.sin(angles)], axis=0).astype(np.float32)
    pieces = [forward[:, :half], forward[:, half:]]
    return (
        np.concatenate([table_columns(piece) for piece in pieces], axis=0),
        np.concatenate([table_columns(piece.T / np.float32(rows)) for piece in pieces], axis=0),
    )


def each_tile(tiles, unroll, action):
    count = math.gcd(tiles, unroll)

    def step(at, _):
        for number in range(count):
            action(at * count + number, number)
        return 0

    if tiles == count:
        step(0, 0)
    else:
        lax.fori_loop(0, tiles // count, step, 0)


def put_halves(ref, parity, row, cols, value):
    size = ref.shape[1] // 2
    high, low = halves(value)
    count = value.shape[0]
    ref[parity, row : row + count, cols] = high
    ref[parity, size + row : size + row + count, cols] = low


def three_pass(table, ref, parity):
    size = ref.shape[1] // 2
    both = jnp.concatenate([ref[parity], ref[parity, :size]], axis=0)
    return jnp.dot(table, both, preferred_element_type=jnp.float32)


def forward_dots(forward_ref, parts_ref, spec_ref):
    rows = spec_ref.shape[1]
    for parity in range(2):
        spec_ref[parity] = three_pass(forward_ref[parity * rows : (parity + 1) * rows], parts_ref, parity)


def backward_dots(backward_ref, bins_ref, conv_ref):
    half = conv_ref.shape[0] // 2
    for parity in range(2):
        rows = slice(parity * half, (parity + 1) * half)
        conv_ref[rows] = three_pass(backward_ref[rows], bins_ref, parity)


def unfolded(spec_ref, row, cols):
    half = spec_ref.shape[1] // 2
    even_cos, odd_cos = spec_ref[0, row : row + 16, cols], spec_ref[1, row : row + 16, cols]
    sine = slice(half + row, half + row + 16)
    even_sin, odd_sin = spec_ref[0, sine, cols], spec_ref[1, sine, cols]
    return even_cos + odd_cos, even_sin + odd_sin, even_cos - odd_cos, odd_sin - even_sin


def filtered(spec_ref, filter_ref, bins_ref, cols, filter_cols):
    half = spec_ref.shape[1] // 2
    for row in range(0, half, 16):
        real, imag, real_far, imag_far = unfolded(spec_ref, row, cols)
        taps = [filter_ref[at * half + row : at * half + row + 16, filter_cols] for at in range(4)]
        out_real, out_imag = real * taps[0] - imag * taps[1], real * taps[1] + imag * taps[0]
        far_real = real_far * taps[2] - imag_far * taps[3]
        far_imag = real_far * taps[3] + imag_far * taps[2]
        put_halves(bins_ref, 0, row, cols, out_real + far_real)
        put_halves(bins_ref, 0, half + row, cols, out_imag - far_imag)
        put_halves(bins_ref, 1, row, cols, out_real - far_real)
        put_halves(bins_ref, 1, half + row, cols, out_imag + far_imag)


def strided_rows(values, buf):
    buf[...] = values.astype(jnp.float32)
    count = buf.shape[0] // 8
    return [buf[pl.ds(v, 8, stride=count), :] for v in range(count)]


def short_sum(parts, rim, taps_ref, at, cols):
    top = lax.broadcasted_iota(jnp.int32, (8, 128), 0) == 0
    before = {}
    for back in range(1, TAPS):
        edge = 0.0 if rim is None else rim[8 - back : 9 - back]
        before[-back] = jnp.where(top, edge, pltpu.roll(parts[-back], 1, 0))
    taps = [jnp.broadcast_to(taps_ref[at, k : k + 1, cols], (8, 128)) for k in range(TAPS)]
    sums = []
    for v in range(len(parts)):
        terms = [taps[k] * (parts[v - k] if v >= k else before[v - k]) for k in range(TAPS)]
        sums.append(((terms[0] + terms[1]) + (terms[2] + terms[3])) + ((terms[4] + terms[5]) + terms[6]))
    return sums


def parity_rows(parts):
    ordered = parts[0::2] + parts[1::2]
    return [jnp.concatenate(ordered[i : i + 2], axis=0) for i in range(0, len(ordered), 2)]


def natural_rows(ref_rows, buf):
    count = buf.shape[0] // 8
    for at, value in enumerate(ref_rows):
        for piece in range(2):
            number = 2 * at + piece
            v = number % (count // 2) * 2 + number // (count // 2)
            buf[pl.ds(v, 8, stride=count), :] = value[8 * piece : 8 * piece + 8]
    return buf[...]


def tile_lanes(tile, first=0):
    return pl.ds(pl.multiple_of(first + tile * 128, 128), 128)


def tile_rows(tile, row, count=16):
    return pl.ds(pl.multiple_of(tile * 128 + row, 16), count)


def place_level(peak, tile, peak_buf, levels_buf):
    for step in (1, 2, 4):
        peak = jnp.maximum(peak, pltpu.roll(peak, step, 0))
    level = jnp.maximum(peak, TINY)
    wide = level * 65537.0
    level = wide - (wide - level)
    peak_buf[:, tile_lanes(tile)] = SPAN / level
    levels_buf[pl.ds(tile, 1), :] = level[0:1]


def put_coded(coded_ref, tile, row, value, gain):
    coded = jnp.exp2(jnp.abs(value) * gain - SPAN / 2)
    coded_ref[tile_rows(tile, row), :] = jnp.where(value < 0, -coded, coded).astype(jnp.bfloat16)


def decoder(levels_buf, tile):
    level = levels_buf[pl.ds(tile, 1), :]
    slope = jnp.broadcast_to(level * (1.0 / (math.log(2.0) * SPAN)), (16, 128))
    middle = jnp.broadcast_to(level / 2, (16, 128))

    def decode(coded):
        coded = coded.astype(jnp.float32)
        size = jnp.log(jnp.abs(coded)) * slope + middle
        return jnp.where(coded < 0, -size, size)

    return decode


def second_layer(feats_ref, in_ref, bias_ref, freq_ref, mid_ref, scaled_buf):
    dot = functools.partial(
        lax.dot_general,
        dimension_numbers=(((0,), (0,)), ((), ())),
        precision=HIGHEST,
        preferred_element_type=jnp.float32,
    )
    count = in_ref.shape[0]
    freq = freq_ref[...]
    scaled_buf[...] = jnp.zeros_like(scaled_buf)
    scaled_buf[0:count] = in_ref[...] * freq
    scaled_buf[count : count + 1] = bias_ref[...] * freq
    layer = jnp.sin(dot(scaled_buf[...], feats_ref[...]))
    return jnp.sin(dot(mid_ref[...] * freq, layer)).T


def encode_tiles(tiles, rows, streams, taps_ref, taps_first, coded_ref, driven_ref, strided_buf, peak_buf, levels_buf):
    def drive(tile, number):
        cols = tile_lanes(tile)
        sums = [
            short_sum(
                strided_rows(streams(way, tile), strided_buf.at[number, way]),
                None, taps_ref, 2 * way, tile_lanes(tile, taps_first),
            )
            for way in range(2)
        ]
        driven = [one * two for one, two in zip(*sums)]
        for row, value in enumerate(parity_rows(driven)):
            driven_ref[16 * row : 16 * row + 16, cols] = value
        peak_buf[:, cols] = functools.reduce(jnp.maximum, [jnp.abs(value) for value in driven])

    each_tile(tiles, strided_buf.shape[0], drive)
    code_tiles(tiles, rows, coded_ref, driven_ref, peak_buf, levels_buf)


def code_tiles(tiles, rows, coded_ref, values_ref, peak_buf, levels_buf):
    each_tile(tiles, 4, lambda tile, _: place_level(peak_buf[:, tile_lanes(tile)], tile, peak_buf, levels_buf))
    coded_ref[tiles * rows : tiles * rows + 16] = levels_buf[...].astype(jnp.bfloat16)

    def code(tile, _):
        cols = tile_lanes(tile)
        gain = peak_buf[:, cols]
        gain = jnp.concatenate([gain, gain], axis=0)
        for row in range(0, rows, 16):
            put_coded(coded_ref, tile, row, values_ref[row : row + 16, cols], gain)

    each_tile(tiles, 4, code)


def first_kernel(
    projected_ref, taps_ref, feats_ref, in_ref, bias_ref, freq_ref, mid_ref, coded_ref, driven_ref, second_ref,
    rows_buf, rim_buf, taps_buf, strided_buf, peak_buf, levels_buf, feats_buf, in_buf, bias_buf, freq_buf, mid_buf,
    scaled_buf, sems, layer_sems,
):
    rows, size = rows_buf.shape[1:]
    tiles = size // 128

    @pl.when(lax.axis_index("ctx") == 0)
    def _():
        span = pl.ds(0, size)
        copies = [
            pltpu.make_async_copy(taps_ref.at[:, :, span], taps_buf, sems.at[0]),
            pltpu.make_async_copy(projected_ref.at[0, :, span], rows_buf.at[0], sems.at[1]),
            pltpu.make_async_copy(projected_ref.at[2, :, span], rows_buf.at[1], sems.at[2]),
            pltpu.make_async_copy(projected_ref.at[:, pl.ds(rows - 16, 16)], rim_buf, sems.at[3]),
        ]
        layer_bufs = (feats_buf, in_buf, bias_buf, freq_buf, mid_buf)
        layer_copies = [
            pltpu.make_async_copy(ref, buf, layer_sems.at[at])
            for at, (ref, buf) in enumerate(zip((feats_ref, in_ref, bias_ref, freq_ref, mid_ref), layer_bufs))
        ]
        for copy in layer_copies + copies:
            copy.start()
        for copy in layer_copies:
            copy.wait()
        second_ref[...] = second_layer(*layer_bufs, scaled_buf)
        for copy in copies:
            copy.wait()
        encode_tiles(
            tiles, rows, lambda way, tile: rows_buf[way, :, tile_lanes(tile)], taps_buf, 0, coded_ref, driven_ref,
            strided_buf, peak_buf, levels_buf,
        )

        for at in range(3):
            for group in range(rim_buf.shape[2] // 1024):
                there = tiles * rows + 16 + (3 * group + at) * 48
                values = [
                    rim_buf[at, :, (8 * group + way) * 128 : (8 * group + way + 1) * 128].astype(jnp.float32)[8:]
                    for way in range(8)
                ]
                values = pack_rims(values)
                for pair in range(3):
                    both = jnp.concatenate(values[2 * pair : 2 * pair + 2], axis=0)
                    coded_ref[there + 16 * pair : there + 16 * pair + 16] = both.astype(jnp.bfloat16)


def pack_rims(values):
    top = lax.broadcasted_iota(jnp.int32, (8, 128), 0) < 2
    return [
        jnp.where(top, pltpu.roll(values[6 + at // 3], 6 - 2 * (at % 3), 0), values[at]) for at in range(6)
    ]


def unpack_rims(values):
    place = lax.broadcasted_iota(jnp.int32, (8, 128), 0)
    rest = []
    for at in range(2):
        turned = [pltpu.roll(values[3 * at + way], 2 + 2 * way, 0) for way in range(3)]
        rest.append(jnp.where(place < 4, turned[0], jnp.where(place < 6, turned[1], turned[2])))
    return values + rest


def read_rims(coded_ref, rims_buf):
    groups = rims_buf.shape[2] // 1024
    start = coded_ref.shape[0] - groups * 144
    for at in range(3):
        for group in range(groups):
            there = start + (3 * group + at) * 48
            packed = coded_ref[there : there + 48].astype(jnp.float32)
            values = unpack_rims([packed[8 * way : 8 * way + 8] for way in range(6)])
            for way, value in enumerate(values):
                rims_buf[at, :, (8 * group + way) * 128 : (8 * group + way + 1) * 128] = value


def encode_kernel(
    first, projected_ref, taps_ref, coded_ref, driven_ref, strided_buf, peak_buf, levels_buf
):
    rows, size = driven_ref.shape

    @pl.when(lax.axis_index("ctx") == 0)
    def _():
        encode_tiles(
            size // 128, rows, lambda way, tile: projected_ref[2 * way, :, tile_lanes(tile, first)], taps_ref, first,
            coded_ref, driven_ref, strided_buf, peak_buf, levels_buf,
        )


def filter_kernel(first, fresh, out_ref, decay_ref, skip_ref, places_ref, forward_ref, *refs):
    if fresh:
        *layer_refs, second_ref, near_ref, far_ref, halves_ref, raw_buf, parts_buf, spec_buf, scale_buf, second_buf, scaled_buf = refs
        place = lax.axis_index("ctx")

        @pl.when(place == 0)
        def _():
            second_buf[...] = second_ref[...]

        @pl.when(place != 0)
        def _():
            second_buf[...] = second_layer(*layer_refs, scaled_buf)

        second_high, second_low = halves(second_buf[...])
        halves_ref[...] = jnp.concatenate([second_high, second_high, second_low], axis=1)
    else:
        halves_ref, near_ref, far_ref, raw_buf, parts_buf, spec_buf, scale_buf = refs
    rows, width = near_ref.shape[0] // 2, near_ref.shape[1]
    half = rows // 2
    out_high, out_low = halves(out_ref[:, first : first + width])
    raw_buf[...] = jnp.dot(
        halves_ref[...], jnp.concatenate([out_high, out_low, out_high], axis=0), preferred_element_type=jnp.float32
    )

    def decay(tile, _):
        cols = tile_lanes(tile)
        fall = -decay_ref[:, tile_lanes(tile, first)]
        total = jnp.zeros((8, 128), jnp.float32)
        for row in range(0, 2 * rows, 16):
            taps = raw_buf[row : row + 16, cols] * jnp.exp(fall * places_ref[row : row + 16])
            total = total + (taps[:8] * taps[:8] + taps[8:] * taps[8:])
            parity = row % rows // half
            put_halves(parts_buf, parity, row % half, tile_lanes(tile, row // rows * width), taps)
        for step in (1, 2, 4):
            total = total + pltpu.roll(total, step, 0)
        scale_buf[:, cols] = 1.0 / jnp.sqrt(total + 1e-05)

    each_tile(width // 128, 4, decay)
    forward_dots(forward_ref, parts_buf, spec_buf)

    def shape(tile, _):
        cols = tile_lanes(tile)
        scale = scale_buf[:, cols]
        scale = jnp.concatenate([scale, scale], axis=0)
        skip = skip_ref[:, tile_lanes(tile, first)]
        for row in range(0, half, 16):
            low = [value * scale for value in unfolded(spec_buf, row, cols)]
            high = [value * scale for value in unfolded(spec_buf, row, tile_lanes(tile, width))]
            sign = 1 if row < half // 2 else -1
            turned = [-sign * low[1], sign * low[0], sign * low[3], -sign * low[2]]
            low = [low[0] + skip, low[1], low[2] + skip, low[3]]
            for at in range(4):
                near_ref[at * half + row : at * half + row + 16, cols] = low[at]
                far_ref[at * half + row : at * half + row + 16, cols] = high[at] + turned[at]

    each_tile(width // 128, 4, shape)


def own_kernel(
    first, send, projected_ref, rims_ref, taps_ref, near_ref, far_ref, forward_ref, backward_ref, *refs
):
    if send:
        base_ref, right_ref, mixed_ref, coded_ref, *bufs = refs
    else:
        *driven_refs, _, base_ref, right_ref, mixed_ref = refs[:6]
        bufs = refs[6:]
    rims_buf, strided_buf, parts_buf, spec_buf, bins_buf, mixed_buf, sems = bufs[:7]
    rows, width = base_ref.shape
    half = rows // 2
    tiles = width // 128
    read_rims(rims_ref, rims_buf)
    place = lax.axis_index("ctx")

    def sums_of(tile, number, ats):
        cols = tile_lanes(tile, first)
        sums = []
        for at in ats:
            parts = strided_rows(projected_ref[at, :, cols], strided_buf.at[number, at])
            sums.append(short_sum(parts, rims_buf[at, :, cols], taps_ref, at, cols))
        return sums

    def put_right(tile, values):
        for at, value in enumerate(parity_rows(values)):
            right_ref[16 * at : 16 * at + 16, tile_lanes(tile)] = value

    def drive(tile, number):
        sums = sums_of(tile, number, range(3))
        put_right(tile, sums[1])
        driven = [one * two for one, two in zip(sums[0], sums[2])]
        for at, value in enumerate(parity_rows(driven)):
            put_halves(parts_buf, 16 * at // half, 16 * at % half, tile_lanes(tile), value)

    if send:
        each_tile(tiles, strided_buf.shape[0], drive)
    else:

        @pl.when(place != 0)
        def _():
            each_tile(tiles, strided_buf.shape[0], drive)

        @pl.when(place == 0)
        def _():
            each_tile(tiles, strided_buf.shape[0], lambda tile, number: put_right(tile, sums_of(tile, number, [1])[0]))
            start = 0
            for ref in driven_refs:

                def recall(tile, _, ref=ref, start=start):
                    for row in range(0, rows, 16):
                        value = ref[row : row + 16, tile_lanes(tile)]
                        put_halves(parts_buf, row // half, row % half, tile_lanes(tile, start), value)

                each_tile(ref.shape[1] // 128, 4, recall)
                start += ref.shape[1]

    forward_dots(forward_ref, parts_buf, spec_buf)
    if send:
        conv_buf, peak_buf, levels_buf = bufs[7:]

        @pl.when(place == 0)
        def _():
            each_tile(
                tiles, 4,
                lambda tile, _: filtered(spec_buf, far_ref, bins_buf, tile_lanes(tile), tile_lanes(tile)),
            )
            backward_dots(backward_ref, bins_buf, conv_buf)

            def peaks(tile, _):
                cols = tile_lanes(tile)
                peak_buf[:, cols] = functools.reduce(
                    jnp.maximum, [jnp.abs(conv_buf[row : row + 8, cols]) for row in range(0, rows, 8)]
                )

            each_tile(tiles, 4, peaks)
            code_tiles(tiles, rows, coded_ref, conv_buf, peak_buf, levels_buf)

    each_tile(
        tiles, 4, lambda tile, _: filtered(spec_buf, near_ref, bins_buf, tile_lanes(tile), tile_lanes(tile))
    )
    backward_dots(backward_ref, bins_buf, base_ref)

    @pl.when(place == 0)
    def _():
        def mix(tile):
            cols = tile_lanes(tile)
            return [right_ref[at : at + 16, cols] * base_ref[at : at + 16, cols] for at in range(0, rows, 16)]

        mix_out(mix, tiles, first, mixed_ref, mixed_buf, strided_buf.at[:, 0], sems)


def mix_out(mix, tiles, first, mixed_ref, buf, strided_buf, sems):
    parts = sems.shape[0]
    copies = []
    for part in range(parts):
        start, count = part * (tiles // parts), tiles // parts

        def one(tile, number, start=start):
            buf[:, tile_lanes(start + tile)] = natural_rows(mix(start + tile), strided_buf.at[number]).astype(jnp.bfloat16)

        each_tile(count, strided_buf.shape[0], one)
        span = slice(start * 128, (start + count) * 128)
        copy = pltpu.make_async_copy(
            buf.at[:, span], mixed_ref.at[:, pl.ds(first + start * 128, count * 128)], sems.at[part]
        )
        copy.start()
        copies.append(copy)
    for copy in copies:
        copy.wait()


def read_levels(coded_ref, levels_buf, tiles, rows):
    levels_buf[...] = coded_ref[tiles * rows : tiles * rows + 16].astype(jnp.float32)


def join_kernel(
    first, coded_ref, far_ref, base_ref, right_ref, forward_ref, backward_ref, sofar_ref, mixed_ref,
    parts_buf, spec_buf, bins_buf, conv_buf, strided_buf, buf, levels_buf, sems,
):
    rows, width = conv_buf.shape
    half = rows // 2
    tiles = width // 128

    @pl.when(lax.axis_index("ctx") != 0)
    def _():
        read_levels(coded_ref, levels_buf, tiles, rows)

        def spread_out(tile, _):
            decode = decoder(levels_buf, tile)
            for row in range(0, rows, 16):
                value = decode(coded_ref[tile_rows(tile, row), :])
                put_halves(parts_buf, row // half, row % half, tile_lanes(tile), value)

        each_tile(tiles, 4, spread_out)
        forward_dots(forward_ref, parts_buf, spec_buf)
        each_tile(
            tiles, 4, lambda tile, _: filtered(spec_buf, far_ref, bins_buf, tile_lanes(tile), tile_lanes(tile, first))
        )
        backward_dots(backward_ref, bins_buf, conv_buf)

        def mix(tile):
            cols = tile_lanes(tile, first)
            return [
                right_ref[at : at + 16, cols] * (conv_buf[at : at + 16, tile_lanes(tile)] + base_ref[at : at + 16, cols])
                for at in range(0, rows, 16)
            ]

        mix_out(mix, tiles, first, mixed_ref, buf, strided_buf, sems)


def last_kernel(
    first, coded_ref, base_ref, right_ref, sofar_ref, mixed_ref, strided_buf, buf, levels_buf, sems
):
    rows, width = base_ref.shape
    tiles = width // 128

    @pl.when(lax.axis_index("ctx") != 0)
    def _():
        read_levels(coded_ref, levels_buf, tiles, rows)

        def mix(tile):
            cols = tile_lanes(tile)
            decode = decoder(levels_buf, tile)
            return [
                right_ref[at : at + 16, cols] * (decode(coded_ref[tile_rows(tile, at), :]) + base_ref[at : at + 16, cols])
                for at in range(0, rows, 16)
            ]

        mix_out(mix, tiles, first, mixed_ref, buf, strided_buf, sems)


def params(mib=40):
    return pltpu.CompilerParams(vmem_limit_bytes=mib * 1024 * 1024)


def cost(us):
    return pl.CostEstimate(flops=int(us * 1e9), bytes_accessed=int(us * 3e6), transcendentals=0)


def one_way(
    projected, short_weight, pos_in, pos_bias, sine_freq, pos_mid, pos_out, decay_rate, skip_gain
):
    _, rows, width = projected.shape
    half = rows // 2
    total_len = 2 * rows
    ahead = [width // 8, width * 5 // 8]
    middle = sum(ahead)
    behind = width - middle
    forward, backward = odd_tables(rows)
    taps = jnp.transpose(short_weight, (1, 0, 2))
    in_vmem = pl.BlockSpec(memory_space=pltpu.VMEM)
    in_hbm = pl.BlockSpec(memory_space=pltpu.HBM)
    floats, shorts = functools.partial(pltpu.VMEM, dtype=jnp.float32), functools.partial(pltpu.VMEM, dtype=jnp.bfloat16)
    pairs = [(0, 1)]

    def arrays(*shapes, dtype=jnp.float32):
        return [jax.ShapeDtypeStruct(shape, dtype) for shape in shapes]

    def message(size, more=0):
        return arrays((size // 128 * rows + 16 + more, 128), dtype=jnp.bfloat16)

    order = parity_order(rows)
    places = np.concatenate([order, order + rows]).astype(np.float32)
    feats = feature_table(places, total_len)
    places = np.repeat(places[:, None], 128, 1)
    layers = (feats, pos_in, pos_bias[None, :], sine_freq[None, :], pos_mid)
    tile_bufs = [floats((2, 2, rows, 128)), floats((8, width)), floats((16, 128))]
    one, two = ahead
    one_code, one_driven, second = pl.pallas_call(
        first_kernel,
        in_specs=[in_hbm] * 7,
        out_specs=[in_vmem] * 3,
        out_shape=message(one, width // 128 * 18) + arrays((rows, one), (total_len, pos_mid.shape[1])),
        scratch_shapes=[shorts((2, rows, one)), shorts((3, 16, width)), floats((3, TAPS, one))]
        + tile_bufs
        + [floats(array.shape) for array in layers]
        + [floats((feats.shape[0], pos_in.shape[1]))]
        + [pltpu.SemaphoreType.DMA((4,)), pltpu.SemaphoreType.DMA((5,))],
        compiler_params=params(),
        cost_estimate=cost(1),
        name="first",
    )(*[pltpu.with_memory_space_constraint(jnp.asarray(array), pltpu.HBM) for array in (projected, taps, *layers)])
    one_code = lax.ppermute(one_code, "ctx", pairs)
    two_code, two_driven = pl.pallas_call(
        functools.partial(encode_kernel, one),
        in_specs=[in_vmem] * 2,
        out_specs=[in_vmem] * 2,
        out_shape=message(two) + arrays((rows, two)),
        scratch_shapes=tile_bufs,
        compiler_params=params(),
        cost_estimate=cost(1),
        name="encode",
    )(projected, taps)
    two_code = lax.ppermute(two_code, "ctx", pairs)

    def spectra(first, size, *more):
        fresh = len(more) > 1
        return pl.pallas_call(
            functools.partial(filter_kernel, first, fresh),
            in_specs=[in_vmem] * (5 + len(more)),
            out_specs=[in_vmem] * (2 + fresh),
            out_shape=arrays((total_len, size), (total_len, size))
            + arrays((total_len, 3 * pos_mid.shape[1]), dtype=jnp.bfloat16) * fresh,
            scratch_shapes=[
                floats((total_len, size)),
                shorts((2, rows, 2 * size)),
                floats((2, rows, 2 * size)),
                floats((8, size)),
            ]
            + [floats((total_len, pos_mid.shape[1])), floats((feats.shape[0], pos_in.shape[1]))] * fresh,
            compiler_params=params(),
            cost_estimate=cost(2),
            name="filter",
        )(pos_out, decay_rate[None, :], skip_gain[None, :], places, forward, *more)

    last_near, last_far, second_halves = spectra(middle, behind, *layers, second)

    def own(first, size, send, near, far, *more):
        return pl.pallas_call(
            functools.partial(own_kernel, first, send),
            in_specs=[in_vmem] * 7 + [in_vmem, in_vmem, in_hbm][: len(more)],
            out_specs=[in_vmem, in_vmem, in_hbm] + [in_vmem] * send,
            out_shape=arrays((rows, size), (rows, size))
            + arrays((rows, width), dtype=jnp.bfloat16)
            + message(size) * send,
            input_output_aliases={} if send else {9: 2},
            scratch_shapes=[
                floats((3, 8, width)),
                floats((2, 3, rows, 128)),
                shorts((2, rows, size)),
                floats((2, rows, size)),
                shorts((2, 2 * rows, size)),
                shorts((rows, size)),
                pltpu.SemaphoreType.DMA((2,)),
            ]
            + [floats((rows, size)), floats((8, size)), floats((16, 128))] * send,
            compiler_params=params(),
            cost_estimate=cost(2),
            name="own",
        )(projected, one_code, taps, near, far, forward, backward, *more)

    last_base, last_right, mixed, code = own(middle, behind, True, last_near, last_far)
    last_code = lax.ppermute(code, "ctx", pairs)
    near, far = spectra(0, middle, second_halves)
    base, right, mixed = own(0, middle, False, near, far, one_driven, two_driven, mixed)
    for first, size, code in ((0, one, one_code), (one, two, two_code)):
        mixed = pl.pallas_call(
            functools.partial(join_kernel, first),
            in_specs=[in_vmem] * 6 + [in_hbm],
            out_specs=in_hbm,
            out_shape=jax.ShapeDtypeStruct((rows, width), jnp.bfloat16),
            input_output_aliases={6: 0},
            scratch_shapes=[
                shorts((2, rows, size)),
                floats((2, rows, size)),
                shorts((2, 2 * rows, size)),
                floats((rows, size)),
                floats((4, rows, 128)),
                shorts((rows, size)),
                floats((16, 128)),
                pltpu.SemaphoreType.DMA((2,)),
            ],
            compiler_params=params(),
            cost_estimate=cost(1),
            name="join",
        )(code, far, base, right, forward, backward, mixed)
    return pl.pallas_call(
        functools.partial(last_kernel, middle),
        in_specs=[in_vmem] * 3 + [in_hbm],
        out_specs=in_hbm,
        out_shape=jax.ShapeDtypeStruct((rows, width), jnp.bfloat16),
        input_output_aliases={3: 0},
        scratch_shapes=[
            floats((4, rows, 128)),
            shorts((rows, behind)),
            floats((16, 128)),
            pltpu.SemaphoreType.DMA((2,)),
        ],
        compiler_params=params(),
        cost_estimate=cost(1),
        name="last",
    )(last_code, last_base, last_right, mixed)


def turn_table(outer_ids, inner_ids, modulus):
    product_grid = outer_ids[:, None] * inner_ids[None, :] % modulus
    angles = product_grid.astype(jnp.float32) * (2.0 * math.pi / modulus)
    return (jnp.cos(angles), jnp.sin(angles))


def section_outer(table, data):
    return jnp.einsum(
        "ka,cab->ckb", table, data, precision=HIGHEST, preferred_element_type=jnp.float32
    )


def section_inner(table, data):
    return jnp.einsum(
        "ckb,bj->ckj", data, table, precision=HIGHEST, preferred_element_type=jnp.float32
    )


def padded_spectrum(signal, outer_count, inner_count, tables):
    cos_half, sin_half, cos_twist, sin_twist, cos_inner, sin_inner = tables
    shaped = signal.reshape(signal.shape[0], outer_count // 2, inner_count)
    real_one = section_outer(cos_half, shaped)
    imag_one = -section_outer(sin_half, shaped)
    real_two = real_one * cos_twist + imag_one * sin_twist
    imag_two = imag_one * cos_twist - real_one * sin_twist
    spec_real = section_inner(cos_inner, real_two) + section_inner(sin_inner, imag_two)
    spec_imag = section_inner(cos_inner, imag_two) - section_inner(sin_inner, real_two)
    return (spec_real, spec_imag)


def causal_local(driven_cols, normed_cols, total_len):
    full_len = 2 * total_len
    inner_count = math.gcd(total_len, 128)
    outer_count = full_len // inner_count
    outer_full = jnp.arange(outer_count, dtype=jnp.int32)
    outer_half = jnp.arange(outer_count // 2, dtype=jnp.int32)
    inner_ids = jnp.arange(inner_count, dtype=jnp.int32)
    cos_half, sin_half = turn_table(outer_full, outer_half, outer_count)
    cos_twist, sin_twist = turn_table(outer_full, inner_ids, full_len)
    cos_inner, sin_inner = turn_table(inner_ids, inner_ids, inner_count)
    tables = (cos_half, sin_half, cos_twist, sin_twist, cos_inner, sin_inner)
    sig_real, sig_imag = padded_spectrum(driven_cols, outer_count, inner_count, tables)
    fil_real, fil_imag = padded_spectrum(normed_cols, outer_count, inner_count, tables)
    prod_real = sig_real * fil_real - sig_imag * fil_imag
    prod_imag = sig_real * fil_imag + sig_imag * fil_real
    back_real = section_inner(cos_inner, prod_real) - section_inner(sin_inner, prod_imag)
    back_imag = section_inner(sin_inner, prod_real) + section_inner(cos_inner, prod_imag)
    turned_real = back_real * cos_twist - back_imag * sin_twist
    turned_imag = back_real * sin_twist + back_imag * cos_twist
    cos_last, sin_last = turn_table(outer_half, outer_full, outer_count)
    result = (
        section_outer(cos_last, turned_real) - section_outer(sin_last, turned_imag)
    ) / full_len
    return result.reshape(driven_cols.shape[0], total_len)


def exchanged(
    projected, short_weight, pos_in, pos_bias, sine_freq, pos_mid, pos_out, decay_rate, skip_gain
):
    ctx_count = lax.axis_size("ctx")
    ctx_place = lax.axis_index("ctx")
    block_rows = projected.shape[1]
    total_len = block_rows * ctx_count
    rim_rows = shifted(projected[:, block_rows - (TAPS - 1) :, :], "ctx", 1)
    extended = jnp.concatenate([rim_rows, projected], axis=1)
    short_out = jnp.zeros(projected.shape, jnp.float32)
    for tap_index in range(TAPS):
        offset = TAPS - 1 - tap_index
        short_out = short_out + short_weight[tap_index][:, None, :] * extended[
            :, offset : offset + block_rows, :
        ].astype(jnp.float32)
    left_gate, right_gate, value_stream = (short_out[0], short_out[1], short_out[2])
    driven = left_gate * value_stream
    own_width = driven.shape[1] // ctx_count
    driven_cols = lax.all_to_all(driven.T, "ctx", split_axis=0, concat_axis=1, tiled=True)
    own_out = lax.dynamic_slice_in_dim(pos_out, ctx_place * own_width, own_width, 1)
    own_decay = lax.dynamic_slice_in_dim(decay_rate, ctx_place * own_width, own_width, 0)
    positions = jnp.arange(total_len, dtype=jnp.int32).astype(jnp.float32)
    long_filter = filter_rows(
        positions, total_len, pos_in, pos_bias, sine_freq, pos_mid, own_out, own_decay
    )
    normed = long_filter / jnp.sqrt(jnp.sum(long_filter * long_filter, axis=0) + 1e-05)
    conv_cols = causal_local(driven_cols, normed.T, total_len)
    long_conv = lax.all_to_all(conv_cols, "ctx", split_axis=1, concat_axis=0, tiled=True).T
    return (right_gate * (long_conv + skip_gain[None, :] * driven)).astype(jnp.bfloat16)


def body(projected, *others):
    if lax.axis_size("ctx") == 2:
        return one_way(projected, *others)
    return exchanged(projected, *others)


def solution(mesh):
    placed = (
        P(None, ("dp", "ctx"), "chan"),
        P(None, None, "chan"),
        P(),
        P(),
        P(),
        P(),
        P(None, "chan"),
        P("chan"),
        P("chan"),
    )
    return jax.shard_map(
        body, mesh=mesh, in_specs=placed, out_specs=P(("dp", "ctx"), "chan"), check_vma=False
    )
```

```python
import functools
import math

import jax
import jax.numpy as jnp
import numpy as np
from jax import lax
from jax.experimental import pallas as pl
from jax.experimental.pallas import tpu as pltpu
from jax.sharding import PartitionSpec as P

BANDS = 16
TAPS = 7
SPAN = 250.0
TINY = 1e-30

HIGHEST = lax.Precision.HIGHEST


def shifted(x, axis, by):
    size = lax.axis_size(axis)
    pairs = [(i, i + by) for i in range(size) if 0 <= i + by < size]
    return lax.ppermute(x, axis, pairs)


def features(positions, total_len):
    band_ids = jnp.arange(1, BANDS + 1, dtype=jnp.float32)
    angles = positions[:, None] * band_ids[None, :] * (2.0 * math.pi / total_len)
    return jnp.concatenate(
        [positions[:, None] / total_len, jnp.cos(angles), jnp.sin(angles)], axis=1
    )


def second_rows(positions, total_len, pos_in, pos_bias, sine_freq, pos_mid):
    inputs = features(positions, total_len)
    first_layer = jnp.sin(
        sine_freq
        * (
            jnp.dot(inputs, pos_in, precision=HIGHEST, preferred_element_type=jnp.float32)
            + pos_bias
        )
    )
    return jnp.sin(
        sine_freq
        * jnp.dot(first_layer, pos_mid, precision=HIGHEST, preferred_element_type=jnp.float32)
    )


def filter_rows(positions, total_len, pos_in, pos_bias, sine_freq, pos_mid, pos_out, decay_rate):
    second_layer = second_rows(positions, total_len, pos_in, pos_bias, sine_freq, pos_mid)
    raw_filter = jnp.dot(
        second_layer, pos_out, precision=HIGHEST, preferred_element_type=jnp.float32
    )
    return raw_filter * jnp.exp(-decay_rate[None, :] * positions[:, None])


def halves(x):
    high = x.astype(jnp.bfloat16)
    low = (x - high.astype(jnp.float32)).astype(jnp.bfloat16)
    return high, low


def feature_table(places, total_len):
    bands = np.arange(1, BANDS + 1, dtype=np.float32)
    angles = places[:, None] * bands[None, :] * np.float32(2.0 * math.pi / total_len)
    first = places[:, None] / np.float32(total_len)
    table = np.concatenate([first, np.cos(angles), np.sin(angles), np.ones_like(first)], axis=1)
    spare = np.zeros((places.shape[0], -table.shape[1] % 8))
    return np.concatenate([table, spare], axis=1).astype(np.float32).T.copy()


def parity_order(rows):
    place = np.arange(rows)
    parity, inner = place // (rows // 2), place % (rows // 2)
    return rows // 8 * (inner % 8) + inner // 8 * 2 + parity


def table_columns(table):
    high = table.astype(jnp.bfloat16)
    low = (table - high.astype(np.float32)).astype(jnp.bfloat16)
    return np.concatenate([high, high, low], axis=1)


def odd_tables(rows):
    half = rows // 2
    order = np.concatenate([np.arange(0, half, 2), np.arange(1, half, 2)])
    turns = (2 * order[:, None] + 1) * parity_order(rows)[None, :] % (4 * rows)
    angles = turns * (np.pi / (2 * rows))
    forward = np.concatenate([np.cos(angles), -np.sin(angles)], axis=0).astype(np.float32)
    pieces = [forward[:, :half], forward[:, half:]]
    return (
        np.concatenate([table_columns(piece) for piece in pieces], axis=0),
        np.concatenate([table_columns(piece.T / np.float32(rows)) for piece in pieces], axis=0),
    )


def each_tile(tiles, unroll, action):
    count = math.gcd(tiles, unroll)

    def step(at, _):
        for number in range(count):
            action(at * count + number, number)
        return 0

    if tiles == count:
        step(0, 0)
    else:
        lax.fori_loop(0, tiles // count, step, 0)


def put_halves(ref, parity, row, cols, value):
    size = ref.shape[1] // 2
    high, low = halves(value)
    count = value.shape[0]
    ref[parity, row : row + count, cols] = high
    ref[parity, size + row : size + row + count, cols] = low


def three_pass(table, ref, parity):
    size = ref.shape[1] // 2
    both = jnp.concatenate([ref[parity], ref[parity, :size]], axis=0)
    return jnp.dot(table, both, preferred_element_type=jnp.float32)


def forward_dots(forward_ref, parts_ref, spec_ref):
    rows = spec_ref.shape[1]
    for parity in range(2):
        spec_ref[parity] = three_pass(forward_ref[parity * rows : (parity + 1) * rows], parts_ref, parity)


def backward_dots(backward_ref, bins_ref, conv_ref):
    half = conv_ref.shape[0] // 2
    for parity in range(2):
        rows = slice(parity * half, (parity + 1) * half)
        conv_ref[rows] = three_pass(backward_ref[rows], bins_ref, parity)


def unfolded(spec_ref, row, cols):
    half = spec_ref.shape[1] // 2
    even_cos, odd_cos = spec_ref[0, row : row + 16, cols], spec_ref[1, row : row + 16, cols]
    sine = slice(half + row, half + row + 16)
    even_sin, odd_sin = spec_ref[0, sine, cols], spec_ref[1, sine, cols]
    return even_cos + odd_cos, even_sin + odd_sin, even_cos - odd_cos, odd_sin - even_sin


def filtered(spec_ref, filter_ref, bins_ref, cols, filter_cols):
    half = spec_ref.shape[1] // 2
    for row in range(0, half, 16):
        real, imag, real_far, imag_far = unfolded(spec_ref, row, cols)
        taps = [filter_ref[at * half + row : at * half + row + 16, filter_cols] for at in range(4)]
        out_real, out_imag = real * taps[0] - imag * taps[1], real * taps[1] + imag * taps[0]
        far_real = real_far * taps[2] - imag_far * taps[3]
        far_imag = real_far * taps[3] + imag_far * taps[2]
        put_halves(bins_ref, 0, row, cols, out_real + far_real)
        put_halves(bins_ref, 0, half + row, cols, out_imag - far_imag)
        put_halves(bins_ref, 1, row, cols, out_real - far_real)
        put_halves(bins_ref, 1, half + row, cols, out_imag + far_imag)


def strided_rows(values, buf):
    buf[...] = values.astype(jnp.float32)
    count = buf.shape[0] // 8
    return [buf[pl.ds(v, 8, stride=count), :] for v in range(count)]


def short_sum(parts, rim, taps_ref, at, cols):
    top = lax.broadcasted_iota(jnp.int32, (8, 128), 0) == 0
    before = {}
    for back in range(1, TAPS):
        edge = 0.0 if rim is None else rim[8 - back : 9 - back]
        before[-back] = jnp.where(top, edge, pltpu.roll(parts[-back], 1, 0))
    taps = [jnp.broadcast_to(taps_ref[at, k : k + 1, cols], (8, 128)) for k in range(TAPS)]
    sums = []
    for v in range(len(parts)):
        terms = [taps[k] * (parts[v - k] if v >= k else before[v - k]) for k in range(TAPS)]
        sums.append(((terms[0] + terms[1]) + (terms[2] + terms[3])) + ((terms[4] + terms[5]) + terms[6]))
    return sums


def parity_rows(parts):
    ordered = parts[0::2] + parts[1::2]
    return [jnp.concatenate(ordered[i : i + 2], axis=0) for i in range(0, len(ordered), 2)]


def natural_rows(ref_rows, buf):
    count = buf.shape[0] // 8
    for at, value in enumerate(ref_rows):
        for piece in range(2):
            number = 2 * at + piece
            v = number % (count // 2) * 2 + number // (count // 2)
            buf[pl.ds(v, 8, stride=count), :] = value[8 * piece : 8 * piece + 8]
    return buf[...]


def tile_lanes(tile, first=0):
    return pl.ds(pl.multiple_of(first + tile * 128, 128), 128)


def tile_rows(tile, row, count=16):
    return pl.ds(pl.multiple_of(tile * 128 + row, 16), count)


def place_level(peak, tile, peak_buf, levels_buf):
    for step in (1, 2, 4):
        peak = jnp.maximum(peak, pltpu.roll(peak, step, 0))
    level = jnp.maximum(peak, TINY)
    wide = level * 65537.0
    level = wide - (wide - level)
    peak_buf[:, tile_lanes(tile)] = SPAN / level
    levels_buf[pl.ds(tile, 1), :] = level[0:1]


def put_coded(coded_ref, tile, row, value, gain):
    coded = jnp.exp2(jnp.abs(value) * gain - SPAN / 2)
    coded_ref[tile_rows(tile, row), :] = jnp.where(value < 0, -coded, coded).astype(jnp.bfloat16)


def decoder(levels_buf, tile):
    level = levels_buf[pl.ds(tile, 1), :]
    slope = jnp.broadcast_to(level * (1.0 / (math.log(2.0) * SPAN)), (16, 128))
    middle = jnp.broadcast_to(level / 2, (16, 128))

    def decode(coded):
        coded = coded.astype(jnp.float32)
        size = jnp.log(jnp.abs(coded)) * slope + middle
        return jnp.where(coded < 0, -size, size)

    return decode


def second_layer(feats_ref, in_ref, bias_ref, freq_ref, mid_ref, scaled_buf):
    dot = functools.partial(
        lax.dot_general,
        dimension_numbers=(((0,), (0,)), ((), ())),
        precision=HIGHEST,
        preferred_element_type=jnp.float32,
    )
    count = in_ref.shape[0]
    freq = freq_ref[...]
    scaled_buf[...] = jnp.zeros_like(scaled_buf)
    scaled_buf[0:count] = in_ref[...] * freq
    scaled_buf[count : count + 1] = bias_ref[...] * freq
    layer = jnp.sin(dot(scaled_buf[...], feats_ref[...]))
    return jnp.sin(dot(mid_ref[...] * freq, layer)).T


def encode_tiles(tiles, rows, streams, taps_ref, taps_first, coded_ref, driven_ref, strided_buf, peak_buf, levels_buf):
    def drive(tile, number):
        cols = tile_lanes(tile)
        sums = [
            short_sum(
                strided_rows(streams(way, tile), strided_buf.at[number, way]),
                None, taps_ref, 2 * way, tile_lanes(tile, taps_first),
            )
            for way in range(2)
        ]
        driven = [one * two for one, two in zip(*sums)]
        for row, value in enumerate(parity_rows(driven)):
            driven_ref[16 * row : 16 * row + 16, cols] = value
        peak_buf[:, cols] = functools.reduce(jnp.maximum, [jnp.abs(value) for value in driven])

    each_tile(tiles, strided_buf.shape[0], drive)
    code_tiles(tiles, rows, coded_ref, driven_ref, peak_buf, levels_buf)


def code_tiles(tiles, rows, coded_ref, values_ref, peak_buf, levels_buf):
    each_tile(tiles, 4, lambda tile, _: place_level(peak_buf[:, tile_lanes(tile)], tile, peak_buf, levels_buf))
    coded_ref[tiles * rows : tiles * rows + 16] = levels_buf[...].astype(jnp.bfloat16)

    def code(tile, _):
        cols = tile_lanes(tile)
        gain = peak_buf[:, cols]
        gain = jnp.concatenate([gain, gain], axis=0)
        for row in range(0, rows, 16):
            put_coded(coded_ref, tile, row, values_ref[row : row + 16, cols], gain)

    each_tile(tiles, 4, code)


def first_kernel(
    projected_ref, taps_ref, coded_ref, driven_ref, rows_buf, rim_buf, taps_buf, strided_buf, peak_buf, levels_buf, sems
):
    rows, size = rows_buf.shape[1:]
    tiles = size // 128

    @pl.when(lax.axis_index("ctx") == 0)
    def _():
        span = pl.ds(0, size)
        copies = [
            pltpu.make_async_copy(taps_ref.at[:, :, span], taps_buf, sems.at[0]),
            pltpu.make_async_copy(projected_ref.at[0, :, span], rows_buf.at[0], sems.at[1]),
            pltpu.make_async_copy(projected_ref.at[2, :, span], rows_buf.at[1], sems.at[2]),
            pltpu.make_async_copy(projected_ref.at[:, pl.ds(rows - 16, 16)], rim_buf, sems.at[3]),
        ]
        for copy in copies:
            copy.start()
        for copy in copies:
            copy.wait()
        encode_tiles(
            tiles, rows, lambda way, tile: rows_buf[way, :, tile_lanes(tile)], taps_buf, 0, coded_ref, driven_ref,
            strided_buf, peak_buf, levels_buf,
        )

        for at in range(3):
            for group in range(rim_buf.shape[2] // 1024):
                there = tiles * rows + 16 + (3 * group + at) * 48
                values = [
                    rim_buf[at, :, (8 * group + way) * 128 : (8 * group + way + 1) * 128].astype(jnp.float32)[8:]
                    for way in range(8)
                ]
                values = pack_rims(values)
                for pair in range(3):
                    both = jnp.concatenate(values[2 * pair : 2 * pair + 2], axis=0)
                    coded_ref[there + 16 * pair : there + 16 * pair + 16] = both.astype(jnp.bfloat16)


def pack_rims(values):
    top = lax.broadcasted_iota(jnp.int32, (8, 128), 0) < 2
    return [
        jnp.where(top, pltpu.roll(values[6 + at // 3], 6 - 2 * (at % 3), 0), values[at]) for at in range(6)
    ]


def unpack_rims(values):
    place = lax.broadcasted_iota(jnp.int32, (8, 128), 0)
    rest = []
    for at in range(2):
        turned = [pltpu.roll(values[3 * at + way], 2 + 2 * way, 0) for way in range(3)]
        rest.append(jnp.where(place < 4, turned[0], jnp.where(place < 6, turned[1], turned[2])))
    return values + rest


def read_rims(coded_ref, rims_buf):
    groups = rims_buf.shape[2] // 1024
    start = coded_ref.shape[0] - groups * 144
    for at in range(3):
        for group in range(groups):
            there = start + (3 * group + at) * 48
            packed = coded_ref[there : there + 48].astype(jnp.float32)
            values = unpack_rims([packed[8 * way : 8 * way + 8] for way in range(6)])
            for way, value in enumerate(values):
                value = jnp.where(lax.axis_index("ctx") == 0, 0.0, value)
                rims_buf[at, :, (8 * group + way) * 128 : (8 * group + way + 1) * 128] = value


def encode_kernel(
    first, projected_ref, taps_ref, coded_ref, driven_ref, strided_buf, peak_buf, levels_buf
):
    rows, size = driven_ref.shape

    @pl.when(lax.axis_index("ctx") == 0)
    def _():
        encode_tiles(
            size // 128, rows, lambda way, tile: projected_ref[2 * way, :, tile_lanes(tile, first)], taps_ref, first,
            coded_ref, driven_ref, strided_buf, peak_buf, levels_buf,
        )


def filter_kernel(first, fresh, out_ref, decay_ref, skip_ref, places_ref, forward_ref, *refs):
    if fresh:
        *layer_refs, near_ref, far_ref, halves_ref, raw_buf, parts_buf, spec_buf, scale_buf, scaled_buf = refs
        second_high, second_low = halves(second_layer(*layer_refs, scaled_buf))
        halves_ref[...] = jnp.concatenate([second_high, second_high, second_low], axis=1)
    else:
        halves_ref, near_ref, far_ref, raw_buf, parts_buf, spec_buf, scale_buf = refs
    rows, width = near_ref.shape[0] // 2, near_ref.shape[1]
    half = rows // 2
    out_high, out_low = halves(out_ref[:, first : first + width])
    raw_buf[...] = jnp.dot(
        halves_ref[...], jnp.concatenate([out_high, out_low, out_high], axis=0), preferred_element_type=jnp.float32
    )

    def decay(tile, _):
        cols = tile_lanes(tile)
        fall = -decay_ref[:, tile_lanes(tile, first)]
        total = jnp.zeros((8, 128), jnp.float32)
        for row in range(0, 2 * rows, 16):
            taps = raw_buf[row : row + 16, cols] * jnp.exp(fall * places_ref[row : row + 16])
            total = total + (taps[:8] * taps[:8] + taps[8:] * taps[8:])
            parity = row % rows // half
            put_halves(parts_buf, parity, row % half, tile_lanes(tile, row // rows * width), taps)
        for step in (1, 2, 4):
            total = total + pltpu.roll(total, step, 0)
        scale_buf[:, cols] = 1.0 / jnp.sqrt(total + 1e-05)

    each_tile(width // 128, 4, decay)
    forward_dots(forward_ref, parts_buf, spec_buf)

    def shape(tile, _):
        cols = tile_lanes(tile)
        scale = scale_buf[:, cols]
        scale = jnp.concatenate([scale, scale], axis=0)
        skip = skip_ref[:, tile_lanes(tile, first)]
        for row in range(0, half, 16):
            low = [value * scale for value in unfolded(spec_buf, row, cols)]
            high = [value * scale for value in unfolded(spec_buf, row, tile_lanes(tile, width))]
            sign = 1 if row < half // 2 else -1
            turned = [-sign * low[1], sign * low[0], sign * low[3], -sign * low[2]]
            low = [low[0] + skip, low[1], low[2] + skip, low[3]]
            for at in range(4):
                near_ref[at * half + row : at * half + row + 16, cols] = low[at]
                far_ref[at * half + row : at * half + row + 16, cols] = high[at] + turned[at]

    each_tile(width // 128, 4, shape)


def own_kernel(
    first, send, projected_ref, rims_ref, taps_ref, near_ref, far_ref, forward_ref, backward_ref, *refs
):
    if send:
        base_ref, right_ref, mixed_ref, coded_ref, *bufs = refs
    else:
        *driven_refs, _, base_ref, right_ref, mixed_ref = refs[:6]
        bufs = refs[6:]
    rims_buf, strided_buf, parts_buf, spec_buf, bins_buf, mixed_buf, sems = bufs[:7]
    rows, width = base_ref.shape
    half = rows // 2
    tiles = width // 128
    read_rims(rims_ref, rims_buf)
    place = lax.axis_index("ctx")

    def sums_of(tile, number, ats):
        cols = tile_lanes(tile, first)
        sums = []
        for at in ats:
            parts = strided_rows(projected_ref[at, :, cols], strided_buf.at[number, at])
            sums.append(short_sum(parts, rims_buf[at, :, cols], taps_ref, at, cols))
        return sums

    def put_right(tile, values):
        for at, value in enumerate(parity_rows(values)):
            right_ref[16 * at : 16 * at + 16, tile_lanes(tile)] = value

    def drive(tile, number):
        sums = sums_of(tile, number, range(3))
        put_right(tile, sums[1])
        driven = [one * two for one, two in zip(sums[0], sums[2])]
        for at, value in enumerate(parity_rows(driven)):
            put_halves(parts_buf, 16 * at // half, 16 * at % half, tile_lanes(tile), value)

    if send:
        each_tile(tiles, strided_buf.shape[0], drive)
    else:

        @pl.when(place != 0)
        def _():
            each_tile(tiles, strided_buf.shape[0], drive)

        @pl.when(place == 0)
        def _():
            each_tile(tiles, strided_buf.shape[0], lambda tile, number: put_right(tile, sums_of(tile, number, [1])[0]))
            start = 0
            for ref in driven_refs:

                def recall(tile, _, ref=ref, start=start):
                    for row in range(0, rows, 16):
                        value = ref[row : row + 16, tile_lanes(tile)]
                        put_halves(parts_buf, row // half, row % half, tile_lanes(tile, start), value)

                each_tile(ref.shape[1] // 128, 4, recall)
                start += ref.shape[1]

    forward_dots(forward_ref, parts_buf, spec_buf)
    if send:
        conv_buf, peak_buf, levels_buf = bufs[7:]

        @pl.when(place == 0)
        def _():
            each_tile(
                tiles, 4,
                lambda tile, _: filtered(spec_buf, far_ref, bins_buf, tile_lanes(tile), tile_lanes(tile)),
            )
            backward_dots(backward_ref, bins_buf, conv_buf)

            def peaks(tile, _):
                cols = tile_lanes(tile)
                peak_buf[:, cols] = functools.reduce(
                    jnp.maximum, [jnp.abs(conv_buf[row : row + 8, cols]) for row in range(0, rows, 8)]
                )

            each_tile(tiles, 4, peaks)
            code_tiles(tiles, rows, coded_ref, conv_buf, peak_buf, levels_buf)

    each_tile(
        tiles, 4, lambda tile, _: filtered(spec_buf, near_ref, bins_buf, tile_lanes(tile), tile_lanes(tile))
    )
    backward_dots(backward_ref, bins_buf, base_ref)

    @pl.when(place == 0)
    def _():
        def mix(tile):
            cols = tile_lanes(tile)
            return [right_ref[at : at + 16, cols] * base_ref[at : at + 16, cols] for at in range(0, rows, 16)]

        mix_out(mix, tiles, first, mixed_ref, mixed_buf, strided_buf.at[:, 0], sems)


def mix_out(mix, tiles, first, mixed_ref, buf, strided_buf, sems):
    parts = sems.shape[0]
    copies = []
    for part in range(parts):
        start, count = part * (tiles // parts), tiles // parts

        def one(tile, number, start=start):
            buf[:, tile_lanes(start + tile)] = natural_rows(mix(start + tile), strided_buf.at[number]).astype(jnp.bfloat16)

        each_tile(count, strided_buf.shape[0], one)
        span = slice(start * 128, (start + count) * 128)
        copy = pltpu.make_async_copy(
            buf.at[:, span], mixed_ref.at[:, pl.ds(first + start * 128, count * 128)], sems.at[part]
        )
        copy.start()
        copies.append(copy)
    for copy in copies:
        copy.wait()


def read_levels(coded_ref, levels_buf, tiles, rows):
    levels_buf[...] = coded_ref[tiles * rows : tiles * rows + 16].astype(jnp.float32)


def join_kernel(
    coded_refs, far_ref, base_ref, right_ref, forward_ref, backward_ref, mixed_ref,
    parts_buf, spec_buf, bins_buf, conv_buf, strided_buf, buf, levels_buf, sems,
):
    rows, width = conv_buf.shape
    half = rows // 2
    tiles = width // 128

    @pl.when(lax.axis_index("ctx") != 0)
    def _():
        counts = [coded_refs[0].shape[0] // rows, coded_refs[1].shape[0] // rows]
        counts[0] = tiles - counts[1]
        for at, ref in enumerate(coded_refs):
            start = counts[0] * 128 * at
            read_levels(ref, levels_buf.at[at], counts[at], rows)

            def spread_out(tile, _, ref=ref, at=at, start=start):
                decode = decoder(levels_buf.at[at], tile)
                for row in range(0, rows, 16):
                    value = decode(ref[tile_rows(tile, row), :])
                    put_halves(parts_buf, row // half, row % half, tile_lanes(tile, start), value)

            each_tile(counts[at], 4, spread_out)
        forward_dots(forward_ref, parts_buf, spec_buf)
        each_tile(
            tiles, 4, lambda tile, _: filtered(spec_buf, far_ref, bins_buf, tile_lanes(tile), tile_lanes(tile))
        )
        backward_dots(backward_ref, bins_buf, conv_buf)

        def mix(tile):
            cols = tile_lanes(tile)
            return [
                right_ref[at : at + 16, cols] * (conv_buf[at : at + 16, cols] + base_ref[at : at + 16, cols])
                for at in range(0, rows, 16)
            ]

        mix_out(mix, tiles, 0, mixed_ref, buf, strided_buf, sems)


def last_kernel(
    first, coded_ref, base_ref, right_ref, sofar_ref, mixed_ref, strided_buf, buf, levels_buf, sems
):
    rows, width = base_ref.shape
    tiles = width // 128

    @pl.when(lax.axis_index("ctx") != 0)
    def _():
        read_levels(coded_ref, levels_buf, tiles, rows)

        def mix(tile):
            cols = tile_lanes(tile)
            decode = decoder(levels_buf, tile)
            return [
                right_ref[at : at + 16, cols] * (decode(coded_ref[tile_rows(tile, at), :]) + base_ref[at : at + 16, cols])
                for at in range(0, rows, 16)
            ]

        mix_out(mix, tiles, first, mixed_ref, buf, strided_buf, sems)


def params(mib=40):
    return pltpu.CompilerParams(vmem_limit_bytes=mib * 1024 * 1024)


def cost(us):
    return pl.CostEstimate(flops=int(us * 1e9), bytes_accessed=int(us * 3e6), transcendentals=0)


def one_way(
    projected, short_weight, pos_in, pos_bias, sine_freq, pos_mid, pos_out, decay_rate, skip_gain
):
    _, rows, width = projected.shape
    half = rows // 2
    total_len = 2 * rows
    ahead = [width // 8, width * 5 // 8]
    middle = sum(ahead)
    behind = width - middle
    forward, backward = odd_tables(rows)
    taps = jnp.transpose(short_weight, (1, 0, 2))
    in_vmem = pl.BlockSpec(memory_space=pltpu.VMEM)
    in_hbm = pl.BlockSpec(memory_space=pltpu.HBM)
    floats, shorts = functools.partial(pltpu.VMEM, dtype=jnp.float32), functools.partial(pltpu.VMEM, dtype=jnp.bfloat16)
    pairs = [(0, 1)]

    def arrays(*shapes, dtype=jnp.float32):
        return [jax.ShapeDtypeStruct(shape, dtype) for shape in shapes]

    def message(size, more=0):
        return arrays((size // 128 * rows + 16 + more, 128), dtype=jnp.bfloat16)

    order = parity_order(rows)
    places = np.concatenate([order, order + rows]).astype(np.float32)
    feats = feature_table(places, total_len)
    places = np.repeat(places[:, None], 128, 1)
    layers = (feats, pos_in, pos_bias[None, :], sine_freq[None, :], pos_mid)
    tile_bufs = [floats((2, 2, rows, 128)), floats((8, width)), floats((16, 128))]
    one, two = ahead
    one_code, one_driven = pl.pallas_call(
        first_kernel,
        in_specs=[in_hbm] * 2,
        out_specs=[in_vmem] * 2,
        out_shape=message(one, width // 128 * 18) + arrays((rows, one)),
        scratch_shapes=[shorts((2, rows, one)), shorts((3, 16, width)), floats((3, TAPS, one))]
        + tile_bufs
        + [pltpu.SemaphoreType.DMA((4,))],
        compiler_params=params(),
        cost_estimate=cost(1),
        name="first",
    )(*[pltpu.with_memory_space_constraint(array, pltpu.HBM) for array in (projected, taps)])
    one_code = lax.ppermute(one_code, "ctx", [(0, 1), (1, 0)])
    two_code, two_driven = pl.pallas_call(
        functools.partial(encode_kernel, one),
        in_specs=[in_vmem] * 2,
        out_specs=[in_vmem] * 2,
        out_shape=message(two) + arrays((rows, two)),
        scratch_shapes=tile_bufs,
        compiler_params=params(),
        cost_estimate=cost(1),
        name="encode",
    )(projected, taps)
    two_code = lax.ppermute(two_code, "ctx", [(0, 1), (1, 0)])

    def spectra(first, size, *more):
        fresh = len(more) > 1
        return pl.pallas_call(
            functools.partial(filter_kernel, first, fresh),
            in_specs=[in_vmem] * (5 + len(more)),
            out_specs=[in_vmem] * (2 + fresh),
            out_shape=arrays((total_len, size), (total_len, size))
            + arrays((total_len, 3 * pos_mid.shape[1]), dtype=jnp.bfloat16) * fresh,
            scratch_shapes=[
                floats((total_len, size)),
                shorts((2, rows, 2 * size)),
                floats((2, rows, 2 * size)),
                floats((8, size)),
            ]
            + [floats((feats.shape[0], pos_in.shape[1]))] * fresh,
            compiler_params=params(),
            cost_estimate=cost(2),
            name="filter",
        )(pos_out, decay_rate[None, :], skip_gain[None, :], places, forward, *more)

    last_near, last_far, second_halves = spectra(middle, behind, *layers)

    def own(first, size, send, near, far, *more):
        return pl.pallas_call(
            functools.partial(own_kernel, first, send),
            in_specs=[in_vmem] * 7 + [in_vmem, in_vmem, in_hbm][: len(more)],
            out_specs=[in_vmem, in_vmem, in_hbm] + [in_vmem] * send,
            out_shape=arrays((rows, size), (rows, size))
            + arrays((rows, width), dtype=jnp.bfloat16)
            + message(size) * send,
            input_output_aliases={} if send else {9: 2},
            scratch_shapes=[
                floats((3, 8, width)),
                floats((2, 3, rows, 128)),
                shorts((2, rows, size)),
                floats((2, rows, size)),
                shorts((2, 2 * rows, size)),
                shorts((rows, size)),
                pltpu.SemaphoreType.DMA((2,)),
            ]
            + [floats((rows, size)), floats((8, size)), floats((16, 128))] * send,
            compiler_params=params(),
            cost_estimate=cost(2),
            name="own",
        )(projected, one_code, taps, near, far, forward, backward, *more)

    last_base, last_right, mixed, code = own(middle, behind, True, last_near, last_far)
    last_code = lax.ppermute(code, "ctx", pairs)
    near, far = spectra(0, middle, second_halves)
    base, right, mixed = own(0, middle, False, near, far, one_driven, two_driven, mixed)
    mixed = pl.pallas_call(
        lambda one_ref, two_ref, *refs: join_kernel((one_ref, two_ref), *refs[:5], *refs[6:]),
        in_specs=[in_vmem] * 7 + [in_hbm],
        out_specs=in_hbm,
        out_shape=jax.ShapeDtypeStruct((rows, width), jnp.bfloat16),
        input_output_aliases={7: 0},
        scratch_shapes=[
            shorts((2, rows, middle)),
            floats((2, rows, middle)),
            shorts((2, 2 * rows, middle)),
            floats((rows, middle)),
            floats((4, rows, 128)),
            shorts((rows, middle)),
            floats((2, 16, 128)),
            pltpu.SemaphoreType.DMA((3,)),
        ],
        compiler_params=params(),
        cost_estimate=cost(2),
        name="join",
    )(one_code, two_code, far, base, right, forward, backward, mixed)
    return pl.pallas_call(
        functools.partial(last_kernel, middle),
        in_specs=[in_vmem] * 3 + [in_hbm],
        out_specs=in_hbm,
        out_shape=jax.ShapeDtypeStruct((rows, width), jnp.bfloat16),
        input_output_aliases={3: 0},
        scratch_shapes=[
            floats((4, rows, 128)),
            shorts((rows, behind)),
            floats((16, 128)),
            pltpu.SemaphoreType.DMA((2,)),
        ],
        compiler_params=params(),
        cost_estimate=cost(1),
        name="last",
    )(last_code, last_base, last_right, mixed)


def turn_table(outer_ids, inner_ids, modulus):
    product_grid = outer_ids[:, None] * inner_ids[None, :] % modulus
    angles = product_grid.astype(jnp.float32) * (2.0 * math.pi / modulus)
    return (jnp.cos(angles), jnp.sin(angles))


def section_outer(table, data):
    return jnp.einsum(
        "ka,cab->ckb", table, data, precision=HIGHEST, preferred_element_type=jnp.float32
    )


def section_inner(table, data):
    return jnp.einsum(
        "ckb,bj->ckj", data, table, precision=HIGHEST, preferred_element_type=jnp.float32
    )


def padded_spectrum(signal, outer_count, inner_count, tables):
    cos_half, sin_half, cos_twist, sin_twist, cos_inner, sin_inner = tables
    shaped = signal.reshape(signal.shape[0], outer_count // 2, inner_count)
    real_one = section_outer(cos_half, shaped)
    imag_one = -section_outer(sin_half, shaped)
    real_two = real_one * cos_twist + imag_one * sin_twist
    imag_two = imag_one * cos_twist - real_one * sin_twist
    spec_real = section_inner(cos_inner, real_two) + section_inner(sin_inner, imag_two)
    spec_imag = section_inner(cos_inner, imag_two) - section_inner(sin_inner, real_two)
    return (spec_real, spec_imag)


def causal_local(driven_cols, normed_cols, total_len):
    full_len = 2 * total_len
    inner_count = math.gcd(total_len, 128)
    outer_count = full_len // inner_count
    outer_full = jnp.arange(outer_count, dtype=jnp.int32)
    outer_half = jnp.arange(outer_count // 2, dtype=jnp.int32)
    inner_ids = jnp.arange(inner_count, dtype=jnp.int32)
    cos_half, sin_half = turn_table(outer_full, outer_half, outer_count)
    cos_twist, sin_twist = turn_table(outer_full, inner_ids, full_len)
    cos_inner, sin_inner = turn_table(inner_ids, inner_ids, inner_count)
    tables = (cos_half, sin_half, cos_twist, sin_twist, cos_inner, sin_inner)
    sig_real, sig_imag = padded_spectrum(driven_cols, outer_count, inner_count, tables)
    fil_real, fil_imag = padded_spectrum(normed_cols, outer_count, inner_count, tables)
    prod_real = sig_real * fil_real - sig_imag * fil_imag
    prod_imag = sig_real * fil_imag + sig_imag * fil_real
    back_real = section_inner(cos_inner, prod_real) - section_inner(sin_inner, prod_imag)
    back_imag = section_inner(sin_inner, prod_real) + section_inner(cos_inner, prod_imag)
    turned_real = back_real * cos_twist - back_imag * sin_twist
    turned_imag = back_real * sin_twist + back_imag * cos_twist
    cos_last, sin_last = turn_table(outer_half, outer_full, outer_count)
    result = (
        section_outer(cos_last, turned_real) - section_outer(sin_last, turned_imag)
    ) / full_len
    return result.reshape(driven_cols.shape[0], total_len)


def exchanged(
    projected, short_weight, pos_in, pos_bias, sine_freq, pos_mid, pos_out, decay_rate, skip_gain
):
    ctx_count = lax.axis_size("ctx")
    ctx_place = lax.axis_index("ctx")
    block_rows = projected.shape[1]
    total_len = block_rows * ctx_count
    rim_rows = shifted(projected[:, block_rows - (TAPS - 1) :, :], "ctx", 1)
    extended = jnp.concatenate([rim_rows, projected], axis=1)
    short_out = jnp.zeros(projected.shape, jnp.float32)
    for tap_index in range(TAPS):
        offset = TAPS - 1 - tap_index
        short_out = short_out + short_weight[tap_index][:, None, :] * extended[
            :, offset : offset + block_rows, :
        ].astype(jnp.float32)
    left_gate, right_gate, value_stream = (short_out[0], short_out[1], short_out[2])
    driven = left_gate * value_stream
    own_width = driven.shape[1] // ctx_count
    driven_cols = lax.all_to_all(driven.T, "ctx", split_axis=0, concat_axis=1, tiled=True)
    own_out = lax.dynamic_slice_in_dim(pos_out, ctx_place * own_width, own_width, 1)
    own_decay = lax.dynamic_slice_in_dim(decay_rate, ctx_place * own_width, own_width, 0)
    positions = jnp.arange(total_len, dtype=jnp.int32).astype(jnp.float32)
    long_filter = filter_rows(
        positions, total_len, pos_in, pos_bias, sine_freq, pos_mid, own_out, own_decay
    )
    normed = long_filter / jnp.sqrt(jnp.sum(long_filter * long_filter, axis=0) + 1e-05)
    conv_cols = causal_local(driven_cols, normed.T, total_len)
    long_conv = lax.all_to_all(conv_cols, "ctx", split_axis=1, concat_axis=0, tiled=True).T
    return (right_gate * (long_conv + skip_gain[None, :] * driven)).astype(jnp.bfloat16)


def body(projected, *others):
    if lax.axis_size("ctx") == 2:
        return one_way(projected, *others)
    return exchanged(projected, *others)


def solution(mesh):
    placed = (
        P(None, ("dp", "ctx"), "chan"),
        P(None, None, "chan"),
        P(),
        P(),
        P(),
        P(),
        P(None, "chan"),
        P("chan"),
        P("chan"),
    )
    return jax.shard_map(
        body, mesh=mesh, in_specs=placed, out_specs=P(("dp", "ctx"), "chan"), check_vma=False
    )
```

```python
import functools
import math

import jax
import jax.numpy as jnp
import numpy as np
from jax import lax
from jax.experimental import pallas as pl
from jax.experimental.pallas import tpu as pltpu
from jax.sharding import PartitionSpec as P

BANDS = 16
TAPS = 7
SPAN = 250.0
TINY = 1e-30

HIGHEST = lax.Precision.HIGHEST


def shifted(x, axis, by):
    size = lax.axis_size(axis)
    pairs = [(i, i + by) for i in range(size) if 0 <= i + by < size]
    return lax.ppermute(x, axis, pairs)


def features(positions, total_len):
    band_ids = jnp.arange(1, BANDS + 1, dtype=jnp.float32)
    angles = positions[:, None] * band_ids[None, :] * (2.0 * math.pi / total_len)
    return jnp.concatenate(
        [positions[:, None] / total_len, jnp.cos(angles), jnp.sin(angles)], axis=1
    )


def second_rows(positions, total_len, pos_in, pos_bias, sine_freq, pos_mid):
    inputs = features(positions, total_len)
    first_layer = jnp.sin(
        sine_freq
        * (
            jnp.dot(inputs, pos_in, precision=HIGHEST, preferred_element_type=jnp.float32)
            + pos_bias
        )
    )
    return jnp.sin(
        sine_freq
        * jnp.dot(first_layer, pos_mid, precision=HIGHEST, preferred_element_type=jnp.float32)
    )


def filter_rows(positions, total_len, pos_in, pos_bias, sine_freq, pos_mid, pos_out, decay_rate):
    second_layer = second_rows(positions, total_len, pos_in, pos_bias, sine_freq, pos_mid)
    raw_filter = jnp.dot(
        second_layer, pos_out, precision=HIGHEST, preferred_element_type=jnp.float32
    )
    return raw_filter * jnp.exp(-decay_rate[None, :] * positions[:, None])


def halves(x):
    high = x.astype(jnp.bfloat16)
    low = (x - high.astype(jnp.float32)).astype(jnp.bfloat16)
    return high, low


def feature_table(places, total_len):
    bands = np.arange(1, BANDS + 1, dtype=np.float32)
    angles = places[:, None] * bands[None, :] * np.float32(2.0 * math.pi / total_len)
    first = places[:, None] / np.float32(total_len)
    table = np.concatenate([first, np.cos(angles), np.sin(angles), np.ones_like(first)], axis=1)
    spare = np.zeros((places.shape[0], -table.shape[1] % 8))
    return np.concatenate([table, spare], axis=1).astype(np.float32).T.copy()


def parity_order(rows):
    place = np.arange(rows)
    parity, inner = place // (rows // 2), place % (rows // 2)
    return rows // 8 * (inner % 8) + inner // 8 * 2 + parity


def table_columns(table):
    high = table.astype(jnp.bfloat16)
    low = (table - high.astype(np.float32)).astype(jnp.bfloat16)
    return np.concatenate([high, high, low], axis=1)


def odd_tables(rows):
    half = rows // 2
    order = np.concatenate([np.arange(0, half, 2), np.arange(1, half, 2)])
    turns = (2 * order[:, None] + 1) * parity_order(rows)[None, :] % (4 * rows)
    angles = turns * (np.pi / (2 * rows))
    forward = np.concatenate([np.cos(angles), -np.sin(angles)], axis=0).astype(np.float32)
    pieces = [forward[:, :half], forward[:, half:]]
    return (
        np.concatenate([table_columns(piece) for piece in pieces], axis=0),
        np.concatenate([table_columns(piece.T / np.float32(rows)) for piece in pieces], axis=0),
    )


def each_tile(tiles, unroll, action):
    count = math.gcd(tiles, unroll)

    def step(at, _):
        for number in range(count):
            action(at * count + number, number)
        return 0

    if tiles == count:
        step(0, 0)
    else:
        lax.fori_loop(0, tiles // count, step, 0)


def put_halves(ref, parity, row, cols, value):
    size = ref.shape[1] // 2
    high, low = halves(value)
    count = value.shape[0]
    ref[parity, row : row + count, cols] = high
    ref[parity, size + row : size + row + count, cols] = low


def three_pass(table, ref, parity):
    size = ref.shape[1] // 2
    both = jnp.concatenate([ref[parity], ref[parity, :size]], axis=0)
    return jnp.dot(table, both, preferred_element_type=jnp.float32)


def forward_dots(forward_ref, parts_ref, spec_ref):
    rows = spec_ref.shape[1]
    for parity in range(2):
        spec_ref[parity] = three_pass(forward_ref[parity * rows : (parity + 1) * rows], parts_ref, parity)


def backward_dots(backward_ref, bins_ref, conv_ref):
    half = conv_ref.shape[0] // 2
    for parity in range(2):
        rows = slice(parity * half, (parity + 1) * half)
        conv_ref[rows] = three_pass(backward_ref[rows], bins_ref, parity)


def unfolded(spec_ref, row, cols):
    half = spec_ref.shape[1] // 2
    even_cos, odd_cos = spec_ref[0, row : row + 16, cols], spec_ref[1, row : row + 16, cols]
    sine = slice(half + row, half + row + 16)
    even_sin, odd_sin = spec_ref[0, sine, cols], spec_ref[1, sine, cols]
    return even_cos + odd_cos, even_sin + odd_sin, even_cos - odd_cos, odd_sin - even_sin


def folded_products(spec_ref, filter_ref, row, cols, filter_cols):
    half = spec_ref.shape[1] // 2
    real, imag, real_far, imag_far = unfolded(spec_ref, row, cols)
    taps = [filter_ref[at * half + row : at * half + row + 16, filter_cols] for at in range(4)]
    out_real, out_imag = real * taps[0] - imag * taps[1], real * taps[1] + imag * taps[0]
    far_real = real_far * taps[2] - imag_far * taps[3]
    far_imag = real_far * taps[3] + imag_far * taps[2]
    return out_real + far_real, out_imag - far_imag, out_real - far_real, out_imag + far_imag


def put_bins(bins_ref, row, cols, products):
    half = bins_ref.shape[1] // 4
    for at, value in enumerate(products):
        put_halves(bins_ref, at // 2, at % 2 * half + row, cols, value)


def filtered(spec_ref, filter_ref, bins_ref, cols, filter_cols):
    for row in range(0, spec_ref.shape[1] // 2, 16):
        put_bins(bins_ref, row, cols, folded_products(spec_ref, filter_ref, row, cols, filter_cols))


def strided_rows(values, buf):
    buf[...] = values.astype(jnp.float32)
    count = buf.shape[0] // 8
    return [buf[pl.ds(v, 8, stride=count), :] for v in range(count)]


def short_sum(parts, rim, taps_ref, at, cols):
    top = lax.broadcasted_iota(jnp.int32, (8, 128), 0) == 0
    before = {}
    for back in range(1, TAPS):
        edge = 0.0 if rim is None else rim[8 - back : 9 - back]
        before[-back] = jnp.where(top, edge, pltpu.roll(parts[-back], 1, 0))
    taps = [jnp.broadcast_to(taps_ref[at, k : k + 1, cols], (8, 128)) for k in range(TAPS)]
    sums = []
    for v in range(len(parts)):
        terms = [taps[k] * (parts[v - k] if v >= k else before[v - k]) for k in range(TAPS)]
        sums.append(((terms[0] + terms[1]) + (terms[2] + terms[3])) + ((terms[4] + terms[5]) + terms[6]))
    return sums


def parity_rows(parts):
    ordered = parts[0::2] + parts[1::2]
    return [jnp.concatenate(ordered[i : i + 2], axis=0) for i in range(0, len(ordered), 2)]


def natural_rows(ref_rows, buf):
    count = buf.shape[0] // 8
    for at, value in enumerate(ref_rows):
        for piece in range(2):
            number = 2 * at + piece
            v = number % (count // 2) * 2 + number // (count // 2)
            buf[pl.ds(v, 8, stride=count), :] = value[8 * piece : 8 * piece + 8]
    return buf[...]


def tile_lanes(tile, first=0):
    return pl.ds(pl.multiple_of(first + tile * 128, 128), 128)


def tile_rows(tile, row, count=16):
    return pl.ds(pl.multiple_of(tile * 128 + row, 16), count)


def place_level(peak, tile, peak_buf, levels_buf):
    for step in (1, 2, 4):
        peak = jnp.maximum(peak, pltpu.roll(peak, step, 0))
    level = jnp.maximum(peak, TINY)
    wide = level * 65537.0
    level = wide - (wide - level)
    peak_buf[:, tile_lanes(tile)] = SPAN / level
    levels_buf[pl.ds(tile, 1), :] = level[0:1]


def put_coded(coded_ref, tile, row, value, gain):
    coded = jnp.exp2(jnp.abs(value) * gain - SPAN / 2)
    coded_ref[tile_rows(tile, row), :] = jnp.where(value < 0, -coded, coded).astype(jnp.bfloat16)


def decoder(levels_buf, tile):
    level = levels_buf[pl.ds(tile, 1), :]
    slope = jnp.broadcast_to(level * (1.0 / (math.log(2.0) * SPAN)), (16, 128))
    middle = jnp.broadcast_to(level / 2, (16, 128))

    def decode(coded):
        coded = coded.astype(jnp.float32)
        size = jnp.log(jnp.abs(coded)) * slope + middle
        return jnp.where(coded < 0, -size, size)

    return decode


def second_layer(feats_ref, in_ref, bias_ref, freq_ref, mid_ref, scaled_buf):
    dot = functools.partial(
        lax.dot_general,
        dimension_numbers=(((0,), (0,)), ((), ())),
        precision=HIGHEST,
        preferred_element_type=jnp.float32,
    )
    count = in_ref.shape[0]
    freq = freq_ref[...]
    scaled_buf[...] = jnp.zeros_like(scaled_buf)
    scaled_buf[0:count] = in_ref[...] * freq
    scaled_buf[count : count + 1] = bias_ref[...] * freq
    layer = jnp.sin(dot(scaled_buf[...], feats_ref[...]))
    return jnp.sin(dot(mid_ref[...] * freq, layer)).T


def encode_tiles(tiles, rows, streams, taps_ref, taps_first, coded_ref, driven_ref, strided_buf, peak_buf, levels_buf):
    def drive(tile, number):
        cols = tile_lanes(tile)
        sums = [
            short_sum(
                strided_rows(streams(way, tile), strided_buf.at[number, way]),
                None, taps_ref, 2 * way, tile_lanes(tile, taps_first),
            )
            for way in range(2)
        ]
        driven = [one * two for one, two in zip(*sums)]
        for row, value in enumerate(parity_rows(driven)):
            driven_ref[16 * row : 16 * row + 16, cols] = value
        peak_buf[:, cols] = functools.reduce(jnp.maximum, [jnp.abs(value) for value in driven])

    each_tile(tiles, strided_buf.shape[0], drive)
    code_tiles(tiles, rows, coded_ref, driven_ref, peak_buf, levels_buf)


def code_tiles(tiles, rows, coded_ref, values_ref, peak_buf, levels_buf):
    each_tile(tiles, 4, lambda tile, _: place_level(peak_buf[:, tile_lanes(tile)], tile, peak_buf, levels_buf))
    coded_ref[tiles * rows : tiles * rows + 16] = levels_buf[...].astype(jnp.bfloat16)

    def code(tile, _):
        cols = tile_lanes(tile)
        gain = peak_buf[:, cols]
        gain = jnp.concatenate([gain, gain], axis=0)
        for row in range(0, rows, 16):
            put_coded(coded_ref, tile, row, values_ref[row : row + 16, cols], gain)

    each_tile(tiles, 4, code)


def first_kernel(
    projected_ref, taps_ref, coded_ref, driven_ref, rows_buf, rim_buf, taps_buf, strided_buf, peak_buf, levels_buf, sems
):
    rows, size = rows_buf.shape[1:]
    tiles = size // 128

    @pl.when(lax.axis_index("ctx") == 0)
    def _():
        span = pl.ds(0, size)
        copies = [
            pltpu.make_async_copy(taps_ref.at[:, :, span], taps_buf, sems.at[0]),
            pltpu.make_async_copy(projected_ref.at[0, :, span], rows_buf.at[0], sems.at[1]),
            pltpu.make_async_copy(projected_ref.at[2, :, span], rows_buf.at[1], sems.at[2]),
            pltpu.make_async_copy(projected_ref.at[:, pl.ds(rows - 16, 16)], rim_buf, sems.at[3]),
        ]
        for copy in copies:
            copy.start()
        for copy in copies:
            copy.wait()
        encode_tiles(
            tiles, rows, lambda way, tile: rows_buf[way, :, tile_lanes(tile)], taps_buf, 0, coded_ref, driven_ref,
            strided_buf, peak_buf, levels_buf,
        )

        for at in range(3):
            for group in range(rim_buf.shape[2] // 1024):
                there = tiles * rows + 16 + (3 * group + at) * 48
                values = [
                    rim_buf[at, :, (8 * group + way) * 128 : (8 * group + way + 1) * 128].astype(jnp.float32)[8:]
                    for way in range(8)
                ]
                values = pack_rims(values)
                for pair in range(3):
                    both = jnp.concatenate(values[2 * pair : 2 * pair + 2], axis=0)
                    coded_ref[there + 16 * pair : there + 16 * pair + 16] = both.astype(jnp.bfloat16)


def pack_rims(values):
    top = lax.broadcasted_iota(jnp.int32, (8, 128), 0) < 2
    return [
        jnp.where(top, pltpu.roll(values[6 + at // 3], 6 - 2 * (at % 3), 0), values[at]) for at in range(6)
    ]


def unpack_rims(values):
    place = lax.broadcasted_iota(jnp.int32, (8, 128), 0)
    rest = []
    for at in range(2):
        turned = [pltpu.roll(values[3 * at + way], 2 + 2 * way, 0) for way in range(3)]
        rest.append(jnp.where(place < 4, turned[0], jnp.where(place < 6, turned[1], turned[2])))
    return values + rest


def read_rims(coded_ref, rims_buf):
    groups = rims_buf.shape[2] // 1024
    start = coded_ref.shape[0] - groups * 144
    for at in range(3):
        for group in range(groups):
            there = start + (3 * group + at) * 48
            packed = coded_ref[there : there + 48].astype(jnp.float32)
            values = unpack_rims([packed[8 * way : 8 * way + 8] for way in range(6)])
            for way, value in enumerate(values):
                rims_buf[at, :, (8 * group + way) * 128 : (8 * group + way + 1) * 128] = value


def encode_kernel(
    first, projected_ref, taps_ref, coded_ref, driven_ref, strided_buf, peak_buf, levels_buf
):
    rows, size = driven_ref.shape

    @pl.when(lax.axis_index("ctx") == 0)
    def _():
        encode_tiles(
            size // 128, rows, lambda way, tile: projected_ref[2 * way, :, tile_lanes(tile, first)], taps_ref, first,
            coded_ref, driven_ref, strided_buf, peak_buf, levels_buf,
        )


def filter_kernel(first, fresh, out_ref, decay_ref, skip_ref, places_ref, forward_ref, *refs):
    if fresh:
        *layer_refs, near_ref, far_ref, halves_ref, raw_buf, parts_buf, spec_buf, scale_buf, scaled_buf = refs
        second_high, second_low = halves(second_layer(*layer_refs, scaled_buf))
        halves_ref[...] = jnp.concatenate([second_high, second_high, second_low], axis=1)
    else:
        halves_ref, near_ref, far_ref, raw_buf, parts_buf, spec_buf, scale_buf = refs
    rows, width = near_ref.shape[0] // 2, near_ref.shape[1]
    half = rows // 2
    out_high, out_low = halves(out_ref[:, first : first + width])
    raw_buf[...] = jnp.dot(
        halves_ref[...], jnp.concatenate([out_high, out_low, out_high], axis=0), preferred_element_type=jnp.float32
    )

    def decay(tile, _):
        cols = tile_lanes(tile)
        fall = -decay_ref[:, tile_lanes(tile, first)]
        total = jnp.zeros((8, 128), jnp.float32)
        for row in range(0, 2 * rows, 16):
            taps = raw_buf[row : row + 16, cols] * jnp.exp(fall * places_ref[row : row + 16])
            total = total + (taps[:8] * taps[:8] + taps[8:] * taps[8:])
            parity = row % rows // half
            put_halves(parts_buf, parity, row % half, tile_lanes(tile, row // rows * width), taps)
        for step in (1, 2, 4):
            total = total + pltpu.roll(total, step, 0)
        scale_buf[:, cols] = 1.0 / jnp.sqrt(total + 1e-05)

    each_tile(width // 128, 4, decay)
    forward_dots(forward_ref, parts_buf, spec_buf)

    def shape(tile, _):
        cols = tile_lanes(tile)
        scale = scale_buf[:, cols]
        scale = jnp.concatenate([scale, scale], axis=0)
        skip = skip_ref[:, tile_lanes(tile, first)]
        for row in range(0, half, 16):
            low = [value * scale for value in unfolded(spec_buf, row, cols)]
            high = [value * scale for value in unfolded(spec_buf, row, tile_lanes(tile, width))]
            sign = 1 if row < half // 2 else -1
            turned = [-sign * low[1], sign * low[0], sign * low[3], -sign * low[2]]
            low = [low[0] + skip, low[1], low[2] + skip, low[3]]
            for at in range(4):
                near_ref[at * half + row : at * half + row + 16, cols] = low[at]
                far_ref[at * half + row : at * half + row + 16, cols] = high[at] + turned[at]

    each_tile(width // 128, 4, shape)


def driven_parts(driven, parts_buf, cols):
    half = parts_buf.shape[1] // 2
    for at, value in enumerate(parity_rows(driven)):
        put_halves(parts_buf, 16 * at // half, 16 * at % half, cols, value)


def put_rows(ref, cols, values):
    for at, value in enumerate(parity_rows(values)):
        ref[16 * at : 16 * at + 16, cols] = value


def send_kernel(
    first, projected_ref, taps_ref, near_ref, far_ref, forward_ref, backward_ref, coded_ref, mixed_ref, gates_ref,
    strided_buf, parts_buf, spec_buf, bins_buf, right_buf, conv_buf, peak_buf, levels_buf, mixed_buf, sems,
):
    rows, width = right_buf.shape
    tiles = width // 128

    @pl.when(lax.axis_index("ctx") == 0)
    def _():
        def drive(tile, number):
            cols = tile_lanes(tile, first)
            sums = [
                short_sum(
                    strided_rows(projected_ref[at, :, cols], strided_buf.at[number, at]), None, taps_ref, at, cols
                )
                for at in range(3)
            ]
            put_rows(right_buf, tile_lanes(tile), sums[1])
            driven_parts([one * two for one, two in zip(sums[0], sums[2])], parts_buf, tile_lanes(tile))

        each_tile(tiles, strided_buf.shape[0], drive)
        forward_dots(forward_ref, parts_buf, spec_buf)
        each_tile(
            tiles, 4, lambda tile, _: filtered(spec_buf, far_ref, bins_buf, tile_lanes(tile), tile_lanes(tile))
        )
        backward_dots(backward_ref, bins_buf, conv_buf)

        def peaks(tile, _):
            cols = tile_lanes(tile)
            peak_buf[:, cols] = functools.reduce(
                jnp.maximum, [jnp.abs(conv_buf[row : row + 8, cols]) for row in range(0, rows, 8)]
            )

        each_tile(tiles, 4, peaks)
        code_tiles(tiles, rows, coded_ref, conv_buf, peak_buf, levels_buf)
        each_tile(
            tiles, 4, lambda tile, _: filtered(spec_buf, near_ref, bins_buf, tile_lanes(tile), tile_lanes(tile))
        )
        backward_dots(backward_ref, bins_buf, conv_buf)

        def mix(tile):
            cols = tile_lanes(tile)
            return [right_buf[at : at + 16, cols] * conv_buf[at : at + 16, cols] for at in range(0, rows, 16)]

        def gate(tile, number):
            cols = tile_lanes(tile)
            parts = strided_rows(projected_ref[1, :, cols], strided_buf.at[number, 1])
            put_rows(gates_ref, cols, short_sum(parts, None, taps_ref, 1, cols))

        each_tile(first // 128, strided_buf.shape[0], gate)
        mix_out(mix, tiles, first, mixed_ref, mixed_buf, strided_buf.at[:, 0], sems)


def own_kernel(
    projected_ref, rims_ref, taps_ref, near_ref, last_near_ref, forward_ref, backward_ref, one_ref, two_ref, gates_ref,
    _, right_ref, bins_ref, base_ref, mixed_ref,
    rims_buf, strided_buf, parts_buf, spec_buf, bins_buf, conv_buf, mixed_buf, sems,
):
    rows, width = right_ref.shape
    half = rows // 2
    middle = near_ref.shape[1]
    place = lax.axis_index("ctx")

    @pl.when(place == 0)
    def _():
        tiles = middle // 128
        start = 0
        for ref in (one_ref, two_ref):

            def recall(tile, _, ref=ref, start=start):
                for row in range(0, rows, 16):
                    value = ref[row : row + 16, tile_lanes(tile)]
                    put_halves(parts_buf, row // half, row % half, tile_lanes(tile, start), value)

            each_tile(ref.shape[1] // 128, 4, recall)
            start += ref.shape[1]
        forward_dots(forward_ref, parts_buf.at[:, :, 0:middle], spec_buf.at[:, :, 0:middle])
        each_tile(
            tiles, 4, lambda tile, _: filtered(spec_buf, near_ref, bins_buf, tile_lanes(tile), tile_lanes(tile))
        )
        backward_dots(backward_ref, bins_buf, conv_buf)

        def mix(tile):
            cols = tile_lanes(tile)
            return [gates_ref[at : at + 16, cols] * conv_buf[at : at + 16, cols] for at in range(0, rows, 16)]

        mix_out(mix, tiles, 0, mixed_ref, mixed_buf, strided_buf.at[:, 0], sems)

    @pl.when(place != 0)
    def _():
        read_rims(rims_ref, rims_buf)

        def drive(tile, number):
            cols = tile_lanes(tile)
            sums = [
                short_sum(
                    strided_rows(projected_ref[at, :, cols], strided_buf.at[number, at]),
                    rims_buf[at, :, cols], taps_ref, at, cols,
                )
                for at in range(3)
            ]
            put_rows(right_ref, cols, sums[1])
            driven_parts([one * two for one, two in zip(sums[0], sums[2])], parts_buf, cols)

        each_tile(width // 128, strided_buf.shape[0], drive)
        forward_dots(forward_ref, parts_buf, spec_buf)

        def keep(tile, _):
            cols = tile_lanes(tile)
            for row in range(0, half, 16):
                for at, value in enumerate(folded_products(spec_buf, near_ref, row, cols, cols)):
                    bins_ref[at * half + row : at * half + row + 16, cols] = value

        each_tile(middle // 128, 4, keep)
        behind = width - middle

        def finish(tile, _):
            there, cols = tile_lanes(tile, middle), tile_lanes(tile)
            for row in range(0, half, 16):
                put_bins(bins_buf, row, cols, folded_products(spec_buf, last_near_ref, row, there, cols))

        each_tile(behind // 128, 4, finish)
        backward_dots(backward_ref, bins_buf.at[:, :, 0:behind], base_ref)


def mix_out(mix, tiles, first, mixed_ref, buf, strided_buf, sems):
    parts = sems.shape[0]
    copies = []
    for part in range(parts):
        start, count = part * (tiles // parts), tiles // parts

        def one(tile, number, start=start):
            buf[:, tile_lanes(start + tile)] = natural_rows(mix(start + tile), strided_buf.at[number]).astype(jnp.bfloat16)

        each_tile(count, strided_buf.shape[0], one)
        span = slice(start * 128, (start + count) * 128)
        copy = pltpu.make_async_copy(
            buf.at[:, span], mixed_ref.at[:, pl.ds(first + start * 128, count * 128)], sems.at[part]
        )
        copy.start()
        copies.append(copy)
    for copy in copies:
        copy.wait()


def read_levels(coded_ref, levels_buf, tiles, rows):
    levels_buf[...] = coded_ref[tiles * rows : tiles * rows + 16].astype(jnp.float32)


def join_kernel(
    coded_refs, far_ref, own_bins_ref, right_ref, forward_ref, backward_ref, mixed_ref,
    parts_buf, spec_buf, bins_buf, conv_buf, strided_buf, buf, levels_buf, sems,
):
    rows, width = conv_buf.shape
    half = rows // 2
    tiles = width // 128

    @pl.when(lax.axis_index("ctx") != 0)
    def _():
        counts = [coded_refs[0].shape[0] // rows, coded_refs[1].shape[0] // rows]
        counts[0] = tiles - counts[1]
        for at, ref in enumerate(coded_refs):
            start = counts[0] * 128 * at
            read_levels(ref, levels_buf.at[at], counts[at], rows)

            def spread_out(tile, _, ref=ref, at=at, start=start):
                decode = decoder(levels_buf.at[at], tile)
                for row in range(0, rows, 16):
                    value = decode(ref[tile_rows(tile, row), :])
                    put_halves(parts_buf, row // half, row % half, tile_lanes(tile, start), value)

            each_tile(counts[at], 4, spread_out)
        forward_dots(forward_ref, parts_buf, spec_buf)

        def add(tile, _):
            cols = tile_lanes(tile)
            for row in range(0, half, 16):
                products = [
                    value + own_bins_ref[at * half + row : at * half + row + 16, cols]
                    for at, value in enumerate(folded_products(spec_buf, far_ref, row, cols, cols))
                ]
                put_bins(bins_buf, row, cols, products)

        each_tile(tiles, 4, add)
        backward_dots(backward_ref, bins_buf, conv_buf)

        def mix(tile):
            cols = tile_lanes(tile)
            return [right_ref[at : at + 16, cols] * conv_buf[at : at + 16, cols] for at in range(0, rows, 16)]

        mix_out(mix, tiles, 0, mixed_ref, buf, strided_buf, sems)


def last_kernel(
    first, coded_ref, base_ref, right_ref, sofar_ref, mixed_ref, strided_buf, buf, levels_buf, sems
):
    rows, width = base_ref.shape
    tiles = width // 128

    @pl.when(lax.axis_index("ctx") != 0)
    def _():
        read_levels(coded_ref, levels_buf, tiles, rows)

        def mix(tile):
            cols = tile_lanes(tile)
            decode = decoder(levels_buf, tile)
            return [
                right_ref[at : at + 16, tile_lanes(tile, first)] * (decode(coded_ref[tile_rows(tile, at), :]) + base_ref[at : at + 16, cols])
                for at in range(0, rows, 16)
            ]

        mix_out(mix, tiles, first, mixed_ref, buf, strided_buf, sems)


def params(mib=40):
    return pltpu.CompilerParams(vmem_limit_bytes=mib * 1024 * 1024)


def cost(us):
    return pl.CostEstimate(flops=int(us * 1e9), bytes_accessed=int(us * 3e6), transcendentals=0)


def one_way(
    projected, short_weight, pos_in, pos_bias, sine_freq, pos_mid, pos_out, decay_rate, skip_gain
):
    _, rows, width = projected.shape
    half = rows // 2
    total_len = 2 * rows
    ahead = [width // 8, width * 5 // 8]
    middle = sum(ahead)
    behind = width - middle
    forward, backward = odd_tables(rows)
    taps = jnp.transpose(short_weight, (1, 0, 2))
    in_vmem = pl.BlockSpec(memory_space=pltpu.VMEM)
    in_hbm = pl.BlockSpec(memory_space=pltpu.HBM)
    floats, shorts = functools.partial(pltpu.VMEM, dtype=jnp.float32), functools.partial(pltpu.VMEM, dtype=jnp.bfloat16)
    pairs = [(0, 1)]

    def arrays(*shapes, dtype=jnp.float32):
        return [jax.ShapeDtypeStruct(shape, dtype) for shape in shapes]

    def message(size, more=0):
        return arrays((size // 128 * rows + 16 + more, 128), dtype=jnp.bfloat16)

    order = parity_order(rows)
    places = np.concatenate([order, order + rows]).astype(np.float32)
    feats = feature_table(places, total_len)
    places = np.repeat(places[:, None], 128, 1)
    layers = (feats, pos_in, pos_bias[None, :], sine_freq[None, :], pos_mid)
    tile_bufs = [floats((2, 2, rows, 128)), floats((8, width)), floats((16, 128))]
    one, two = ahead
    one_code, one_driven = pl.pallas_call(
        first_kernel,
        in_specs=[in_hbm] * 2,
        out_specs=[in_vmem] * 2,
        out_shape=message(one, width // 128 * 18) + arrays((rows, one)),
        scratch_shapes=[shorts((2, rows, one)), shorts((3, 16, width)), floats((3, TAPS, one))]
        + tile_bufs
        + [pltpu.SemaphoreType.DMA((4,))],
        compiler_params=params(),
        cost_estimate=cost(1),
        name="first",
    )(*[pltpu.with_memory_space_constraint(array, pltpu.HBM) for array in (projected, taps)])
    one_code = lax.ppermute(one_code, "ctx", [(0, 1), (1, 0)])
    two_code, two_driven = pl.pallas_call(
        functools.partial(encode_kernel, one),
        in_specs=[in_vmem] * 2,
        out_specs=[in_vmem] * 2,
        out_shape=message(two) + arrays((rows, two)),
        scratch_shapes=tile_bufs,
        compiler_params=params(),
        cost_estimate=cost(1),
        name="encode",
    )(projected, taps)
    two_code = lax.ppermute(two_code, "ctx", [(0, 1), (1, 0)])

    def spectra(first, size, *more):
        fresh = len(more) > 1
        return pl.pallas_call(
            functools.partial(filter_kernel, first, fresh),
            in_specs=[in_vmem] * (5 + len(more)),
            out_specs=[in_vmem] * (2 + fresh),
            out_shape=arrays((total_len, size), (total_len, size))
            + arrays((total_len, 3 * pos_mid.shape[1]), dtype=jnp.bfloat16) * fresh,
            scratch_shapes=[
                floats((total_len, size)),
                shorts((2, rows, 2 * size)),
                floats((2, rows, 2 * size)),
                floats((8, size)),
            ]
            + [floats((feats.shape[0], pos_in.shape[1]))] * fresh,
            compiler_params=params(),
            cost_estimate=cost(2),
            name="filter",
        )(pos_out, decay_rate[None, :], skip_gain[None, :], places, forward, *more)

    last_near, last_far, second_halves = spectra(middle, behind, *layers)

    near, far = spectra(0, middle, second_halves)
    last_near, near = lax.optimization_barrier((last_near, near))
    last_code, mixed, gates = pl.pallas_call(
        functools.partial(send_kernel, middle),
        in_specs=[in_vmem] * 6,
        out_specs=[in_vmem, in_hbm, in_vmem],
        out_shape=message(behind) + arrays((rows, width), dtype=jnp.bfloat16) + arrays((rows, middle)),
        scratch_shapes=[
            floats((2, 3, rows, 128)),
            shorts((2, rows, behind)),
            floats((2, rows, behind)),
            shorts((2, 2 * rows, behind)),
            floats((rows, behind)),
            floats((rows, behind)),
            floats((8, behind)),
            floats((16, 128)),
            shorts((rows, behind)),
            pltpu.SemaphoreType.DMA((2,)),
        ],
        compiler_params=params(),
        cost_estimate=cost(2),
        name="send",
    )(projected, taps, last_near, last_far, forward, backward)
    last_code = lax.ppermute(last_code, "ctx", pairs)
    right, own_bins, last_base, mixed = pl.pallas_call(
        own_kernel,
        in_specs=[in_vmem] * 10 + [in_hbm],
        out_specs=[in_vmem] * 3 + [in_hbm],
        out_shape=arrays((rows, width), (total_len, middle), (rows, behind))
        + arrays((rows, width), dtype=jnp.bfloat16),
        input_output_aliases={10: 3},
        scratch_shapes=[
            floats((3, 8, width)),
            floats((2, 3, rows, 128)),
            shorts((2, rows, width)),
            floats((2, rows, width)),
            shorts((2, 2 * rows, middle)),
            floats((rows, middle)),
            shorts((rows, middle)),
            pltpu.SemaphoreType.DMA((2,)),
        ],
        compiler_params=params(),
        cost_estimate=cost(4),
        name="own",
    )(projected, one_code, taps, near, last_near, forward, backward, one_driven, two_driven, gates, mixed)
    mixed = pl.pallas_call(
        lambda one_ref, two_ref, *refs: join_kernel((one_ref, two_ref), *refs[:5], *refs[6:]),
        in_specs=[in_vmem] * 7 + [in_hbm],
        out_specs=in_hbm,
        out_shape=jax.ShapeDtypeStruct((rows, width), jnp.bfloat16),
        input_output_aliases={7: 0},
        scratch_shapes=[
            shorts((2, rows, middle)),
            floats((2, rows, middle)),
            shorts((2, 2 * rows, middle)),
            floats((rows, middle)),
            floats((4, rows, 128)),
            shorts((rows, middle)),
            floats((2, 16, 128)),
            pltpu.SemaphoreType.DMA((3,)),
        ],
        compiler_params=params(),
        cost_estimate=cost(2),
        name="join",
    )(one_code, two_code, far, own_bins, right, forward, backward, mixed)
    return pl.pallas_call(
        functools.partial(last_kernel, middle),
        in_specs=[in_vmem] * 3 + [in_hbm],
        out_specs=in_hbm,
        out_shape=jax.ShapeDtypeStruct((rows, width), jnp.bfloat16),
        input_output_aliases={3: 0},
        scratch_shapes=[
            floats((4, rows, 128)),
            shorts((rows, behind)),
            floats((16, 128)),
            pltpu.SemaphoreType.DMA((2,)),
        ],
        compiler_params=params(),
        cost_estimate=cost(1),
        name="last",
    )(last_code, last_base, right, mixed)


def turn_table(outer_ids, inner_ids, modulus):
    product_grid = outer_ids[:, None] * inner_ids[None, :] % modulus
    angles = product_grid.astype(jnp.float32) * (2.0 * math.pi / modulus)
    return (jnp.cos(angles), jnp.sin(angles))


def section_outer(table, data):
    return jnp.einsum(
        "ka,cab->ckb", table, data, precision=HIGHEST, preferred_element_type=jnp.float32
    )


def section_inner(table, data):
    return jnp.einsum(
        "ckb,bj->ckj", data, table, precision=HIGHEST, preferred_element_type=jnp.float32
    )


def padded_spectrum(signal, outer_count, inner_count, tables):
    cos_half, sin_half, cos_twist, sin_twist, cos_inner, sin_inner = tables
    shaped = signal.reshape(signal.shape[0], outer_count // 2, inner_count)
    real_one = section_outer(cos_half, shaped)
    imag_one = -section_outer(sin_half, shaped)
    real_two = real_one * cos_twist + imag_one * sin_twist
    imag_two = imag_one * cos_twist - real_one * sin_twist
    spec_real = section_inner(cos_inner, real_two) + section_inner(sin_inner, imag_two)
    spec_imag = section_inner(cos_inner, imag_two) - section_inner(sin_inner, real_two)
    return (spec_real, spec_imag)


def causal_local(driven_cols, normed_cols, total_len):
    full_len = 2 * total_len
    inner_count = math.gcd(total_len, 128)
    outer_count = full_len // inner_count
    outer_full = jnp.arange(outer_count, dtype=jnp.int32)
    outer_half = jnp.arange(outer_count // 2, dtype=jnp.int32)
    inner_ids = jnp.arange(inner_count, dtype=jnp.int32)
    cos_half, sin_half = turn_table(outer_full, outer_half, outer_count)
    cos_twist, sin_twist = turn_table(outer_full, inner_ids, full_len)
    cos_inner, sin_inner = turn_table(inner_ids, inner_ids, inner_count)
    tables = (cos_half, sin_half, cos_twist, sin_twist, cos_inner, sin_inner)
    sig_real, sig_imag = padded_spectrum(driven_cols, outer_count, inner_count, tables)
    fil_real, fil_imag = padded_spectrum(normed_cols, outer_count, inner_count, tables)
    prod_real = sig_real * fil_real - sig_imag * fil_imag
    prod_imag = sig_real * fil_imag + sig_imag * fil_real
    back_real = section_inner(cos_inner, prod_real) - section_inner(sin_inner, prod_imag)
    back_imag = section_inner(sin_inner, prod_real) + section_inner(cos_inner, prod_imag)
    turned_real = back_real * cos_twist - back_imag * sin_twist
    turned_imag = back_real * sin_twist + back_imag * cos_twist
    cos_last, sin_last = turn_table(outer_half, outer_full, outer_count)
    result = (
        section_outer(cos_last, turned_real) - section_outer(sin_last, turned_imag)
    ) / full_len
    return result.reshape(driven_cols.shape[0], total_len)


def exchanged(
    projected, short_weight, pos_in, pos_bias, sine_freq, pos_mid, pos_out, decay_rate, skip_gain
):
    ctx_count = lax.axis_size("ctx")
    ctx_place = lax.axis_index("ctx")
    block_rows = projected.shape[1]
    total_len = block_rows * ctx_count
    rim_rows = shifted(projected[:, block_rows - (TAPS - 1) :, :], "ctx", 1)
    extended = jnp.concatenate([rim_rows, projected], axis=1)
    short_out = jnp.zeros(projected.shape, jnp.float32)
    for tap_index in range(TAPS):
        offset = TAPS - 1 - tap_index
        short_out = short_out + short_weight[tap_index][:, None, :] * extended[
            :, offset : offset + block_rows, :
        ].astype(jnp.float32)
    left_gate, right_gate, value_stream = (short_out[0], short_out[1], short_out[2])
    driven = left_gate * value_stream
    own_width = driven.shape[1] // ctx_count
    driven_cols = lax.all_to_all(driven.T, "ctx", split_axis=0, concat_axis=1, tiled=True)
    own_out = lax.dynamic_slice_in_dim(pos_out, ctx_place * own_width, own_width, 1)
    own_decay = lax.dynamic_slice_in_dim(decay_rate, ctx_place * own_width, own_width, 0)
    positions = jnp.arange(total_len, dtype=jnp.int32).astype(jnp.float32)
    long_filter = filter_rows(
        positions, total_len, pos_in, pos_bias, sine_freq, pos_mid, own_out, own_decay
    )
    normed = long_filter / jnp.sqrt(jnp.sum(long_filter * long_filter, axis=0) + 1e-05)
    conv_cols = causal_local(driven_cols, normed.T, total_len)
    long_conv = lax.all_to_all(conv_cols, "ctx", split_axis=1, concat_axis=0, tiled=True).T
    return (right_gate * (long_conv + skip_gain[None, :] * driven)).astype(jnp.bfloat16)


def body(projected, *others):
    if lax.axis_size("ctx") == 2:
        return one_way(projected, *others)
    return exchanged(projected, *others)


def solution(mesh):
    placed = (
        P(None, ("dp", "ctx"), "chan"),
        P(None, None, "chan"),
        P(),
        P(),
        P(),
        P(),
        P(None, "chan"),
        P("chan"),
        P("chan"),
    )
    return jax.shard_map(
        body, mesh=mesh, in_specs=placed, out_specs=P(("dp", "ctx"), "chan"), check_vma=False
    )
```

```python
import functools
import math

import jax
import jax.numpy as jnp
import numpy as np
from jax import lax
from jax.experimental import pallas as pl
from jax.experimental.pallas import tpu as pltpu
from jax.sharding import PartitionSpec as P

BANDS = 16
TAPS = 7
SPAN = 250.0
TINY = 1e-30

HIGHEST = lax.Precision.HIGHEST


def shifted(x, axis, by):
    size = lax.axis_size(axis)
    pairs = [(i, i + by) for i in range(size) if 0 <= i + by < size]
    return lax.ppermute(x, axis, pairs)


def features(positions, total_len):
    band_ids = jnp.arange(1, BANDS + 1, dtype=jnp.float32)
    angles = positions[:, None] * band_ids[None, :] * (2.0 * math.pi / total_len)
    return jnp.concatenate(
        [positions[:, None] / total_len, jnp.cos(angles), jnp.sin(angles)], axis=1
    )


def second_rows(positions, total_len, pos_in, pos_bias, sine_freq, pos_mid):
    inputs = features(positions, total_len)
    first_layer = jnp.sin(
        sine_freq
        * (
            jnp.dot(inputs, pos_in, precision=HIGHEST, preferred_element_type=jnp.float32)
            + pos_bias
        )
    )
    return jnp.sin(
        sine_freq
        * jnp.dot(first_layer, pos_mid, precision=HIGHEST, preferred_element_type=jnp.float32)
    )


def filter_rows(positions, total_len, pos_in, pos_bias, sine_freq, pos_mid, pos_out, decay_rate):
    second_layer = second_rows(positions, total_len, pos_in, pos_bias, sine_freq, pos_mid)
    raw_filter = jnp.dot(
        second_layer, pos_out, precision=HIGHEST, preferred_element_type=jnp.float32
    )
    return raw_filter * jnp.exp(-decay_rate[None, :] * positions[:, None])


def halves(x):
    high = x.astype(jnp.bfloat16)
    low = (x - high.astype(jnp.float32)).astype(jnp.bfloat16)
    return high, low


def feature_table(places, total_len):
    bands = np.arange(1, BANDS + 1, dtype=np.float32)
    angles = places[:, None] * bands[None, :] * np.float32(2.0 * math.pi / total_len)
    first = places[:, None] / np.float32(total_len)
    table = np.concatenate([first, np.cos(angles), np.sin(angles), np.ones_like(first)], axis=1)
    spare = np.zeros((places.shape[0], -table.shape[1] % 8))
    return np.concatenate([table, spare], axis=1).astype(np.float32).T.copy()


def parity_order(rows):
    place = np.arange(rows)
    parity, inner = place // (rows // 2), place % (rows // 2)
    return rows // 8 * (inner % 8) + inner // 8 * 2 + parity


def table_columns(table):
    high = table.astype(jnp.bfloat16)
    low = (table - high.astype(np.float32)).astype(jnp.bfloat16)
    return np.concatenate([high, high, low], axis=1)


def odd_tables(rows):
    half = rows // 2
    order = np.concatenate([np.arange(0, half, 2), np.arange(1, half, 2)])
    turns = (2 * order[:, None] + 1) * parity_order(rows)[None, :] % (4 * rows)
    angles = turns * (np.pi / (2 * rows))
    forward = np.concatenate([np.cos(angles), -np.sin(angles)], axis=0).astype(np.float32)
    pieces = [forward[:, :half], forward[:, half:]]
    return (
        np.concatenate([table_columns(piece) for piece in pieces], axis=0),
        np.concatenate([table_columns(piece.T / np.float32(rows)) for piece in pieces], axis=0),
    )


def each_tile(tiles, unroll, action):
    count = math.gcd(tiles, unroll)

    def step(at, _):
        for number in range(count):
            action(at * count + number, number)
        return 0

    if tiles == count:
        step(0, 0)
    else:
        lax.fori_loop(0, tiles // count, step, 0)


def put_halves(ref, parity, row, cols, value):
    size = ref.shape[1] // 2
    high, low = halves(value)
    count = value.shape[0]
    ref[parity, row : row + count, cols] = high
    ref[parity, size + row : size + row + count, cols] = low


def three_pass(table, ref, parity):
    size = ref.shape[1] // 2
    both = jnp.concatenate([ref[parity], ref[parity, :size]], axis=0)
    return jnp.dot(table, both, preferred_element_type=jnp.float32)


def forward_dots(forward_ref, parts_ref, spec_ref):
    rows = spec_ref.shape[1]
    for parity in range(2):
        spec_ref[parity] = three_pass(forward_ref[parity * rows : (parity + 1) * rows], parts_ref, parity)


def backward_dots(backward_ref, bins_ref, conv_ref):
    half = conv_ref.shape[0] // 2
    for parity in range(2):
        rows = slice(parity * half, (parity + 1) * half)
        conv_ref[rows] = three_pass(backward_ref[rows], bins_ref, parity)


def unfolded(spec_ref, row, cols):
    half = spec_ref.shape[1] // 2
    even_cos, odd_cos = spec_ref[0, row : row + 16, cols], spec_ref[1, row : row + 16, cols]
    sine = slice(half + row, half + row + 16)
    even_sin, odd_sin = spec_ref[0, sine, cols], spec_ref[1, sine, cols]
    return even_cos + odd_cos, even_sin + odd_sin, even_cos - odd_cos, odd_sin - even_sin


def folded_products(spec_ref, filter_ref, row, cols, filter_cols):
    half = spec_ref.shape[1] // 2
    real, imag, real_far, imag_far = unfolded(spec_ref, row, cols)
    taps = [filter_ref[at * half + row : at * half + row + 16, filter_cols] for at in range(4)]
    out_real, out_imag = real * taps[0] - imag * taps[1], real * taps[1] + imag * taps[0]
    far_real = real_far * taps[2] - imag_far * taps[3]
    far_imag = real_far * taps[3] + imag_far * taps[2]
    return out_real + far_real, out_imag - far_imag, out_real - far_real, out_imag + far_imag


def put_bins(bins_ref, row, cols, products):
    half = bins_ref.shape[1] // 4
    for at, value in enumerate(products):
        put_halves(bins_ref, at // 2, at % 2 * half + row, cols, value)


def filtered(spec_ref, filter_ref, bins_ref, cols, filter_cols):
    for row in range(0, spec_ref.shape[1] // 2, 16):
        put_bins(bins_ref, row, cols, folded_products(spec_ref, filter_ref, row, cols, filter_cols))


def strided_rows(values, buf):
    buf[...] = values.astype(jnp.float32)
    count = buf.shape[0] // 8
    return [buf[pl.ds(v, 8, stride=count), :] for v in range(count)]


def short_sum(parts, rim, taps_ref, at, cols):
    top = lax.broadcasted_iota(jnp.int32, (8, 128), 0) == 0
    before = {}
    for back in range(1, TAPS):
        edge = 0.0 if rim is None else rim[8 - back : 9 - back]
        before[-back] = jnp.where(top, edge, pltpu.roll(parts[-back], 1, 0))
    taps = [jnp.broadcast_to(taps_ref[at, k : k + 1, cols], (8, 128)) for k in range(TAPS)]
    sums = []
    for v in range(len(parts)):
        terms = [taps[k] * (parts[v - k] if v >= k else before[v - k]) for k in range(TAPS)]
        sums.append(((terms[0] + terms[1]) + (terms[2] + terms[3])) + ((terms[4] + terms[5]) + terms[6]))
    return sums


def parity_rows(parts):
    ordered = parts[0::2] + parts[1::2]
    return [jnp.concatenate(ordered[i : i + 2], axis=0) for i in range(0, len(ordered), 2)]


def natural_rows(ref_rows, buf):
    count = buf.shape[0] // 8
    for at, value in enumerate(ref_rows):
        for piece in range(2):
            number = 2 * at + piece
            v = number % (count // 2) * 2 + number // (count // 2)
            buf[pl.ds(v, 8, stride=count), :] = value[8 * piece : 8 * piece + 8]
    return buf[...]


def tile_lanes(tile, first=0):
    return pl.ds(pl.multiple_of(first + tile * 128, 128), 128)


def tile_rows(tile, row, count=16):
    return pl.ds(pl.multiple_of(tile * 128 + row, 16), count)


def place_level(peak, tile, peak_buf, levels_buf, levels_first):
    for step in (1, 2, 4):
        peak = jnp.maximum(peak, pltpu.roll(peak, step, 0))
    level = jnp.maximum(peak, TINY)
    wide = level * 65537.0
    level = wide - (wide - level)
    peak_buf[:, tile_lanes(tile)] = SPAN / level
    levels_buf[pl.ds(levels_first + tile, 1), :] = level[0:1]


def put_coded(coded_ref, tile, row, value, gain):
    coded = jnp.exp2(jnp.abs(value) * gain - SPAN / 2)
    coded_ref[tile_rows(tile, row), :] = jnp.where(value < 0, -coded, coded).astype(jnp.bfloat16)


def decoder(levels_buf, tile):
    level = levels_buf[pl.ds(tile, 1), :]
    slope = jnp.broadcast_to(level * (1.0 / (math.log(2.0) * SPAN)), (16, 128))
    middle = jnp.broadcast_to(level / 2, (16, 128))

    def decode(coded):
        coded = coded.astype(jnp.float32)
        size = jnp.log(jnp.abs(coded)) * slope + middle
        return jnp.where(coded < 0, -size, size)

    return decode


def second_layer(feats_ref, in_ref, bias_ref, freq_ref, mid_ref, scaled_buf):
    dot = functools.partial(
        lax.dot_general,
        dimension_numbers=(((0,), (0,)), ((), ())),
        precision=HIGHEST,
        preferred_element_type=jnp.float32,
    )
    count = in_ref.shape[0]
    freq = freq_ref[...]
    scaled_buf[...] = jnp.zeros_like(scaled_buf)
    scaled_buf[0:count] = in_ref[...] * freq
    scaled_buf[count : count + 1] = bias_ref[...] * freq
    layer = jnp.sin(dot(scaled_buf[...], feats_ref[...]))
    return jnp.sin(dot(mid_ref[...] * freq, layer)).T


def encode_tiles(
    tiles, rows, streams, taps_ref, taps_first, coded_ref, driven_ref, strided_buf, peak_buf, levels_buf, levels_first=0
):
    def drive(tile, number):
        cols = tile_lanes(tile)
        sums = [
            short_sum(
                strided_rows(streams(way, tile), strided_buf.at[number, way]),
                None, taps_ref, 2 * way, tile_lanes(tile, taps_first),
            )
            for way in range(2)
        ]
        driven = [one * two for one, two in zip(*sums)]
        for row, value in enumerate(parity_rows(driven)):
            driven_ref[16 * row : 16 * row + 16, cols] = value
        peak_buf[:, cols] = functools.reduce(jnp.maximum, [jnp.abs(value) for value in driven])

    each_tile(tiles, strided_buf.shape[0], drive)
    code_tiles(tiles, rows, coded_ref, driven_ref, peak_buf, levels_buf, levels_first)


def code_tiles(tiles, rows, coded_ref, values_ref, peak_buf, levels_buf, levels_first=0):
    each_tile(
        tiles, 4,
        lambda tile, _: place_level(peak_buf[:, tile_lanes(tile)], tile, peak_buf, levels_buf, levels_first),
    )
    if levels_first == 0:
        coded_ref[tiles * rows : tiles * rows + 16] = levels_buf[...].astype(jnp.bfloat16)

    def code(tile, _):
        cols = tile_lanes(tile)
        gain = peak_buf[:, cols]
        gain = jnp.concatenate([gain, gain], axis=0)
        for row in range(0, rows, 16):
            put_coded(coded_ref, tile, row, values_ref[row : row + 16, cols], gain)

    each_tile(tiles, 4, code)


def first_kernel(
    projected_ref, taps_ref, coded_ref, driven_ref, levels_ref, rows_buf, rim_buf, taps_buf, strided_buf, peak_buf, sems
):
    rows, size = rows_buf.shape[1:]
    tiles = size // 128

    @pl.when(lax.axis_index("ctx") == 0)
    def _():
        span = pl.ds(0, size)
        copies = [
            pltpu.make_async_copy(taps_ref.at[:, :, span], taps_buf, sems.at[0]),
            pltpu.make_async_copy(projected_ref.at[0, :, span], rows_buf.at[0], sems.at[1]),
            pltpu.make_async_copy(projected_ref.at[2, :, span], rows_buf.at[1], sems.at[2]),
            pltpu.make_async_copy(projected_ref.at[:, pl.ds(rows - 16, 16)], rim_buf, sems.at[3]),
        ]
        for copy in copies:
            copy.start()
        for copy in copies[:3]:
            copy.wait()
        levels_ref[...] = jnp.zeros_like(levels_ref)
        encode_tiles(
            tiles, rows, lambda way, tile: rows_buf[way, :, tile_lanes(tile)], taps_buf, 0, coded_ref, driven_ref,
            strided_buf, peak_buf, levels_ref, 16 - tiles,
        )
        copies[3].wait()
        for at in range(3):
            for group in range(rim_buf.shape[2] // 1024):
                there = tiles * rows + (3 * group + at) * 48
                values = [
                    rim_buf[at, :, (8 * group + way) * 128 : (8 * group + way + 1) * 128].astype(jnp.float32)[8:]
                    for way in range(8)
                ]
                values = pack_rims(values)
                for pair in range(3):
                    both = jnp.concatenate(values[2 * pair : 2 * pair + 2], axis=0)
                    coded_ref[there + 16 * pair : there + 16 * pair + 16] = both.astype(jnp.bfloat16)


def pack_rims(values):
    top = lax.broadcasted_iota(jnp.int32, (8, 128), 0) < 2
    return [
        jnp.where(top, pltpu.roll(values[6 + at // 3], 6 - 2 * (at % 3), 0), values[at]) for at in range(6)
    ]


def unpack_rims(values):
    place = lax.broadcasted_iota(jnp.int32, (8, 128), 0)
    rest = []
    for at in range(2):
        turned = [pltpu.roll(values[3 * at + way], 2 + 2 * way, 0) for way in range(3)]
        rest.append(jnp.where(place < 4, turned[0], jnp.where(place < 6, turned[1], turned[2])))
    return values + rest


def read_rims(coded_ref, rims_buf):
    groups = rims_buf.shape[2] // 1024
    start = coded_ref.shape[0] - groups * 144
    for at in range(3):
        for group in range(groups):
            there = start + (3 * group + at) * 48
            packed = coded_ref[there : there + 48].astype(jnp.float32)
            values = unpack_rims([packed[8 * way : 8 * way + 8] for way in range(6)])
            for way, value in enumerate(values):
                rims_buf[at, :, (8 * group + way) * 128 : (8 * group + way + 1) * 128] = value


def encode_kernel(
    first, projected_ref, taps_ref, one_levels_ref, coded_ref, driven_ref, strided_buf, peak_buf, levels_buf
):
    rows, size = driven_ref.shape

    @pl.when(lax.axis_index("ctx") == 0)
    def _():
        levels_buf[...] = one_levels_ref[...]
        encode_tiles(
            size // 128, rows, lambda way, tile: projected_ref[2 * way, :, tile_lanes(tile, first)], taps_ref, first,
            coded_ref, driven_ref, strided_buf, peak_buf, levels_buf,
        )


def network_halves(layer_refs, halves_ref, scaled_buf):
    second_high, second_low = halves(second_layer(*layer_refs, scaled_buf))
    halves_ref[...] = jnp.concatenate([second_high, second_high, second_low], axis=1)


def network_filter_kernel(first, *refs):
    weight_refs, layer_refs, (near_ref, far_ref, halves_ref), bufs = refs[:5], refs[5:10], refs[10:13], refs[13:]
    network_halves(layer_refs, halves_ref, bufs[-1])
    filter_spectra(first, *weight_refs, halves_ref, near_ref, far_ref, *bufs[:-1])


def filter_spectra(
    first, out_ref, decay_ref, skip_ref, places_ref, forward_ref, halves_ref, near_ref, far_ref,
    raw_buf, parts_buf, spec_buf, scale_buf,
):
    rows, width = near_ref.shape[0] // 2, near_ref.shape[1]
    half = rows // 2
    out_high, out_low = halves(out_ref[:, first : first + width])
    raw_buf[...] = jnp.dot(
        halves_ref[...], jnp.concatenate([out_high, out_low, out_high], axis=0), preferred_element_type=jnp.float32
    )

    def decay(tile, _):
        cols = tile_lanes(tile)
        fall = -decay_ref[:, tile_lanes(tile, first)]
        total = jnp.zeros((8, 128), jnp.float32)
        for row in range(0, 2 * rows, 16):
            taps = raw_buf[row : row + 16, cols] * jnp.exp(fall * places_ref[row : row + 16])
            total = total + (taps[:8] * taps[:8] + taps[8:] * taps[8:])
            parity = row % rows // half
            put_halves(parts_buf, parity, row % half, tile_lanes(tile, row // rows * width), taps)
        for step in (1, 2, 4):
            total = total + pltpu.roll(total, step, 0)
        scale_buf[:, cols] = 1.0 / jnp.sqrt(total + 1e-05)

    each_tile(width // 128, 4, decay)
    forward_dots(forward_ref, parts_buf, spec_buf)

    def shape(tile, _):
        cols = tile_lanes(tile)
        scale = scale_buf[:, cols]
        scale = jnp.concatenate([scale, scale], axis=0)
        skip = skip_ref[:, tile_lanes(tile, first)]
        for row in range(0, half, 16):
            low = [value * scale for value in unfolded(spec_buf, row, cols)]
            high = [value * scale for value in unfolded(spec_buf, row, tile_lanes(tile, width))]
            sign = 1 if row < half // 2 else -1
            turned = [-sign * low[1], sign * low[0], sign * low[3], -sign * low[2]]
            low = [low[0] + skip, low[1], low[2] + skip, low[3]]
            for at in range(4):
                near_ref[at * half + row : at * half + row + 16, cols] = low[at]
                far_ref[at * half + row : at * half + row + 16, cols] = high[at] + turned[at]

    each_tile(width // 128, 4, shape)


def driven_parts(driven, parts_buf, cols):
    half = parts_buf.shape[1] // 2
    for at, value in enumerate(parity_rows(driven)):
        put_halves(parts_buf, 16 * at // half, 16 * at % half, cols, value)


def put_rows(ref, cols, values):
    for at, value in enumerate(parity_rows(values)):
        ref[16 * at : 16 * at + 16, cols] = value


def send_kernel(
    first, projected_ref, taps_ref, near_ref, far_ref, forward_ref, backward_ref, coded_ref, mixed_ref, gates_ref,
    strided_buf, parts_buf, spec_buf, bins_buf, right_buf, conv_buf, peak_buf, levels_buf,
):
    rows, width = right_buf.shape
    tiles = width // 128

    @pl.when(lax.axis_index("ctx") == 0)
    def _():
        def drive(tile, number):
            cols = tile_lanes(tile, first)
            sums = [
                short_sum(
                    strided_rows(projected_ref[at, :, cols], strided_buf.at[number, at]), None, taps_ref, at, cols
                )
                for at in range(3)
            ]
            put_rows(right_buf, tile_lanes(tile), sums[1])
            driven_parts([one * two for one, two in zip(sums[0], sums[2])], parts_buf, tile_lanes(tile))

        each_tile(tiles, strided_buf.shape[0], drive)
        forward_dots(forward_ref, parts_buf, spec_buf)
        each_tile(
            tiles, 4, lambda tile, _: filtered(spec_buf, far_ref, bins_buf, tile_lanes(tile), tile_lanes(tile))
        )
        backward_dots(backward_ref, bins_buf, conv_buf)

        def peaks(tile, _):
            cols = tile_lanes(tile)
            peak_buf[:, cols] = functools.reduce(
                jnp.maximum, [jnp.abs(conv_buf[row : row + 8, cols]) for row in range(0, rows, 8)]
            )

        each_tile(tiles, 4, peaks)
        code_tiles(tiles, rows, coded_ref, conv_buf, peak_buf, levels_buf)
        each_tile(
            tiles, 4, lambda tile, _: filtered(spec_buf, near_ref, bins_buf, tile_lanes(tile), tile_lanes(tile))
        )
        backward_dots(backward_ref, bins_buf, conv_buf)

        def mix(tile):
            cols = tile_lanes(tile)
            return [right_buf[at : at + 16, cols] * conv_buf[at : at + 16, cols] for at in range(0, rows, 16)]

        def gate(tile, number):
            cols = tile_lanes(tile)
            parts = strided_rows(projected_ref[1, :, cols], strided_buf.at[number, 1])
            put_rows(gates_ref, cols, short_sum(parts, None, taps_ref, 1, cols))

        each_tile(first // 128, strided_buf.shape[0], gate)
        mix_tiles(mix, tiles, mixed_ref, strided_buf.at[:, 0])


def own_kernel(
    projected_ref, rims_ref, taps_ref, near_ref, last_near_ref, forward_ref, backward_ref, one_ref, two_ref, gates_ref,
    behind_ref, right_ref, bins_ref, base_ref, mixed_ref,
    rims_buf, strided_buf, parts_buf, spec_buf, bins_buf, conv_buf, mixed_buf, sems,
):
    rows, width = right_ref.shape
    half = rows // 2
    middle = near_ref.shape[1]
    place = lax.axis_index("ctx")

    @pl.when(place == 0)
    def _():
        tiles = middle // 128
        behind = pltpu.make_async_copy(behind_ref, mixed_ref.at[:, pl.ds(middle, width - middle)], sems.at[0])
        behind.start()
        start = 0
        for ref in (one_ref, two_ref):

            def recall(tile, _, ref=ref, start=start):
                for row in range(0, rows, 16):
                    value = ref[row : row + 16, tile_lanes(tile)]
                    put_halves(parts_buf, row // half, row % half, tile_lanes(tile, start), value)

            each_tile(ref.shape[1] // 128, 4, recall)
            start += ref.shape[1]
        forward_dots(forward_ref, parts_buf.at[:, :, 0:middle], spec_buf.at[:, :, 0:middle])
        each_tile(
            tiles, 4, lambda tile, _: filtered(spec_buf, near_ref, bins_buf, tile_lanes(tile), tile_lanes(tile))
        )
        backward_dots(backward_ref, bins_buf, conv_buf)

        def mix(tile):
            cols = tile_lanes(tile)
            return [gates_ref[at : at + 16, cols] * conv_buf[at : at + 16, cols] for at in range(0, rows, 16)]

        mix_tiles(mix, tiles, mixed_buf, strided_buf.at[:, 0])
        ahead = pltpu.make_async_copy(mixed_buf, mixed_ref.at[:, pl.ds(0, middle)], sems.at[1])
        ahead.start()
        ahead.wait()
        behind.wait()

    @pl.when(place != 0)
    def _():
        read_rims(rims_ref, rims_buf)

        def drive(tile, number):
            cols = tile_lanes(tile)
            sums = [
                short_sum(
                    strided_rows(projected_ref[at, :, cols], strided_buf.at[number, at]),
                    rims_buf[at, :, cols], taps_ref, at, cols,
                )
                for at in range(3)
            ]
            put_rows(right_ref, cols, sums[1])
            driven_parts([one * two for one, two in zip(sums[0], sums[2])], parts_buf, cols)

        each_tile(width // 128, strided_buf.shape[0], drive)
        forward_dots(forward_ref, parts_buf, spec_buf)

        def keep(tile, _):
            cols = tile_lanes(tile)
            for row in range(0, half, 16):
                for at, value in enumerate(folded_products(spec_buf, near_ref, row, cols, cols)):
                    bins_ref[at * half + row : at * half + row + 16, cols] = value

        each_tile(middle // 128, 12, keep)
        behind = width - middle

        def finish(tile, _):
            there, cols = tile_lanes(tile, middle), tile_lanes(tile)
            for row in range(0, half, 16):
                put_bins(bins_buf, row, cols, folded_products(spec_buf, last_near_ref, row, there, cols))

        each_tile(behind // 128, 4, finish)
        backward_dots(backward_ref, bins_buf.at[:, :, 0:behind], base_ref)


def mix_tiles(mix, tiles, mixed_ref, strided_buf):
    def one(tile, number):
        mixed_ref[:, tile_lanes(tile)] = natural_rows(mix(tile), strided_buf.at[number]).astype(jnp.bfloat16)

    each_tile(tiles, strided_buf.shape[0], one)


def read_levels(coded_ref, levels_buf, tiles, rows):
    levels_buf[...] = coded_ref[tiles * rows : tiles * rows + 16].astype(jnp.float32)


def join_kernel(
    coded_refs, far_ref, own_bins_ref, right_ref, forward_ref, backward_ref, mixed_ref,
    parts_buf, spec_buf, bins_buf, conv_buf, strided_buf, levels_buf,
):
    rows, width = conv_buf.shape
    half = rows // 2
    tiles = width // 128

    @pl.when(lax.axis_index("ctx") != 0)
    def _():
        counts = [coded_refs[0].shape[0] // rows, coded_refs[1].shape[0] // rows]
        counts[0] = tiles - counts[1]
        read_levels(coded_refs[1], levels_buf, counts[1], rows)
        for at, ref in enumerate(coded_refs):
            start = counts[0] * 128 * at
            levels_first = 0 if at else 16 - counts[0]

            def spread_out(tile, _, ref=ref, start=start, levels_first=levels_first):
                decode = decoder(levels_buf, levels_first + tile)
                for row in range(0, rows, 16):
                    value = decode(ref[tile_rows(tile, row), :])
                    put_halves(parts_buf, row // half, row % half, tile_lanes(tile, start), value)

            each_tile(counts[at], 4, spread_out)
        forward_dots(forward_ref, parts_buf, spec_buf)

        def add(tile, _):
            cols = tile_lanes(tile)
            for row in range(0, half, 16):
                products = [
                    value + own_bins_ref[at * half + row : at * half + row + 16, cols]
                    for at, value in enumerate(folded_products(spec_buf, far_ref, row, cols, cols))
                ]
                put_bins(bins_buf, row, cols, products)

        each_tile(tiles, 12, add)
        backward_dots(backward_ref, bins_buf, conv_buf)

        def mix(tile):
            cols = tile_lanes(tile)
            return [right_ref[at : at + 16, cols] * conv_buf[at : at + 16, cols] for at in range(0, rows, 16)]

        mix_tiles(mix, tiles, mixed_ref, strided_buf)


def last_kernel(
    first, coded_ref, base_ref, right_ref, ahead_ref, _, mixed_ref, strided_buf, buf, levels_buf, sems
):
    rows, width = base_ref.shape
    tiles = width // 128

    @pl.when(lax.axis_index("ctx") != 0)
    def _():
        ahead = pltpu.make_async_copy(ahead_ref, mixed_ref.at[:, pl.ds(0, first)], sems.at[0])
        ahead.start()
        read_levels(coded_ref, levels_buf, tiles, rows)

        def mix(tile):
            decode = decoder(levels_buf, tile)
            return [
                right_ref[at : at + 16, tile_lanes(tile, first)]
                * (decode(coded_ref[tile_rows(tile, at), :]) + base_ref[at : at + 16, tile_lanes(tile)])
                for at in range(0, rows, 16)
            ]

        mix_tiles(mix, tiles, buf, strided_buf)
        behind = pltpu.make_async_copy(buf, mixed_ref.at[:, pl.ds(first, width)], sems.at[1])
        behind.start()
        behind.wait()
        ahead.wait()


def params(mib=40):
    return pltpu.CompilerParams(vmem_limit_bytes=mib * 1024 * 1024)


def cost(us):
    return pl.CostEstimate(flops=int(us * 1e9), bytes_accessed=int(us * 3e6), transcendentals=0)


def one_way(
    projected, short_weight, pos_in, pos_bias, sine_freq, pos_mid, pos_out, decay_rate, skip_gain
):
    _, rows, width = projected.shape
    half = rows // 2
    total_len = 2 * rows
    ahead = [width // 8, width * 5 // 8]
    middle = sum(ahead)
    behind = width - middle
    forward, backward = odd_tables(rows)
    taps = jnp.transpose(short_weight, (1, 0, 2))
    in_vmem = pl.BlockSpec(memory_space=pltpu.VMEM)
    in_hbm = pl.BlockSpec(memory_space=pltpu.HBM)
    floats, shorts = functools.partial(pltpu.VMEM, dtype=jnp.float32), functools.partial(pltpu.VMEM, dtype=jnp.bfloat16)
    pairs = [(0, 1)]

    def arrays(*shapes, dtype=jnp.float32):
        return [jax.ShapeDtypeStruct(shape, dtype) for shape in shapes]

    def message(size, more=0):
        return arrays((size // 128 * rows + 16 + more, 128), dtype=jnp.bfloat16)

    order = parity_order(rows)
    places = np.concatenate([order, order + rows]).astype(np.float32)
    feats = feature_table(places, total_len)
    places = np.repeat(places[:, None], 128, 1)
    layers = (feats, pos_in, pos_bias[None, :], sine_freq[None, :], pos_mid)
    tile_bufs = [floats((2, 2, rows, 128)), floats((8, width)), floats((16, 128))]
    one, two = ahead
    one_code, one_driven, one_levels = pl.pallas_call(
        first_kernel,
        in_specs=[in_hbm] * 2,
        out_specs=[in_vmem] * 3,
        out_shape=arrays((one // 128 * rows + width // 128 * 18, 128), dtype=jnp.bfloat16)
        + arrays((rows, one), (16, 128)),
        scratch_shapes=[shorts((2, rows, one)), shorts((3, 16, width)), floats((3, TAPS, one))]
        + tile_bufs[:2]
        + [pltpu.SemaphoreType.DMA((4,))],
        compiler_params=params(),
        cost_estimate=cost(1),
        name="first",
    )(*[pltpu.with_memory_space_constraint(array, pltpu.HBM) for array in (projected, taps)])
    one_code = lax.ppermute(one_code, "ctx", [(0, 1), (1, 0)])
    weights = (pos_out, decay_rate[None, :], skip_gain[None, :], places, forward)
    hidden = pos_mid.shape[1]

    def spectra_bufs(size):
        return [floats((total_len, size)), shorts((2, rows, 2 * size)), floats((2, rows, 2 * size)), floats((8, size))]

    spectra = arrays((total_len, behind), (total_len, behind)) + arrays((total_len, 3 * hidden), dtype=jnp.bfloat16)
    two_code, two_driven = pl.pallas_call(
        functools.partial(encode_kernel, one),
        in_specs=[in_vmem] * 3,
        out_specs=[in_vmem] * 2,
        out_shape=message(two) + arrays((rows, two)),
        scratch_shapes=tile_bufs,
        compiler_params=params(),
        cost_estimate=cost(1),
        name="encode",
    )(projected, taps, one_levels)
    two_code = lax.ppermute(two_code, "ctx", [(0, 1), (1, 0)])
    last_near, last_far, second_halves = pl.pallas_call(
        functools.partial(network_filter_kernel, middle),
        in_specs=[in_vmem] * 10,
        out_specs=[in_vmem] * 3,
        out_shape=spectra,
        scratch_shapes=spectra_bufs(behind) + [floats((feats.shape[0], hidden))],
        compiler_params=params(),
        cost_estimate=cost(2),
        name="filter",
    )(*weights, *layers)
    near, far = pl.pallas_call(
        functools.partial(filter_spectra, 0),
        in_specs=[in_vmem] * 6,
        out_specs=[in_vmem] * 2,
        out_shape=arrays((total_len, middle), (total_len, middle)),
        scratch_shapes=spectra_bufs(middle),
        compiler_params=params(),
        cost_estimate=cost(2),
        name="filter",
    )(*weights, second_halves)
    last_near, near = lax.optimization_barrier((last_near, near))
    last_code, behind_mixed, gates = pl.pallas_call(
        functools.partial(send_kernel, middle),
        in_specs=[in_vmem] * 6,
        out_specs=[in_vmem] * 3,
        out_shape=message(behind) + arrays((rows, behind), dtype=jnp.bfloat16) + arrays((rows, middle)),
        scratch_shapes=[
            floats((2, 3, rows, 128)),
            shorts((2, rows, behind)),
            floats((2, rows, behind)),
            shorts((2, 2 * rows, behind)),
            floats((rows, behind)),
            floats((rows, behind)),
            floats((8, behind)),
            floats((16, 128)),
        ],
        compiler_params=params(),
        cost_estimate=cost(2),
        name="send",
    )(projected, taps, last_near, last_far, forward, backward)
    last_code = lax.ppermute(last_code, "ctx", pairs)
    right, own_bins, last_base, mixed = pl.pallas_call(
        own_kernel,
        in_specs=[in_vmem] * 11,
        out_specs=[in_vmem] * 3 + [in_hbm],
        out_shape=arrays((rows, width), (total_len, middle), (rows, behind))
        + arrays((rows, width), dtype=jnp.bfloat16),
        scratch_shapes=[
            floats((3, 8, width)),
            floats((2, 3, rows, 128)),
            shorts((2, rows, width)),
            floats((2, rows, width)),
            shorts((2, 2 * rows, middle)),
            floats((rows, middle)),
            shorts((rows, middle)),
            pltpu.SemaphoreType.DMA((2,)),
        ],
        compiler_params=params(),
        cost_estimate=cost(4),
        name="own",
    )(projected, one_code, taps, near, last_near, forward, backward, one_driven, two_driven, gates, behind_mixed)
    ahead_mixed = pl.pallas_call(
        lambda one_ref, two_ref, *refs: join_kernel((one_ref, two_ref), *refs),
        in_specs=[in_vmem] * 7,
        out_specs=in_vmem,
        out_shape=jax.ShapeDtypeStruct((rows, middle), jnp.bfloat16),
        scratch_shapes=[
            shorts((2, rows, middle)),
            floats((2, rows, middle)),
            shorts((2, 2 * rows, middle)),
            floats((rows, middle)),
            floats((4, rows, 128)),
            floats((16, 128)),
        ],
        compiler_params=params(),
        cost_estimate=cost(2),
        name="join",
    )(one_code, two_code, far, own_bins, right, forward, backward)
    return pl.pallas_call(
        functools.partial(last_kernel, middle),
        in_specs=[in_vmem] * 4 + [in_hbm],
        out_specs=in_hbm,
        out_shape=jax.ShapeDtypeStruct((rows, width), jnp.bfloat16),
        input_output_aliases={4: 0},
        scratch_shapes=[
            floats((4, rows, 128)),
            shorts((rows, behind)),
            floats((16, 128)),
            pltpu.SemaphoreType.DMA((2,)),
        ],
        compiler_params=params(),
        cost_estimate=cost(1),
        name="last",
    )(last_code, last_base, right, ahead_mixed, mixed)


def turn_table(outer_ids, inner_ids, modulus):
    product_grid = outer_ids[:, None] * inner_ids[None, :] % modulus
    angles = product_grid.astype(jnp.float32) * (2.0 * math.pi / modulus)
    return (jnp.cos(angles), jnp.sin(angles))


def section_outer(table, data):
    return jnp.einsum(
        "ka,cab->ckb", table, data, precision=HIGHEST, preferred_element_type=jnp.float32
    )


def section_inner(table, data):
    return jnp.einsum(
        "ckb,bj->ckj", data, table, precision=HIGHEST, preferred_element_type=jnp.float32
    )


def padded_spectrum(signal, outer_count, inner_count, tables):
    cos_half, sin_half, cos_twist, sin_twist, cos_inner, sin_inner = tables
    shaped = signal.reshape(signal.shape[0], outer_count // 2, inner_count)
    real_one = section_outer(cos_half, shaped)
    imag_one = -section_outer(sin_half, shaped)
    real_two = real_one * cos_twist + imag_one * sin_twist
    imag_two = imag_one * cos_twist - real_one * sin_twist
    spec_real = section_inner(cos_inner, real_two) + section_inner(sin_inner, imag_two)
    spec_imag = section_inner(cos_inner, imag_two) - section_inner(sin_inner, real_two)
    return (spec_real, spec_imag)


def causal_local(driven_cols, normed_cols, total_len):
    full_len = 2 * total_len
    inner_count = math.gcd(total_len, 128)
    outer_count = full_len // inner_count
    outer_full = jnp.arange(outer_count, dtype=jnp.int32)
    outer_half = jnp.arange(outer_count // 2, dtype=jnp.int32)
    inner_ids = jnp.arange(inner_count, dtype=jnp.int32)
    cos_half, sin_half = turn_table(outer_full, outer_half, outer_count)
    cos_twist, sin_twist = turn_table(outer_full, inner_ids, full_len)
    cos_inner, sin_inner = turn_table(inner_ids, inner_ids, inner_count)
    tables = (cos_half, sin_half, cos_twist, sin_twist, cos_inner, sin_inner)
    sig_real, sig_imag = padded_spectrum(driven_cols, outer_count, inner_count, tables)
    fil_real, fil_imag = padded_spectrum(normed_cols, outer_count, inner_count, tables)
    prod_real = sig_real * fil_real - sig_imag * fil_imag
    prod_imag = sig_real * fil_imag + sig_imag * fil_real
    back_real = section_inner(cos_inner, prod_real) - section_inner(sin_inner, prod_imag)
    back_imag = section_inner(sin_inner, prod_real) + section_inner(cos_inner, prod_imag)
    turned_real = back_real * cos_twist - back_imag * sin_twist
    turned_imag = back_real * sin_twist + back_imag * cos_twist
    cos_last, sin_last = turn_table(outer_half, outer_full, outer_count)
    result = (
        section_outer(cos_last, turned_real) - section_outer(sin_last, turned_imag)
    ) / full_len
    return result.reshape(driven_cols.shape[0], total_len)


def exchanged(
    projected, short_weight, pos_in, pos_bias, sine_freq, pos_mid, pos_out, decay_rate, skip_gain
):
    ctx_count = lax.axis_size("ctx")
    ctx_place = lax.axis_index("ctx")
    block_rows = projected.shape[1]
    total_len = block_rows * ctx_count
    rim_rows = shifted(projected[:, block_rows - (TAPS - 1) :, :], "ctx", 1)
    extended = jnp.concatenate([rim_rows, projected], axis=1)
    short_out = jnp.zeros(projected.shape, jnp.float32)
    for tap_index in range(TAPS):
        offset = TAPS - 1 - tap_index
        short_out = short_out + short_weight[tap_index][:, None, :] * extended[
            :, offset : offset + block_rows, :
        ].astype(jnp.float32)
    left_gate, right_gate, value_stream = (short_out[0], short_out[1], short_out[2])
    driven = left_gate * value_stream
    own_width = driven.shape[1] // ctx_count
    driven_cols = lax.all_to_all(driven.T, "ctx", split_axis=0, concat_axis=1, tiled=True)
    own_out = lax.dynamic_slice_in_dim(pos_out, ctx_place * own_width, own_width, 1)
    own_decay = lax.dynamic_slice_in_dim(decay_rate, ctx_place * own_width, own_width, 0)
    positions = jnp.arange(total_len, dtype=jnp.int32).astype(jnp.float32)
    long_filter = filter_rows(
        positions, total_len, pos_in, pos_bias, sine_freq, pos_mid, own_out, own_decay
    )
    normed = long_filter / jnp.sqrt(jnp.sum(long_filter * long_filter, axis=0) + 1e-05)
    conv_cols = causal_local(driven_cols, normed.T, total_len)
    long_conv = lax.all_to_all(conv_cols, "ctx", split_axis=1, concat_axis=0, tiled=True).T
    return (right_gate * (long_conv + skip_gain[None, :] * driven)).astype(jnp.bfloat16)


def body(projected, *others):
    if lax.axis_size("ctx") == 2:
        return one_way(projected, *others)
    return exchanged(projected, *others)


def solution(mesh):
    placed = (
        P(None, ("dp", "ctx"), "chan"),
        P(None, None, "chan"),
        P(),
        P(),
        P(),
        P(),
        P(None, "chan"),
        P("chan"),
        P("chan"),
    )
    return jax.shard_map(
        body, mesh=mesh, in_specs=placed, out_specs=P(("dp", "ctx"), "chan"), check_vma=False
    )
```

```python
import functools
import math

import jax
import jax.numpy as jnp
import numpy as np
from jax import lax
from jax.experimental import pallas as pl
from jax.experimental.pallas import tpu as pltpu
from jax.sharding import PartitionSpec as P

BANDS = 16
TAPS = 7
SPAN = 250.0
TINY = 1e-30

HIGHEST = lax.Precision.HIGHEST


def shifted(x, axis, by):
    size = lax.axis_size(axis)
    pairs = [(i, i + by) for i in range(size) if 0 <= i + by < size]
    return lax.ppermute(x, axis, pairs)


def features(positions, total_len):
    band_ids = jnp.arange(1, BANDS + 1, dtype=jnp.float32)
    angles = positions[:, None] * band_ids[None, :] * (2.0 * math.pi / total_len)
    return jnp.concatenate(
        [positions[:, None] / total_len, jnp.cos(angles), jnp.sin(angles)], axis=1
    )


def second_rows(positions, total_len, pos_in, pos_bias, sine_freq, pos_mid):
    inputs = features(positions, total_len)
    first_layer = jnp.sin(
        sine_freq
        * (
            jnp.dot(inputs, pos_in, precision=HIGHEST, preferred_element_type=jnp.float32)
            + pos_bias
        )
    )
    return jnp.sin(
        sine_freq
        * jnp.dot(first_layer, pos_mid, precision=HIGHEST, preferred_element_type=jnp.float32)
    )


def filter_rows(positions, total_len, pos_in, pos_bias, sine_freq, pos_mid, pos_out, decay_rate):
    second_layer = second_rows(positions, total_len, pos_in, pos_bias, sine_freq, pos_mid)
    raw_filter = jnp.dot(
        second_layer, pos_out, precision=HIGHEST, preferred_element_type=jnp.float32
    )
    return raw_filter * jnp.exp(-decay_rate[None, :] * positions[:, None])


def halves(x):
    high = x.astype(jnp.bfloat16)
    low = (x - high.astype(jnp.float32)).astype(jnp.bfloat16)
    return high, low


def feature_table(places, total_len):
    bands = np.arange(1, BANDS + 1, dtype=np.float32)
    angles = places[:, None] * bands[None, :] * np.float32(2.0 * math.pi / total_len)
    first = places[:, None] / np.float32(total_len)
    table = np.concatenate([first, np.cos(angles), np.sin(angles), np.ones_like(first)], axis=1)
    spare = np.zeros((places.shape[0], -table.shape[1] % 8))
    return np.concatenate([table, spare], axis=1).astype(np.float32).T.copy()


def parity_order(rows):
    place = np.arange(rows)
    parity, inner = place // (rows // 2), place % (rows // 2)
    return rows // 8 * (inner % 8) + inner // 8 * 2 + parity


def table_columns(table):
    high = table.astype(jnp.bfloat16)
    low = (table - high.astype(np.float32)).astype(jnp.bfloat16)
    return np.concatenate([high, high, low], axis=1)


def odd_tables(rows):
    half = rows // 2
    order = np.concatenate([np.arange(0, half, 2), np.arange(1, half, 2)])
    turns = (2 * order[:, None] + 1) * parity_order(rows)[None, :] % (4 * rows)
    angles = turns * (np.pi / (2 * rows))
    forward = np.concatenate([np.cos(angles), -np.sin(angles)], axis=0).astype(np.float32)
    pieces = [forward[:, :half], forward[:, half:]]
    return (
        np.concatenate([table_columns(piece) for piece in pieces], axis=0),
        np.concatenate([table_columns(piece.T / np.float32(rows)) for piece in pieces], axis=0),
    )


def each_tile(tiles, unroll, action):
    count = math.gcd(tiles, unroll)

    def step(at, _):
        for number in range(count):
            action(at * count + number, number)
        return 0

    if tiles == count:
        step(0, 0)
    else:
        lax.fori_loop(0, tiles // count, step, 0)


def put_halves(ref, parity, row, cols, value):
    size = ref.shape[1] // 2
    high, low = halves(value)
    count = value.shape[0]
    ref[parity, row : row + count, cols] = high
    ref[parity, size + row : size + row + count, cols] = low


def three_pass(table, ref, parity):
    size = ref.shape[1] // 2
    both = jnp.concatenate([ref[parity], ref[parity, :size]], axis=0)
    return jnp.dot(table, both, preferred_element_type=jnp.float32)


def forward_dots(forward_ref, parts_ref, spec_ref):
    rows = spec_ref.shape[1]
    for parity in range(2):
        spec_ref[parity] = three_pass(forward_ref[parity * rows : (parity + 1) * rows], parts_ref, parity)


def backward_dots(backward_ref, bins_ref, conv_ref):
    half = conv_ref.shape[0] // 2
    for parity in range(2):
        rows = slice(parity * half, (parity + 1) * half)
        conv_ref[rows] = three_pass(backward_ref[rows], bins_ref, parity)


def unfolded(spec_ref, row, cols):
    half = spec_ref.shape[1] // 2
    even_cos, odd_cos = spec_ref[0, row : row + 16, cols], spec_ref[1, row : row + 16, cols]
    sine = slice(half + row, half + row + 16)
    even_sin, odd_sin = spec_ref[0, sine, cols], spec_ref[1, sine, cols]
    return even_cos + odd_cos, even_sin + odd_sin, even_cos - odd_cos, odd_sin - even_sin


def folded_products(spec_ref, filter_ref, row, cols, filter_cols):
    half = spec_ref.shape[1] // 2
    real, imag, real_far, imag_far = unfolded(spec_ref, row, cols)
    taps = [filter_ref[at * half + row : at * half + row + 16, filter_cols] for at in range(4)]
    out_real, out_imag = real * taps[0] - imag * taps[1], real * taps[1] + imag * taps[0]
    far_real = real_far * taps[2] - imag_far * taps[3]
    far_imag = real_far * taps[3] + imag_far * taps[2]
    return out_real + far_real, out_imag - far_imag, out_real - far_real, out_imag + far_imag


def put_bins(bins_ref, row, cols, products):
    half = bins_ref.shape[1] // 4
    for at, value in enumerate(products):
        put_halves(bins_ref, at // 2, at % 2 * half + row, cols, value)


def filtered(spec_ref, filter_ref, bins_ref, cols, filter_cols):
    for row in range(0, spec_ref.shape[1] // 2, 16):
        put_bins(bins_ref, row, cols, folded_products(spec_ref, filter_ref, row, cols, filter_cols))


def strided_rows(values, buf):
    buf[...] = values.astype(jnp.float32)
    count = buf.shape[0] // 8
    return [buf[pl.ds(v, 8, stride=count), :] for v in range(count)]


def short_sum(parts, rim, taps_ref, at, cols):
    top = lax.broadcasted_iota(jnp.int32, (8, 128), 0) == 0
    before = {}
    for back in range(1, TAPS):
        edge = 0.0 if rim is None else rim[8 - back : 9 - back]
        before[-back] = jnp.where(top, edge, pltpu.roll(parts[-back], 1, 0))
    taps = [jnp.broadcast_to(taps_ref[at, k : k + 1, cols], (8, 128)) for k in range(TAPS)]
    sums = []
    for v in range(len(parts)):
        terms = [taps[k] * (parts[v - k] if v >= k else before[v - k]) for k in range(TAPS)]
        sums.append(((terms[0] + terms[1]) + (terms[2] + terms[3])) + ((terms[4] + terms[5]) + terms[6]))
    return sums


def parity_rows(parts):
    ordered = parts[0::2] + parts[1::2]
    return [jnp.concatenate(ordered[i : i + 2], axis=0) for i in range(0, len(ordered), 2)]


def natural_rows(ref_rows, buf):
    count = buf.shape[0] // 8
    for at, value in enumerate(ref_rows):
        for piece in range(2):
            number = 2 * at + piece
            v = number % (count // 2) * 2 + number // (count // 2)
            buf[pl.ds(v, 8, stride=count), :] = value[8 * piece : 8 * piece + 8]
    return buf[...]


def tile_lanes(tile, first=0):
    return pl.ds(pl.multiple_of(first + tile * 128, 128), 128)


def tile_rows(tile, row, count=16):
    return pl.ds(pl.multiple_of(tile * 128 + row, 16), count)


def place_level(peak, tile, peak_buf, levels_buf, levels_first):
    for step in (1, 2, 4):
        peak = jnp.maximum(peak, pltpu.roll(peak, step, 0))
    level = jnp.maximum(peak, TINY)
    wide = level * 65537.0
    level = wide - (wide - level)
    peak_buf[:, tile_lanes(tile)] = SPAN / level
    levels_buf[pl.ds(levels_first + tile, 1), :] = level[0:1]


def put_coded(coded_ref, tile, row, value, gain):
    coded = jnp.exp2(jnp.abs(value) * gain - SPAN / 2)
    coded_ref[tile_rows(tile, row), :] = jnp.where(value < 0, -coded, coded).astype(jnp.bfloat16)


def decoder(levels_buf, tile):
    level = levels_buf[pl.ds(tile, 1), :]
    slope = jnp.broadcast_to(level * (1.0 / (math.log(2.0) * SPAN)), (16, 128))
    middle = jnp.broadcast_to(level / 2, (16, 128))

    def decode(coded):
        coded = coded.astype(jnp.float32)
        size = jnp.log(jnp.abs(coded)) * slope + middle
        return jnp.where(coded < 0, -size, size)

    return decode


def second_layer(feats_ref, in_ref, bias_ref, freq_ref, mid_ref, scaled_buf):
    dot = functools.partial(
        lax.dot_general,
        dimension_numbers=(((0,), (0,)), ((), ())),
        precision=HIGHEST,
        preferred_element_type=jnp.float32,
    )
    count = in_ref.shape[0]
    freq = freq_ref[...]
    scaled_buf[...] = jnp.zeros_like(scaled_buf)
    scaled_buf[0:count] = in_ref[...] * freq
    scaled_buf[count : count + 1] = bias_ref[...] * freq
    layer = jnp.sin(dot(scaled_buf[...], feats_ref[...]))
    return jnp.sin(dot(mid_ref[...] * freq, layer)).T


def encode_tiles(
    tiles, rows, streams, taps_ref, taps_first, coded_ref, driven_ref, strided_buf, peak_buf, levels_buf, levels_first=0
):
    def drive(tile, number):
        cols = tile_lanes(tile)
        sums = [
            short_sum(
                strided_rows(streams(way, tile), strided_buf.at[number, way]),
                None, taps_ref, 2 * way, tile_lanes(tile, taps_first),
            )
            for way in range(2)
        ]
        driven = [one * two for one, two in zip(*sums)]
        for row, value in enumerate(parity_rows(driven)):
            driven_ref[16 * row : 16 * row + 16, cols] = value
        peak_buf[:, cols] = functools.reduce(jnp.maximum, [jnp.abs(value) for value in driven])

    each_tile(tiles, strided_buf.shape[0], drive)
    code_tiles(tiles, rows, coded_ref, driven_ref, peak_buf, levels_buf, levels_first)


def code_tiles(tiles, rows, coded_ref, values_ref, peak_buf, levels_buf, levels_first=0):
    each_tile(
        tiles, 4,
        lambda tile, _: place_level(peak_buf[:, tile_lanes(tile)], tile, peak_buf, levels_buf, levels_first),
    )
    if levels_first == 0:
        coded_ref[tiles * rows : tiles * rows + 16] = levels_buf[...].astype(jnp.bfloat16)

    def code(tile, _):
        cols = tile_lanes(tile)
        gain = peak_buf[:, cols]
        gain = jnp.concatenate([gain, gain], axis=0)
        for row in range(0, rows, 16):
            put_coded(coded_ref, tile, row, values_ref[row : row + 16, cols], gain)

    each_tile(tiles, 4, code)


def first_kernel(
    projected_ref, taps_ref, coded_ref, driven_ref, levels_ref, rows_buf, rim_buf, taps_buf, strided_buf, peak_buf, sems
):
    rows, size = rows_buf.shape[1:]
    tiles = size // 128

    @pl.when(lax.axis_index("ctx") == 0)
    def _():
        span = pl.ds(0, size)
        copies = [
            pltpu.make_async_copy(taps_ref.at[:, :, span], taps_buf, sems.at[0]),
            pltpu.make_async_copy(projected_ref.at[0, :, span], rows_buf.at[0], sems.at[1]),
            pltpu.make_async_copy(projected_ref.at[2, :, span], rows_buf.at[1], sems.at[2]),
            pltpu.make_async_copy(projected_ref.at[:, pl.ds(rows - 16, 16)], rim_buf, sems.at[3]),
        ]
        for copy in copies:
            copy.start()
        for copy in copies[:3]:
            copy.wait()
        levels_ref[...] = jnp.zeros_like(levels_ref)
        encode_tiles(
            tiles, rows, lambda way, tile: rows_buf[way, :, tile_lanes(tile)], taps_buf, 0, coded_ref, driven_ref,
            strided_buf, peak_buf, levels_ref, 16 - tiles,
        )
        copies[3].wait()
        for at in range(3):
            for group in range(rim_buf.shape[2] // 1024):
                there = tiles * rows + (3 * group + at) * 48
                values = [
                    rim_buf[at, :, (8 * group + way) * 128 : (8 * group + way + 1) * 128].astype(jnp.float32)[8:]
                    for way in range(8)
                ]
                values = pack_rims(values)
                for pair in range(3):
                    both = jnp.concatenate(values[2 * pair : 2 * pair + 2], axis=0)
                    coded_ref[there + 16 * pair : there + 16 * pair + 16] = both.astype(jnp.bfloat16)


def pack_rims(values):
    top = lax.broadcasted_iota(jnp.int32, (8, 128), 0) < 2
    return [
        jnp.where(top, pltpu.roll(values[6 + at // 3], 6 - 2 * (at % 3), 0), values[at]) for at in range(6)
    ]


def unpack_rims(values):
    place = lax.broadcasted_iota(jnp.int32, (8, 128), 0)
    rest = []
    for at in range(2):
        turned = [pltpu.roll(values[3 * at + way], 2 + 2 * way, 0) for way in range(3)]
        rest.append(jnp.where(place < 4, turned[0], jnp.where(place < 6, turned[1], turned[2])))
    return values + rest


def read_rims(coded_ref, rims_buf):
    groups = rims_buf.shape[2] // 1024
    start = coded_ref.shape[0] - groups * 144
    for at in range(3):
        for group in range(groups):
            there = start + (3 * group + at) * 48
            packed = coded_ref[there : there + 48].astype(jnp.float32)
            values = unpack_rims([packed[8 * way : 8 * way + 8] for way in range(6)])
            for way, value in enumerate(values):
                rims_buf[at, :, (8 * group + way) * 128 : (8 * group + way + 1) * 128] = value


def encode_kernel(
    first, projected_ref, taps_ref, one_levels_ref, coded_ref, driven_ref, strided_buf, peak_buf, levels_buf
):
    rows, size = driven_ref.shape

    @pl.when(lax.axis_index("ctx") == 0)
    def _():
        levels_buf[...] = one_levels_ref[...]
        encode_tiles(
            size // 128, rows, lambda way, tile: projected_ref[2 * way, :, tile_lanes(tile, first)], taps_ref, first,
            coded_ref, driven_ref, strided_buf, peak_buf, levels_buf,
        )


def network_halves(layer_refs, halves_ref, scaled_buf):
    second_high, second_low = halves(second_layer(*layer_refs, scaled_buf))
    halves_ref[...] = jnp.concatenate([second_high, second_high, second_low], axis=1)


def network_filter_kernel(first, *refs):
    weight_refs, layer_refs, (near_ref, far_ref, halves_ref), bufs = refs[:5], refs[5:10], refs[10:13], refs[13:]
    network_halves(layer_refs, halves_ref, bufs[-1])
    filter_spectra(first, *weight_refs, halves_ref, near_ref, far_ref, *bufs[:-1])


def filter_spectra(
    first, out_ref, decay_ref, skip_ref, places_ref, forward_ref, halves_ref, near_ref, far_ref,
    raw_buf, parts_buf, spec_buf, scale_buf,
):
    rows, width = near_ref.shape[0] // 2, near_ref.shape[1]
    half = rows // 2
    out_high, out_low = halves(out_ref[:, first : first + width])
    raw_buf[...] = jnp.dot(
        halves_ref[...], jnp.concatenate([out_high, out_low, out_high], axis=0), preferred_element_type=jnp.float32
    )

    def decay(tile, _):
        cols = tile_lanes(tile)
        fall = -decay_ref[:, tile_lanes(tile, first)]
        total = jnp.zeros((8, 128), jnp.float32)
        for row in range(0, 2 * rows, 16):
            taps = raw_buf[row : row + 16, cols] * jnp.exp(fall * places_ref[row : row + 16])
            total = total + (taps[:8] * taps[:8] + taps[8:] * taps[8:])
            parity = row % rows // half
            put_halves(parts_buf, parity, row % half, tile_lanes(tile, row // rows * width), taps)
        for step in (1, 2, 4):
            total = total + pltpu.roll(total, step, 0)
        scale_buf[:, cols] = 1.0 / jnp.sqrt(total + 1e-05)

    each_tile(width // 128, 12, decay)
    forward_dots(forward_ref, parts_buf, spec_buf)

    def shape(tile, _):
        cols = tile_lanes(tile)
        scale = scale_buf[:, cols]
        scale = jnp.concatenate([scale, scale], axis=0)
        skip = skip_ref[:, tile_lanes(tile, first)]
        for row in range(0, half, 16):
            low = [value * scale for value in unfolded(spec_buf, row, cols)]
            high = [value * scale for value in unfolded(spec_buf, row, tile_lanes(tile, width))]
            sign = 1 if row < half // 2 else -1
            turned = [-sign * low[1], sign * low[0], sign * low[3], -sign * low[2]]
            low = [low[0] + skip, low[1], low[2] + skip, low[3]]
            for at in range(4):
                near_ref[at * half + row : at * half + row + 16, cols] = low[at]
                far_ref[at * half + row : at * half + row + 16, cols] = high[at] + turned[at]

    each_tile(width // 128, 12, shape)


def driven_parts(driven, parts_buf, cols):
    half = parts_buf.shape[1] // 2
    for at, value in enumerate(parity_rows(driven)):
        put_halves(parts_buf, 16 * at // half, 16 * at % half, cols, value)


def put_rows(ref, cols, values):
    for at, value in enumerate(parity_rows(values)):
        ref[16 * at : 16 * at + 16, cols] = value


def send_kernel(
    first, projected_ref, taps_ref, near_ref, far_ref, forward_ref, backward_ref, ahead_near_ref, one_ref, two_ref,
    coded_ref, mixed_ref, gates_ref, ahead_bins_ref,
    strided_buf, parts_buf, spec_buf, bins_buf, right_buf, conv_buf, peak_buf, levels_buf, ahead_parts_buf,
    ahead_spec_buf,
):
    rows, width = right_buf.shape
    half = rows // 2
    tiles = width // 128

    @pl.when(lax.axis_index("ctx") == 0)
    def _():
        def drive(tile, number):
            cols = tile_lanes(tile, first)
            sums = [
                short_sum(
                    strided_rows(projected_ref[at, :, cols], strided_buf.at[number, at]), None, taps_ref, at, cols
                )
                for at in range(3)
            ]
            put_rows(right_buf, tile_lanes(tile), sums[1])
            driven_parts([one * two for one, two in zip(sums[0], sums[2])], parts_buf, tile_lanes(tile))

        each_tile(tiles, strided_buf.shape[0], drive)
        forward_dots(forward_ref, parts_buf, spec_buf)
        each_tile(
            tiles, 4, lambda tile, _: filtered(spec_buf, far_ref, bins_buf, tile_lanes(tile), tile_lanes(tile))
        )
        backward_dots(backward_ref, bins_buf, conv_buf)

        def peaks(tile, _):
            cols = tile_lanes(tile)
            peak_buf[:, cols] = functools.reduce(
                jnp.maximum, [jnp.abs(conv_buf[row : row + 8, cols]) for row in range(0, rows, 8)]
            )

        each_tile(tiles, 4, peaks)
        code_tiles(tiles, rows, coded_ref, conv_buf, peak_buf, levels_buf)
        each_tile(
            tiles, 4, lambda tile, _: filtered(spec_buf, near_ref, bins_buf, tile_lanes(tile), tile_lanes(tile))
        )
        backward_dots(backward_ref, bins_buf, conv_buf)

        def mix(tile):
            cols = tile_lanes(tile)
            return [right_buf[at : at + 16, cols] * conv_buf[at : at + 16, cols] for at in range(0, rows, 16)]

        def gate(tile, number):
            cols = tile_lanes(tile)
            parts = strided_rows(projected_ref[1, :, cols], strided_buf.at[number, 1])
            put_rows(gates_ref, cols, short_sum(parts, None, taps_ref, 1, cols))

        each_tile(first // 128, strided_buf.shape[0], gate)
        start = 0
        for ref in (one_ref, two_ref):

            def recall(tile, _, ref=ref, start=start):
                for row in range(0, rows, 16):
                    value = ref[row : row + 16, tile_lanes(tile)]
                    put_halves(ahead_parts_buf, row // half, row % half, tile_lanes(tile, start), value)

            each_tile(ref.shape[1] // 128, 4, recall)
            start += ref.shape[1]
        forward_dots(forward_ref, ahead_parts_buf, ahead_spec_buf)
        each_tile(
            first // 128, 4,
            lambda tile, _: filtered(
                ahead_spec_buf, ahead_near_ref, ahead_bins_ref, tile_lanes(tile), tile_lanes(tile)
            ),
        )
        mix_tiles(mix, tiles, mixed_ref, strided_buf.at[:, 0])


def own_kernel(
    projected_ref, rims_ref, taps_ref, near_ref, last_near_ref, forward_ref, backward_ref, gates_ref, ahead_bins_ref,
    behind_ref, right_ref, bins_ref, base_ref, mixed_ref,
    rims_buf, strided_buf, parts_buf, spec_buf, bins_buf, conv_buf, mixed_buf, sems,
):
    rows, width = right_ref.shape
    half = rows // 2
    middle = near_ref.shape[1]
    place = lax.axis_index("ctx")

    @pl.when(place == 0)
    def _():
        tiles = middle // 128
        behind = pltpu.make_async_copy(behind_ref, mixed_ref.at[:, pl.ds(middle, width - middle)], sems.at[0])
        behind.start()
        backward_dots(backward_ref, ahead_bins_ref, conv_buf)

        def mix(tile):
            cols = tile_lanes(tile)
            return [gates_ref[at : at + 16, cols] * conv_buf[at : at + 16, cols] for at in range(0, rows, 16)]

        mix_tiles(mix, tiles, mixed_buf, strided_buf.at[:, 0])
        ahead = pltpu.make_async_copy(mixed_buf, mixed_ref.at[:, pl.ds(0, middle)], sems.at[1])
        ahead.start()
        ahead.wait()
        behind.wait()

    @pl.when(place != 0)
    def _():
        read_rims(rims_ref, rims_buf)

        def drive(tile, number):
            cols = tile_lanes(tile)
            sums = [
                short_sum(
                    strided_rows(projected_ref[at, :, cols], strided_buf.at[number, at]),
                    rims_buf[at, :, cols], taps_ref, at, cols,
                )
                for at in range(3)
            ]
            put_rows(right_ref, cols, sums[1])
            driven_parts([one * two for one, two in zip(sums[0], sums[2])], parts_buf, cols)

        each_tile(width // 128, strided_buf.shape[0], drive)
        forward_dots(forward_ref, parts_buf, spec_buf)

        def keep(tile, _):
            cols = tile_lanes(tile)
            for row in range(0, half, 16):
                for at, value in enumerate(folded_products(spec_buf, near_ref, row, cols, cols)):
                    bins_ref[at * half + row : at * half + row + 16, cols] = value

        each_tile(middle // 128, 12, keep)
        behind = width - middle

        def finish(tile, _):
            there, cols = tile_lanes(tile, middle), tile_lanes(tile)
            for row in range(0, half, 16):
                put_bins(bins_buf, row, cols, folded_products(spec_buf, last_near_ref, row, there, cols))

        each_tile(behind // 128, 4, finish)
        backward_dots(backward_ref, bins_buf, base_ref)


def mix_tiles(mix, tiles, mixed_ref, strided_buf):
    def one(tile, number):
        mixed_ref[:, tile_lanes(tile)] = natural_rows(mix(tile), strided_buf.at[number]).astype(jnp.bfloat16)

    each_tile(tiles, strided_buf.shape[0], one)


def read_levels(coded_ref, levels_buf, tiles, rows):
    levels_buf[...] = coded_ref[tiles * rows : tiles * rows + 16].astype(jnp.float32)


def join_kernel(
    coded_refs, far_ref, own_bins_ref, right_ref, forward_ref, backward_ref, mixed_ref,
    parts_buf, spec_buf, bins_buf, conv_buf, strided_buf, levels_buf,
):
    rows, width = conv_buf.shape
    half = rows // 2
    tiles = width // 128

    @pl.when(lax.axis_index("ctx") != 0)
    def _():
        counts = [coded_refs[0].shape[0] // rows, coded_refs[1].shape[0] // rows]
        counts[0] = tiles - counts[1]
        read_levels(coded_refs[1], levels_buf, counts[1], rows)
        for at, ref in enumerate(coded_refs):
            start = counts[0] * 128 * at
            levels_first = 0 if at else 16 - counts[0]

            def spread_out(tile, _, ref=ref, start=start, levels_first=levels_first):
                decode = decoder(levels_buf, levels_first + tile)
                for row in range(0, rows, 16):
                    value = decode(ref[tile_rows(tile, row), :])
                    put_halves(parts_buf, row // half, row % half, tile_lanes(tile, start), value)

            each_tile(counts[at], 4, spread_out)
        forward_dots(forward_ref, parts_buf, spec_buf)

        def add(tile, _):
            cols = tile_lanes(tile)
            for row in range(0, half, 16):
                products = [
                    value + own_bins_ref[at * half + row : at * half + row + 16, cols]
                    for at, value in enumerate(folded_products(spec_buf, far_ref, row, cols, cols))
                ]
                put_bins(bins_buf, row, cols, products)

        each_tile(tiles, 12, add)
        backward_dots(backward_ref, bins_buf, conv_buf)

        def mix(tile):
            cols = tile_lanes(tile)
            return [right_ref[at : at + 16, cols] * conv_buf[at : at + 16, cols] for at in range(0, rows, 16)]

        mix_tiles(mix, tiles, mixed_ref, strided_buf)


def last_kernel(
    first, coded_ref, base_ref, right_ref, ahead_ref, _, mixed_ref, strided_buf, buf, levels_buf, sems
):
    rows, width = base_ref.shape
    tiles = width // 128

    @pl.when(lax.axis_index("ctx") != 0)
    def _():
        ahead = pltpu.make_async_copy(ahead_ref, mixed_ref.at[:, pl.ds(0, first)], sems.at[0])
        ahead.start()
        read_levels(coded_ref, levels_buf, tiles, rows)

        def mix(tile):
            decode = decoder(levels_buf, tile)
            return [
                right_ref[at : at + 16, tile_lanes(tile, first)]
                * (decode(coded_ref[tile_rows(tile, at), :]) + base_ref[at : at + 16, tile_lanes(tile)])
                for at in range(0, rows, 16)
            ]

        mix_tiles(mix, tiles, buf, strided_buf)
        behind = pltpu.make_async_copy(buf, mixed_ref.at[:, pl.ds(first, width)], sems.at[1])
        behind.start()
        behind.wait()
        ahead.wait()


def params(mib=40):
    return pltpu.CompilerParams(vmem_limit_bytes=mib * 1024 * 1024)


def cost(us):
    return pl.CostEstimate(flops=int(us * 1e9), bytes_accessed=int(us * 3e6), transcendentals=0)


def one_way(
    projected, short_weight, pos_in, pos_bias, sine_freq, pos_mid, pos_out, decay_rate, skip_gain
):
    _, rows, width = projected.shape
    half = rows // 2
    total_len = 2 * rows
    ahead = [width // 8, width * 5 // 8]
    middle = sum(ahead)
    behind = width - middle
    forward, backward = odd_tables(rows)
    taps = jnp.transpose(short_weight, (1, 0, 2))
    in_vmem = pl.BlockSpec(memory_space=pltpu.VMEM)
    in_hbm = pl.BlockSpec(memory_space=pltpu.HBM)
    floats, shorts = functools.partial(pltpu.VMEM, dtype=jnp.float32), functools.partial(pltpu.VMEM, dtype=jnp.bfloat16)
    pairs = [(0, 1)]

    def arrays(*shapes, dtype=jnp.float32):
        return [jax.ShapeDtypeStruct(shape, dtype) for shape in shapes]

    def message(size, more=0):
        return arrays((size // 128 * rows + 16 + more, 128), dtype=jnp.bfloat16)

    order = parity_order(rows)
    places = np.concatenate([order, order + rows]).astype(np.float32)
    feats = feature_table(places, total_len)
    places = np.repeat(places[:, None], 128, 1)
    layers = (feats, pos_in, pos_bias[None, :], sine_freq[None, :], pos_mid)
    tile_bufs = [floats((2, 2, rows, 128)), floats((8, width)), floats((16, 128))]
    one, two = ahead
    one_code, one_driven, one_levels = pl.pallas_call(
        first_kernel,
        in_specs=[in_hbm] * 2,
        out_specs=[in_vmem] * 3,
        out_shape=arrays((one // 128 * rows + width // 128 * 18, 128), dtype=jnp.bfloat16)
        + arrays((rows, one), (16, 128)),
        scratch_shapes=[shorts((2, rows, one)), shorts((3, 16, width)), floats((3, TAPS, one))]
        + tile_bufs[:2]
        + [pltpu.SemaphoreType.DMA((4,))],
        compiler_params=params(),
        cost_estimate=cost(1),
        name="first",
    )(*[pltpu.with_memory_space_constraint(array, pltpu.HBM) for array in (projected, taps)])
    one_code = lax.ppermute(one_code, "ctx", [(0, 1), (1, 0)])
    weights = (pos_out, decay_rate[None, :], skip_gain[None, :], places, forward)
    hidden = pos_mid.shape[1]

    def spectra_bufs(size):
        return [floats((total_len, size)), shorts((2, rows, 2 * size)), floats((2, rows, 2 * size)), floats((8, size))]

    spectra = arrays((total_len, behind), (total_len, behind)) + arrays((total_len, 3 * hidden), dtype=jnp.bfloat16)
    two_code, two_driven = pl.pallas_call(
        functools.partial(encode_kernel, one),
        in_specs=[in_vmem] * 3,
        out_specs=[in_vmem] * 2,
        out_shape=message(two) + arrays((rows, two)),
        scratch_shapes=tile_bufs,
        compiler_params=params(),
        cost_estimate=cost(1),
        name="encode",
    )(projected, taps, one_levels)
    two_code = lax.ppermute(two_code, "ctx", [(0, 1), (1, 0)])
    last_near, last_far, second_halves = pl.pallas_call(
        functools.partial(network_filter_kernel, middle),
        in_specs=[in_vmem] * 10,
        out_specs=[in_vmem] * 3,
        out_shape=spectra,
        scratch_shapes=spectra_bufs(behind) + [floats((feats.shape[0], hidden))],
        compiler_params=params(),
        cost_estimate=cost(2),
        name="filter",
    )(*weights, *layers)
    near, far = pl.pallas_call(
        functools.partial(filter_spectra, 0),
        in_specs=[in_vmem] * 6,
        out_specs=[in_vmem] * 2,
        out_shape=arrays((total_len, middle), (total_len, middle)),
        scratch_shapes=spectra_bufs(middle),
        compiler_params=params(),
        cost_estimate=cost(2),
        name="filter",
    )(*weights, second_halves)
    last_near, near = lax.optimization_barrier((last_near, near))
    last_code, behind_mixed, gates, ahead_bins = pl.pallas_call(
        functools.partial(send_kernel, middle),
        in_specs=[in_vmem] * 9,
        out_specs=[in_vmem] * 4,
        out_shape=message(behind)
        + arrays((rows, behind), dtype=jnp.bfloat16)
        + arrays((rows, middle))
        + arrays((2, 2 * rows, middle), dtype=jnp.bfloat16),
        scratch_shapes=[
            floats((2, 3, rows, 128)),
            shorts((2, rows, behind)),
            floats((2, rows, behind)),
            shorts((2, 2 * rows, behind)),
            floats((rows, behind)),
            floats((rows, behind)),
            floats((8, behind)),
            floats((16, 128)),
            shorts((2, rows, middle)),
            floats((2, rows, middle)),
        ],
        compiler_params=params(),
        cost_estimate=cost(2),
        name="send",
    )(projected, taps, last_near, last_far, forward, backward, near, one_driven, two_driven)
    last_code = lax.ppermute(last_code, "ctx", pairs)
    right, own_bins, last_base, mixed = pl.pallas_call(
        own_kernel,
        in_specs=[in_vmem] * 10,
        out_specs=[in_vmem] * 3 + [in_hbm],
        out_shape=arrays((rows, width), (total_len, middle), (rows, behind))
        + arrays((rows, width), dtype=jnp.bfloat16),
        scratch_shapes=[
            floats((3, 8, width)),
            floats((2, 3, rows, 128)),
            shorts((2, rows, width)),
            floats((2, rows, width)),
            shorts((2, 2 * rows, behind)),
            floats((rows, middle)),
            shorts((rows, middle)),
            pltpu.SemaphoreType.DMA((2,)),
        ],
        compiler_params=params(),
        cost_estimate=cost(4),
        name="own",
    )(projected, one_code, taps, near, last_near, forward, backward, gates, ahead_bins, behind_mixed)
    ahead_mixed = pl.pallas_call(
        lambda one_ref, two_ref, *refs: join_kernel((one_ref, two_ref), *refs),
        in_specs=[in_vmem] * 7,
        out_specs=in_vmem,
        out_shape=jax.ShapeDtypeStruct((rows, middle), jnp.bfloat16),
        scratch_shapes=[
            shorts((2, rows, middle)),
            floats((2, rows, middle)),
            shorts((2, 2 * rows, middle)),
            floats((rows, middle)),
            floats((4, rows, 128)),
            floats((16, 128)),
        ],
        compiler_params=params(),
        cost_estimate=cost(2),
        name="join",
    )(one_code, two_code, far, own_bins, right, forward, backward)
    return pl.pallas_call(
        functools.partial(last_kernel, middle),
        in_specs=[in_vmem] * 4 + [in_hbm],
        out_specs=in_hbm,
        out_shape=jax.ShapeDtypeStruct((rows, width), jnp.bfloat16),
        input_output_aliases={4: 0},
        scratch_shapes=[
            floats((4, rows, 128)),
            shorts((rows, behind)),
            floats((16, 128)),
            pltpu.SemaphoreType.DMA((2,)),
        ],
        compiler_params=params(),
        cost_estimate=cost(1),
        name="last",
    )(last_code, last_base, right, ahead_mixed, mixed)


def turn_table(outer_ids, inner_ids, modulus):
    product_grid = outer_ids[:, None] * inner_ids[None, :] % modulus
    angles = product_grid.astype(jnp.float32) * (2.0 * math.pi / modulus)
    return (jnp.cos(angles), jnp.sin(angles))


def section_outer(table, data):
    return jnp.einsum(
        "ka,cab->ckb", table, data, precision=HIGHEST, preferred_element_type=jnp.float32
    )


def section_inner(table, data):
    return jnp.einsum(
        "ckb,bj->ckj", data, table, precision=HIGHEST, preferred_element_type=jnp.float32
    )


def padded_spectrum(signal, outer_count, inner_count, tables):
    cos_half, sin_half, cos_twist, sin_twist, cos_inner, sin_inner = tables
    shaped = signal.reshape(signal.shape[0], outer_count // 2, inner_count)
    real_one = section_outer(cos_half, shaped)
    imag_one = -section_outer(sin_half, shaped)
    real_two = real_one * cos_twist + imag_one * sin_twist
    imag_two = imag_one * cos_twist - real_one * sin_twist
    spec_real = section_inner(cos_inner, real_two) + section_inner(sin_inner, imag_two)
    spec_imag = section_inner(cos_inner, imag_two) - section_inner(sin_inner, real_two)
    return (spec_real, spec_imag)


def causal_local(driven_cols, normed_cols, total_len):
    full_len = 2 * total_len
    inner_count = math.gcd(total_len, 128)
    outer_count = full_len // inner_count
    outer_full = jnp.arange(outer_count, dtype=jnp.int32)
    outer_half = jnp.arange(outer_count // 2, dtype=jnp.int32)
    inner_ids = jnp.arange(inner_count, dtype=jnp.int32)
    cos_half, sin_half = turn_table(outer_full, outer_half, outer_count)
    cos_twist, sin_twist = turn_table(outer_full, inner_ids, full_len)
    cos_inner, sin_inner = turn_table(inner_ids, inner_ids, inner_count)
    tables = (cos_half, sin_half, cos_twist, sin_twist, cos_inner, sin_inner)
    sig_real, sig_imag = padded_spectrum(driven_cols, outer_count, inner_count, tables)
    fil_real, fil_imag = padded_spectrum(normed_cols, outer_count, inner_count, tables)
    prod_real = sig_real * fil_real - sig_imag * fil_imag
    prod_imag = sig_real * fil_imag + sig_imag * fil_real
    back_real = section_inner(cos_inner, prod_real) - section_inner(sin_inner, prod_imag)
    back_imag = section_inner(sin_inner, prod_real) + section_inner(cos_inner, prod_imag)
    turned_real = back_real * cos_twist - back_imag * sin_twist
    turned_imag = back_real * sin_twist + back_imag * cos_twist
    cos_last, sin_last = turn_table(outer_half, outer_full, outer_count)
    result = (
        section_outer(cos_last, turned_real) - section_outer(sin_last, turned_imag)
    ) / full_len
    return result.reshape(driven_cols.shape[0], total_len)


def exchanged(
    projected, short_weight, pos_in, pos_bias, sine_freq, pos_mid, pos_out, decay_rate, skip_gain
):
    ctx_count = lax.axis_size("ctx")
    ctx_place = lax.axis_index("ctx")
    block_rows = projected.shape[1]
    total_len = block_rows * ctx_count
    rim_rows = shifted(projected[:, block_rows - (TAPS - 1) :, :], "ctx", 1)
    extended = jnp.concatenate([rim_rows, projected], axis=1)
    short_out = jnp.zeros(projected.shape, jnp.float32)
    for tap_index in range(TAPS):
        offset = TAPS - 1 - tap_index
        short_out = short_out + short_weight[tap_index][:, None, :] * extended[
            :, offset : offset + block_rows, :
        ].astype(jnp.float32)
    left_gate, right_gate, value_stream = (short_out[0], short_out[1], short_out[2])
    driven = left_gate * value_stream
    own_width = driven.shape[1] // ctx_count
    driven_cols = lax.all_to_all(driven.T, "ctx", split_axis=0, concat_axis=1, tiled=True)
    own_out = lax.dynamic_slice_in_dim(pos_out, ctx_place * own_width, own_width, 1)
    own_decay = lax.dynamic_slice_in_dim(decay_rate, ctx_place * own_width, own_width, 0)
    positions = jnp.arange(total_len, dtype=jnp.int32).astype(jnp.float32)
    long_filter = filter_rows(
        positions, total_len, pos_in, pos_bias, sine_freq, pos_mid, own_out, own_decay
    )
    normed = long_filter / jnp.sqrt(jnp.sum(long_filter * long_filter, axis=0) + 1e-05)
    conv_cols = causal_local(driven_cols, normed.T, total_len)
    long_conv = lax.all_to_all(conv_cols, "ctx", split_axis=1, concat_axis=0, tiled=True).T
    return (right_gate * (long_conv + skip_gain[None, :] * driven)).astype(jnp.bfloat16)


def body(projected, *others):
    if lax.axis_size("ctx") == 2:
        return one_way(projected, *others)
    return exchanged(projected, *others)


def solution(mesh):
    placed = (
        P(None, ("dp", "ctx"), "chan"),
        P(None, None, "chan"),
        P(),
        P(),
        P(),
        P(),
        P(None, "chan"),
        P("chan"),
        P("chan"),
    )
    return jax.shard_map(
        body, mesh=mesh, in_specs=placed, out_specs=P(("dp", "ctx"), "chan"), check_vma=False
    )
```

```python
import functools
import math

import jax
import jax.numpy as jnp
import numpy as np
from jax import lax
from jax.experimental import pallas as pl
from jax.experimental.pallas import tpu as pltpu
from jax.sharding import PartitionSpec as P

BANDS = 16
TAPS = 7
SPAN = 250.0
TINY = 1e-30

HIGHEST = lax.Precision.HIGHEST


def shifted(x, axis, by):
    size = lax.axis_size(axis)
    pairs = [(i, i + by) for i in range(size) if 0 <= i + by < size]
    return lax.ppermute(x, axis, pairs)


def features(positions, total_len):
    band_ids = jnp.arange(1, BANDS + 1, dtype=jnp.float32)
    angles = positions[:, None] * band_ids[None, :] * (2.0 * math.pi / total_len)
    return jnp.concatenate(
        [positions[:, None] / total_len, jnp.cos(angles), jnp.sin(angles)], axis=1
    )


def second_rows(positions, total_len, pos_in, pos_bias, sine_freq, pos_mid):
    inputs = features(positions, total_len)
    first_layer = jnp.sin(
        sine_freq
        * (
            jnp.dot(inputs, pos_in, precision=HIGHEST, preferred_element_type=jnp.float32)
            + pos_bias
        )
    )
    return jnp.sin(
        sine_freq
        * jnp.dot(first_layer, pos_mid, precision=HIGHEST, preferred_element_type=jnp.float32)
    )


def filter_rows(positions, total_len, pos_in, pos_bias, sine_freq, pos_mid, pos_out, decay_rate):
    second_layer = second_rows(positions, total_len, pos_in, pos_bias, sine_freq, pos_mid)
    raw_filter = jnp.dot(
        second_layer, pos_out, precision=HIGHEST, preferred_element_type=jnp.float32
    )
    return raw_filter * jnp.exp(-decay_rate[None, :] * positions[:, None])


def halves(x):
    high = x.astype(jnp.bfloat16)
    low = (x - high.astype(jnp.float32)).astype(jnp.bfloat16)
    return high, low


def feature_table(places, total_len):
    bands = np.arange(1, BANDS + 1, dtype=np.float32)
    angles = places[:, None] * bands[None, :] * np.float32(2.0 * math.pi / total_len)
    first = places[:, None] / np.float32(total_len)
    table = np.concatenate([first, np.cos(angles), np.sin(angles), np.ones_like(first)], axis=1)
    spare = np.zeros((places.shape[0], -table.shape[1] % 8))
    return np.concatenate([table, spare], axis=1).astype(np.float32).T.copy()


def parity_order(rows):
    place = np.arange(rows)
    parity, inner = place // (rows // 2), place % (rows // 2)
    return rows // 8 * (inner % 8) + inner // 8 * 2 + parity


def table_columns(table):
    high = table.astype(jnp.bfloat16)
    low = (table - high.astype(np.float32)).astype(jnp.bfloat16)
    return np.concatenate([high, high, low], axis=1)


def odd_tables(rows):
    half = rows // 2
    order = np.concatenate([np.arange(0, half, 2), np.arange(1, half, 2)])
    turns = (2 * order[:, None] + 1) * parity_order(rows)[None, :] % (4 * rows)
    angles = turns * (np.pi / (2 * rows))
    forward = np.concatenate([np.cos(angles), -np.sin(angles)], axis=0).astype(np.float32)
    pieces = [forward[:, :half], forward[:, half:]]
    return (
        np.concatenate([table_columns(piece) for piece in pieces], axis=0),
        np.concatenate([table_columns(piece.T / np.float32(rows)) for piece in pieces], axis=0),
    )


def each_tile(tiles, unroll, action):
    count = math.gcd(tiles, unroll)

    def step(at, _):
        for number in range(count):
            action(at * count + number, number)
        return 0

    if tiles == count:
        step(0, 0)
    else:
        lax.fori_loop(0, tiles // count, step, 0)


def put_halves(ref, parity, row, cols, value):
    size = ref.shape[1] // 2
    high, low = halves(value)
    count = value.shape[0]
    ref[parity, row : row + count, cols] = high
    ref[parity, size + row : size + row + count, cols] = low


def three_pass(table, ref, parity):
    size = ref.shape[1] // 2
    both = jnp.concatenate([ref[parity], ref[parity, :size]], axis=0)
    return jnp.dot(table, both, preferred_element_type=jnp.float32)


def forward_dots(forward_ref, parts_ref, spec_ref):
    rows = spec_ref.shape[1]
    for parity in range(2):
        spec_ref[parity] = three_pass(forward_ref[parity * rows : (parity + 1) * rows], parts_ref, parity)


def backward_dots(backward_ref, bins_ref, conv_ref):
    half = conv_ref.shape[0] // 2
    for parity in range(2):
        rows = slice(parity * half, (parity + 1) * half)
        conv_ref[rows] = three_pass(backward_ref[rows], bins_ref, parity)


def unfolded(spec_ref, row, cols):
    half = spec_ref.shape[1] // 2
    even_cos, odd_cos = spec_ref[0, row : row + 16, cols], spec_ref[1, row : row + 16, cols]
    sine = slice(half + row, half + row + 16)
    even_sin, odd_sin = spec_ref[0, sine, cols], spec_ref[1, sine, cols]
    return even_cos + odd_cos, even_sin + odd_sin, even_cos - odd_cos, odd_sin - even_sin


def folded_products(spec_ref, filter_ref, row, cols, filter_cols):
    half = spec_ref.shape[1] // 2
    real, imag, real_far, imag_far = unfolded(spec_ref, row, cols)
    taps = [filter_ref[at * half + row : at * half + row + 16, filter_cols] for at in range(4)]
    out_real, out_imag = real * taps[0] - imag * taps[1], real * taps[1] + imag * taps[0]
    far_real = real_far * taps[2] - imag_far * taps[3]
    far_imag = real_far * taps[3] + imag_far * taps[2]
    return out_real + far_real, out_imag - far_imag, out_real - far_real, out_imag + far_imag


def put_bins(bins_ref, row, cols, products):
    half = bins_ref.shape[1] // 4
    for at, value in enumerate(products):
        put_halves(bins_ref, at // 2, at % 2 * half + row, cols, value)


def filtered(spec_ref, filter_ref, bins_ref, cols, filter_cols):
    for row in range(0, spec_ref.shape[1] // 2, 16):
        put_bins(bins_ref, row, cols, folded_products(spec_ref, filter_ref, row, cols, filter_cols))


def strided_rows(values, buf):
    buf[...] = values.astype(jnp.float32)
    count = buf.shape[0] // 8
    return [buf[pl.ds(v, 8, stride=count), :] for v in range(count)]


def short_sum(parts, rim, taps_ref, at, cols):
    top = lax.broadcasted_iota(jnp.int32, (8, 128), 0) == 0
    before = {}
    for back in range(1, TAPS):
        edge = 0.0 if rim is None else rim[8 - back : 9 - back]
        before[-back] = jnp.where(top, edge, pltpu.roll(parts[-back], 1, 0))
    taps = [jnp.broadcast_to(taps_ref[at, k : k + 1, cols], (8, 128)) for k in range(TAPS)]
    sums = []
    for v in range(len(parts)):
        terms = [taps[k] * (parts[v - k] if v >= k else before[v - k]) for k in range(TAPS)]
        sums.append(((terms[0] + terms[1]) + (terms[2] + terms[3])) + ((terms[4] + terms[5]) + terms[6]))
    return sums


def parity_rows(parts):
    ordered = parts[0::2] + parts[1::2]
    return [jnp.concatenate(ordered[i : i + 2], axis=0) for i in range(0, len(ordered), 2)]


def natural_rows(ref_rows, buf):
    count = buf.shape[0] // 8
    for at, value in enumerate(ref_rows):
        for piece in range(2):
            number = 2 * at + piece
            v = number % (count // 2) * 2 + number // (count // 2)
            buf[pl.ds(v, 8, stride=count), :] = value[8 * piece : 8 * piece + 8]
    return buf[...]


def tile_lanes(tile, first=0):
    return pl.ds(pl.multiple_of(first + tile * 128, 128), 128)


def tile_rows(tile, row, count=16):
    return pl.ds(pl.multiple_of(tile * 128 + row, 16), count)


def natural_tile(ref, cols, buf):
    return natural_rows([ref[at : at + 16, cols] for at in range(0, ref.shape[0], 16)], buf)


def place_level(peak, tile, peak_buf, levels_buf, levels_first):
    for step in (1, 2, 4):
        peak = jnp.maximum(peak, pltpu.roll(peak, step, 0))
    level = jnp.maximum(peak, TINY)
    wide = level * 65537.0
    level = wide - (wide - level)
    peak_buf[:, tile_lanes(tile)] = SPAN / level
    levels_buf[pl.ds(levels_first + tile, 1), :] = level[0:1]


def put_coded(coded_ref, tile, row, value, gain):
    coded = jnp.exp2(jnp.abs(value) * gain - SPAN / 2)
    coded_ref[tile_rows(tile, row), :] = jnp.where(value < 0, -coded, coded).astype(jnp.bfloat16)


def decoder(levels_buf, tile):
    level = levels_buf[pl.ds(tile, 1), :]
    slope = jnp.broadcast_to(level * (1.0 / (math.log(2.0) * SPAN)), (16, 128))
    middle = jnp.broadcast_to(level / 2, (16, 128))

    def decode(coded):
        coded = coded.astype(jnp.float32)
        size = jnp.log(jnp.abs(coded)) * slope + middle
        return jnp.where(coded < 0, -size, size)

    return decode


def second_layer(feats_ref, in_ref, bias_ref, freq_ref, mid_ref, scaled_buf):
    dot = functools.partial(
        lax.dot_general,
        dimension_numbers=(((0,), (0,)), ((), ())),
        precision=HIGHEST,
        preferred_element_type=jnp.float32,
    )
    count = in_ref.shape[0]
    freq = freq_ref[...]
    scaled_buf[...] = jnp.zeros_like(scaled_buf)
    scaled_buf[0:count] = in_ref[...] * freq
    scaled_buf[count : count + 1] = bias_ref[...] * freq
    layer = jnp.sin(dot(scaled_buf[...], feats_ref[...]))
    return jnp.sin(dot(mid_ref[...] * freq, layer)).T


def encode_tiles(
    tiles, rows, streams, taps_ref, taps_first, coded_ref, driven_ref, strided_buf, peak_buf, levels_buf, levels_first=0
):
    def drive(tile, number):
        cols = tile_lanes(tile)
        sums = [
            short_sum(
                strided_rows(streams(way, tile), strided_buf.at[number, way]),
                None, taps_ref, 2 * way, tile_lanes(tile, taps_first),
            )
            for way in range(2)
        ]
        driven = [one * two for one, two in zip(*sums)]
        for row, value in enumerate(parity_rows(driven)):
            driven_ref[16 * row : 16 * row + 16, cols] = value
        peak_buf[:, cols] = functools.reduce(jnp.maximum, [jnp.abs(value) for value in driven])

    each_tile(tiles, strided_buf.shape[0], drive)
    code_tiles(tiles, rows, coded_ref, driven_ref, peak_buf, levels_buf, levels_first)


def code_tiles(tiles, rows, coded_ref, values_ref, peak_buf, levels_buf, levels_first=0):
    each_tile(
        tiles, 4,
        lambda tile, _: place_level(peak_buf[:, tile_lanes(tile)], tile, peak_buf, levels_buf, levels_first),
    )
    if levels_first == 0:
        coded_ref[tiles * rows : tiles * rows + 16] = levels_buf[...].astype(jnp.bfloat16)

    def code(tile, _):
        cols = tile_lanes(tile)
        gain = peak_buf[:, cols]
        gain = jnp.concatenate([gain, gain], axis=0)
        for row in range(0, rows, 16):
            put_coded(coded_ref, tile, row, values_ref[row : row + 16, cols], gain)

    each_tile(tiles, 4, code)


def first_kernel(
    projected_ref, taps_ref, coded_ref, driven_ref, levels_ref, rows_buf, rim_buf, taps_buf, strided_buf, peak_buf, sems
):
    rows, size = rows_buf.shape[1:]
    tiles = size // 128

    @pl.when(lax.axis_index("ctx") == 0)
    def _():
        span = pl.ds(0, size)
        copies = [
            pltpu.make_async_copy(taps_ref.at[:, :, span], taps_buf, sems.at[0]),
            pltpu.make_async_copy(projected_ref.at[0, :, span], rows_buf.at[0], sems.at[1]),
            pltpu.make_async_copy(projected_ref.at[2, :, span], rows_buf.at[1], sems.at[2]),
            pltpu.make_async_copy(projected_ref.at[:, pl.ds(rows - 16, 16)], rim_buf, sems.at[3]),
        ]
        for copy in copies:
            copy.start()
        for copy in copies[:3]:
            copy.wait()
        levels_ref[...] = jnp.zeros_like(levels_ref)
        encode_tiles(
            tiles, rows, lambda way, tile: rows_buf[way, :, tile_lanes(tile)], taps_buf, 0, coded_ref, driven_ref,
            strided_buf, peak_buf, levels_ref, 16 - tiles,
        )
        copies[3].wait()
        for at in range(3):
            for group in range(rim_buf.shape[2] // 1024):
                there = tiles * rows + (3 * group + at) * 48
                values = [
                    rim_buf[at, :, (8 * group + way) * 128 : (8 * group + way + 1) * 128].astype(jnp.float32)[8:]
                    for way in range(8)
                ]
                values = pack_rims(values)
                for pair in range(3):
                    both = jnp.concatenate(values[2 * pair : 2 * pair + 2], axis=0)
                    coded_ref[there + 16 * pair : there + 16 * pair + 16] = both.astype(jnp.bfloat16)


def pack_rims(values):
    top = lax.broadcasted_iota(jnp.int32, (8, 128), 0) < 2
    return [
        jnp.where(top, pltpu.roll(values[6 + at // 3], 6 - 2 * (at % 3), 0), values[at]) for at in range(6)
    ]


def unpack_rims(values):
    place = lax.broadcasted_iota(jnp.int32, (8, 128), 0)
    rest = []
    for at in range(2):
        turned = [pltpu.roll(values[3 * at + way], 2 + 2 * way, 0) for way in range(3)]
        rest.append(jnp.where(place < 4, turned[0], jnp.where(place < 6, turned[1], turned[2])))
    return values + rest


def read_rims(coded_ref, rims_buf):
    groups = rims_buf.shape[2] // 1024
    start = coded_ref.shape[0] - groups * 144
    for at in range(3):
        for group in range(groups):
            there = start + (3 * group + at) * 48
            packed = coded_ref[there : there + 48].astype(jnp.float32)
            values = unpack_rims([packed[8 * way : 8 * way + 8] for way in range(6)])
            for way, value in enumerate(values):
                rims_buf[at, :, (8 * group + way) * 128 : (8 * group + way + 1) * 128] = value


def encode_kernel(
    first, projected_ref, taps_ref, one_levels_ref, coded_ref, driven_ref, strided_buf, peak_buf, levels_buf
):
    rows, size = driven_ref.shape

    @pl.when(lax.axis_index("ctx") == 0)
    def _():
        levels_buf[...] = one_levels_ref[...]
        encode_tiles(
            size // 128, rows, lambda way, tile: projected_ref[2 * way, :, tile_lanes(tile, first)], taps_ref, first,
            coded_ref, driven_ref, strided_buf, peak_buf, levels_buf,
        )


def network_halves(layer_refs, halves_ref, scaled_buf):
    second_high, second_low = halves(second_layer(*layer_refs, scaled_buf))
    halves_ref[...] = jnp.concatenate([second_high, second_high, second_low], axis=1)


def network_filter_kernel(first, *refs):
    weight_refs, layer_refs, (near_ref, far_ref, halves_ref), bufs = refs[:5], refs[5:10], refs[10:13], refs[13:]
    network_halves(layer_refs, halves_ref, bufs[-1])
    filter_spectra(first, *weight_refs, halves_ref, near_ref, far_ref, *bufs[:-1])


def filter_spectra(
    first, out_ref, decay_ref, skip_ref, places_ref, forward_ref, halves_ref, near_ref, far_ref,
    raw_buf, parts_buf, spec_buf, scale_buf,
):
    rows, width = near_ref.shape[0] // 2, near_ref.shape[1]
    half = rows // 2
    out_high, out_low = halves(out_ref[:, first : first + width])
    raw_buf[...] = jnp.dot(
        halves_ref[...], jnp.concatenate([out_high, out_low, out_high], axis=0), preferred_element_type=jnp.float32
    )

    def decay(tile, _):
        cols = tile_lanes(tile)
        fall = -decay_ref[:, tile_lanes(tile, first)]
        total = jnp.zeros((8, 128), jnp.float32)
        for row in range(0, 2 * rows, 16):
            taps = raw_buf[row : row + 16, cols] * jnp.exp(fall * places_ref[row : row + 16])
            total = total + (taps[:8] * taps[:8] + taps[8:] * taps[8:])
            parity = row % rows // half
            put_halves(parts_buf, parity, row % half, tile_lanes(tile, row // rows * width), taps)
        for step in (1, 2, 4):
            total = total + pltpu.roll(total, step, 0)
        scale_buf[:, cols] = 1.0 / jnp.sqrt(total + 1e-05)

    each_tile(width // 128, 12, decay)
    forward_dots(forward_ref, parts_buf, spec_buf)

    def shape(tile, _):
        cols = tile_lanes(tile)
        scale = scale_buf[:, cols]
        scale = jnp.concatenate([scale, scale], axis=0)
        skip = skip_ref[:, tile_lanes(tile, first)]
        for row in range(0, half, 16):
            low = [value * scale for value in unfolded(spec_buf, row, cols)]
            high = [value * scale for value in unfolded(spec_buf, row, tile_lanes(tile, width))]
            sign = 1 if row < half // 2 else -1
            turned = [-sign * low[1], sign * low[0], sign * low[3], -sign * low[2]]
            low = [low[0] + skip, low[1], low[2] + skip, low[3]]
            for at in range(4):
                near_ref[at * half + row : at * half + row + 16, cols] = low[at]
                far_ref[at * half + row : at * half + row + 16, cols] = high[at] + turned[at]

    each_tile(width // 128, 12, shape)


def driven_parts(driven, parts_buf, cols):
    half = parts_buf.shape[1] // 2
    for at, value in enumerate(parity_rows(driven)):
        put_halves(parts_buf, 16 * at // half, 16 * at % half, cols, value)


def put_rows(ref, cols, values):
    for at, value in enumerate(parity_rows(values)):
        ref[16 * at : 16 * at + 16, cols] = value


def send_kernel(
    first, projected_ref, taps_ref, near_ref, far_ref, forward_ref, backward_ref, ahead_near_ref, one_ref, two_ref,
    coded_ref, mixed_ref, gates_ref, ahead_bins_ref,
    strided_buf, parts_buf, spec_buf, bins_buf, right_buf, conv_buf, peak_buf, levels_buf, ahead_parts_buf,
    ahead_spec_buf,
):
    rows, width = right_buf.shape
    half = rows // 2
    tiles = width // 128

    @pl.when(lax.axis_index("ctx") == 0)
    def _():
        def drive(tile, number):
            cols = tile_lanes(tile, first)
            sums = [
                short_sum(
                    strided_rows(projected_ref[at, :, cols], strided_buf.at[number, at]), None, taps_ref, at, cols
                )
                for at in range(3)
            ]
            put_rows(right_buf, tile_lanes(tile), sums[1])
            driven_parts([one * two for one, two in zip(sums[0], sums[2])], parts_buf, tile_lanes(tile))

        each_tile(tiles, strided_buf.shape[0], drive)
        forward_dots(forward_ref, parts_buf, spec_buf)
        each_tile(
            tiles, 4, lambda tile, _: filtered(spec_buf, far_ref, bins_buf, tile_lanes(tile), tile_lanes(tile))
        )
        backward_dots(backward_ref, bins_buf, conv_buf)

        def peaks(tile, number):
            cols = tile_lanes(tile)
            conv_buf[:, cols] = natural_tile(conv_buf, cols, strided_buf.at[number, 0])
            peak_buf[:, cols] = functools.reduce(
                jnp.maximum, [jnp.abs(conv_buf[row : row + 8, cols]) for row in range(0, rows, 8)]
            )

        each_tile(tiles, strided_buf.shape[0], peaks)
        code_tiles(tiles, rows, coded_ref, conv_buf, peak_buf, levels_buf)
        each_tile(
            tiles, 4, lambda tile, _: filtered(spec_buf, near_ref, bins_buf, tile_lanes(tile), tile_lanes(tile))
        )
        backward_dots(backward_ref, bins_buf, conv_buf)

        def mix(tile):
            cols = tile_lanes(tile)
            return [right_buf[at : at + 16, cols] * conv_buf[at : at + 16, cols] for at in range(0, rows, 16)]

        def gate(tile, number):
            cols = tile_lanes(tile)
            parts = strided_rows(projected_ref[1, :, cols], strided_buf.at[number, 1])
            put_rows(gates_ref, cols, short_sum(parts, None, taps_ref, 1, cols))

        each_tile(first // 128, strided_buf.shape[0], gate)
        start = 0
        for ref in (one_ref, two_ref):

            def recall(tile, _, ref=ref, start=start):
                for row in range(0, rows, 16):
                    value = ref[row : row + 16, tile_lanes(tile)]
                    put_halves(ahead_parts_buf, row // half, row % half, tile_lanes(tile, start), value)

            each_tile(ref.shape[1] // 128, 4, recall)
            start += ref.shape[1]
        forward_dots(forward_ref, ahead_parts_buf, ahead_spec_buf)
        each_tile(
            first // 128, 4,
            lambda tile, _: filtered(
                ahead_spec_buf, ahead_near_ref, ahead_bins_ref, tile_lanes(tile), tile_lanes(tile)
            ),
        )
        mix_tiles(mix, tiles, mixed_ref, strided_buf.at[:, 0])


def own_kernel(
    projected_ref, rims_ref, taps_ref, near_ref, last_near_ref, forward_ref, backward_ref, gates_ref, ahead_bins_ref,
    behind_ref, right_ref, bins_ref, base_ref, last_right_ref, mixed_ref,
    rims_buf, strided_buf, parts_buf, spec_buf, bins_buf, conv_buf, mixed_buf, sems,
):
    rows, width = right_ref.shape
    half = rows // 2
    middle = near_ref.shape[1]
    place = lax.axis_index("ctx")

    @pl.when(place == 0)
    def _():
        tiles = middle // 128
        behind = pltpu.make_async_copy(behind_ref, mixed_ref.at[:, pl.ds(middle, width - middle)], sems.at[0])
        behind.start()
        backward_dots(backward_ref, ahead_bins_ref, conv_buf)

        def mix(tile):
            cols = tile_lanes(tile)
            return [gates_ref[at : at + 16, cols] * conv_buf[at : at + 16, cols] for at in range(0, rows, 16)]

        mix_tiles(mix, tiles, mixed_buf, strided_buf.at[:, 0])
        ahead = pltpu.make_async_copy(mixed_buf, mixed_ref.at[:, pl.ds(0, middle)], sems.at[1])
        ahead.start()
        ahead.wait()
        behind.wait()

    @pl.when(place != 0)
    def _():
        read_rims(rims_ref, rims_buf)

        def drive(tile, number):
            cols = tile_lanes(tile)
            sums = [
                short_sum(
                    strided_rows(projected_ref[at, :, cols], strided_buf.at[number, at]),
                    rims_buf[at, :, cols], taps_ref, at, cols,
                )
                for at in range(3)
            ]
            put_rows(right_ref, cols, sums[1])
            driven_parts([one * two for one, two in zip(sums[0], sums[2])], parts_buf, cols)

        each_tile(width // 128, strided_buf.shape[0], drive)
        forward_dots(forward_ref, parts_buf, spec_buf)

        def keep(tile, _):
            cols = tile_lanes(tile)
            for row in range(0, half, 16):
                for at, value in enumerate(folded_products(spec_buf, near_ref, row, cols, cols)):
                    bins_ref[at * half + row : at * half + row + 16, cols] = value

        each_tile(middle // 128, 12, keep)
        behind = width - middle

        def finish(tile, _):
            there, cols = tile_lanes(tile, middle), tile_lanes(tile)
            for row in range(0, half, 16):
                put_bins(bins_buf, row, cols, folded_products(spec_buf, last_near_ref, row, there, cols))

        each_tile(behind // 128, 4, finish)
        backward_dots(backward_ref, bins_buf, base_ref)

        def reorder(tile, number):
            cols = tile_lanes(tile)
            base_ref[:, cols] = natural_tile(base_ref, cols, strided_buf.at[number, 0])
            last_right_ref[:, cols] = natural_tile(right_ref, tile_lanes(tile, middle), strided_buf.at[number, 1])

        each_tile(behind // 128, strided_buf.shape[0], reorder)


def mix_tiles(mix, tiles, mixed_ref, strided_buf):
    def one(tile, number):
        mixed_ref[:, tile_lanes(tile)] = natural_rows(mix(tile), strided_buf.at[number]).astype(jnp.bfloat16)

    each_tile(tiles, strided_buf.shape[0], one)


def read_levels(coded_ref, levels_buf, tiles, rows):
    levels_buf[...] = coded_ref[tiles * rows : tiles * rows + 16].astype(jnp.float32)


def join_kernel(
    coded_refs, far_ref, own_bins_ref, right_ref, forward_ref, backward_ref, mixed_ref,
    parts_buf, spec_buf, bins_buf, conv_buf, strided_buf, levels_buf,
):
    rows, width = conv_buf.shape
    half = rows // 2
    tiles = width // 128

    @pl.when(lax.axis_index("ctx") != 0)
    def _():
        counts = [coded_refs[0].shape[0] // rows, coded_refs[1].shape[0] // rows]
        counts[0] = tiles - counts[1]
        read_levels(coded_refs[1], levels_buf, counts[1], rows)
        for at, ref in enumerate(coded_refs):
            start = counts[0] * 128 * at
            levels_first = 0 if at else 16 - counts[0]

            def spread_out(tile, _, ref=ref, start=start, levels_first=levels_first):
                decode = decoder(levels_buf, levels_first + tile)
                for row in range(0, rows, 16):
                    value = decode(ref[tile_rows(tile, row), :])
                    put_halves(parts_buf, row // half, row % half, tile_lanes(tile, start), value)

            each_tile(counts[at], 4, spread_out)
        forward_dots(forward_ref, parts_buf, spec_buf)

        def add(tile, _):
            cols = tile_lanes(tile)
            for row in range(0, half, 16):
                products = [
                    value + own_bins_ref[at * half + row : at * half + row + 16, cols]
                    for at, value in enumerate(folded_products(spec_buf, far_ref, row, cols, cols))
                ]
                put_bins(bins_buf, row, cols, products)

        each_tile(tiles, 12, add)
        backward_dots(backward_ref, bins_buf, conv_buf)

        def mix(tile):
            cols = tile_lanes(tile)
            return [right_ref[at : at + 16, cols] * conv_buf[at : at + 16, cols] for at in range(0, rows, 16)]

        mix_tiles(mix, tiles, mixed_ref, strided_buf)


def last_kernel(
    first, coded_ref, base_ref, right_ref, ahead_ref, _, mixed_ref, buf, levels_buf, sems
):
    rows, width = base_ref.shape
    tiles = width // 128

    @pl.when(lax.axis_index("ctx") != 0)
    def _():
        ahead = pltpu.make_async_copy(ahead_ref, mixed_ref.at[:, pl.ds(0, first)], sems.at[0])
        ahead.start()
        read_levels(coded_ref, levels_buf, tiles, rows)

        def mix(tile, _):
            cols = tile_lanes(tile)
            decode = decoder(levels_buf, tile)
            for at in range(0, rows, 16):
                conv = decode(coded_ref[tile_rows(tile, at), :]) + base_ref[at : at + 16, cols]
                buf[at : at + 16, cols] = (right_ref[at : at + 16, cols] * conv).astype(jnp.bfloat16)

        each_tile(tiles, 4, mix)
        behind = pltpu.make_async_copy(buf, mixed_ref.at[:, pl.ds(first, width)], sems.at[1])
        behind.start()
        behind.wait()
        ahead.wait()


def params(mib=40):
    return pltpu.CompilerParams(vmem_limit_bytes=mib * 1024 * 1024)


def cost(us):
    return pl.CostEstimate(flops=int(us * 1e9), bytes_accessed=int(us * 3e6), transcendentals=0)


def one_way(
    projected, short_weight, pos_in, pos_bias, sine_freq, pos_mid, pos_out, decay_rate, skip_gain
):
    _, rows, width = projected.shape
    half = rows // 2
    total_len = 2 * rows
    ahead = [width // 8, width * 5 // 8]
    middle = sum(ahead)
    behind = width - middle
    forward, backward = odd_tables(rows)
    taps = jnp.transpose(short_weight, (1, 0, 2))
    in_vmem = pl.BlockSpec(memory_space=pltpu.VMEM)
    in_hbm = pl.BlockSpec(memory_space=pltpu.HBM)
    floats, shorts = functools.partial(pltpu.VMEM, dtype=jnp.float32), functools.partial(pltpu.VMEM, dtype=jnp.bfloat16)
    pairs = [(0, 1)]

    def arrays(*shapes, dtype=jnp.float32):
        return [jax.ShapeDtypeStruct(shape, dtype) for shape in shapes]

    def message(size, more=0):
        return arrays((size // 128 * rows + 16 + more, 128), dtype=jnp.bfloat16)

    order = parity_order(rows)
    places = np.concatenate([order, order + rows]).astype(np.float32)
    feats = feature_table(places, total_len)
    places = np.repeat(places[:, None], 128, 1)
    layers = (feats, pos_in, pos_bias[None, :], sine_freq[None, :], pos_mid)
    tile_bufs = [floats((2, 2, rows, 128)), floats((8, width)), floats((16, 128))]
    one, two = ahead
    one_code, one_driven, one_levels = pl.pallas_call(
        first_kernel,
        in_specs=[in_hbm] * 2,
        out_specs=[in_vmem] * 3,
        out_shape=arrays((one // 128 * rows + width // 128 * 18, 128), dtype=jnp.bfloat16)
        + arrays((rows, one), (16, 128)),
        scratch_shapes=[shorts((2, rows, one)), shorts((3, 16, width)), floats((3, TAPS, one))]
        + tile_bufs[:2]
        + [pltpu.SemaphoreType.DMA((4,))],
        compiler_params=params(),
        cost_estimate=cost(1),
        name="first",
    )(*[pltpu.with_memory_space_constraint(array, pltpu.HBM) for array in (projected, taps)])
    one_code = lax.ppermute(one_code, "ctx", [(0, 1), (1, 0)])
    weights = (pos_out, decay_rate[None, :], skip_gain[None, :], places, forward)
    hidden = pos_mid.shape[1]

    def spectra_bufs(size):
        return [floats((total_len, size)), shorts((2, rows, 2 * size)), floats((2, rows, 2 * size)), floats((8, size))]

    spectra = arrays((total_len, behind), (total_len, behind)) + arrays((total_len, 3 * hidden), dtype=jnp.bfloat16)
    two_code, two_driven = pl.pallas_call(
        functools.partial(encode_kernel, one),
        in_specs=[in_vmem] * 3,
        out_specs=[in_vmem] * 2,
        out_shape=message(two) + arrays((rows, two)),
        scratch_shapes=tile_bufs,
        compiler_params=params(),
        cost_estimate=cost(1),
        name="encode",
    )(projected, taps, one_levels)
    two_code = lax.ppermute(two_code, "ctx", [(0, 1), (1, 0)])
    last_near, last_far, second_halves = pl.pallas_call(
        functools.partial(network_filter_kernel, middle),
        in_specs=[in_vmem] * 10,
        out_specs=[in_vmem] * 3,
        out_shape=spectra,
        scratch_shapes=spectra_bufs(behind) + [floats((feats.shape[0], hidden))],
        compiler_params=params(),
        cost_estimate=cost(2),
        name="filter",
    )(*weights, *layers)
    near, far = pl.pallas_call(
        functools.partial(filter_spectra, 0),
        in_specs=[in_vmem] * 6,
        out_specs=[in_vmem] * 2,
        out_shape=arrays((total_len, middle), (total_len, middle)),
        scratch_shapes=spectra_bufs(middle),
        compiler_params=params(),
        cost_estimate=cost(2),
        name="filter",
    )(*weights, second_halves)
    last_near, near = lax.optimization_barrier((last_near, near))
    last_code, behind_mixed, gates, ahead_bins = pl.pallas_call(
        functools.partial(send_kernel, middle),
        in_specs=[in_vmem] * 9,
        out_specs=[in_vmem] * 4,
        out_shape=message(behind)
        + arrays((rows, behind), dtype=jnp.bfloat16)
        + arrays((rows, middle))
        + arrays((2, 2 * rows, middle), dtype=jnp.bfloat16),
        scratch_shapes=[
            floats((2, 3, rows, 128)),
            shorts((2, rows, behind)),
            floats((2, rows, behind)),
            shorts((2, 2 * rows, behind)),
            floats((rows, behind)),
            floats((rows, behind)),
            floats((8, behind)),
            floats((16, 128)),
            shorts((2, rows, middle)),
            floats((2, rows, middle)),
        ],
        compiler_params=params(),
        cost_estimate=cost(2),
        name="send",
    )(projected, taps, last_near, last_far, forward, backward, near, one_driven, two_driven)
    last_code = lax.ppermute(last_code, "ctx", pairs)
    right, own_bins, last_base, last_right, mixed = pl.pallas_call(
        own_kernel,
        in_specs=[in_vmem] * 10,
        out_specs=[in_vmem] * 4 + [in_hbm],
        out_shape=arrays((rows, width), (total_len, middle), (rows, behind), (rows, behind))
        + arrays((rows, width), dtype=jnp.bfloat16),
        scratch_shapes=[
            floats((3, 8, width)),
            floats((2, 3, rows, 128)),
            shorts((2, rows, width)),
            floats((2, rows, width)),
            shorts((2, 2 * rows, behind)),
            floats((rows, middle)),
            shorts((rows, middle)),
            pltpu.SemaphoreType.DMA((2,)),
        ],
        compiler_params=params(),
        cost_estimate=cost(4),
        name="own",
    )(projected, one_code, taps, near, last_near, forward, backward, gates, ahead_bins, behind_mixed)
    ahead_mixed = pl.pallas_call(
        lambda one_ref, two_ref, *refs: join_kernel((one_ref, two_ref), *refs),
        in_specs=[in_vmem] * 7,
        out_specs=in_vmem,
        out_shape=jax.ShapeDtypeStruct((rows, middle), jnp.bfloat16),
        scratch_shapes=[
            shorts((2, rows, middle)),
            floats((2, rows, middle)),
            shorts((2, 2 * rows, middle)),
            floats((rows, middle)),
            floats((4, rows, 128)),
            floats((16, 128)),
        ],
        compiler_params=params(),
        cost_estimate=cost(2),
        name="join",
    )(one_code, two_code, far, own_bins, right, forward, backward)
    return pl.pallas_call(
        functools.partial(last_kernel, middle),
        in_specs=[in_vmem] * 4 + [in_hbm],
        out_specs=in_hbm,
        out_shape=jax.ShapeDtypeStruct((rows, width), jnp.bfloat16),
        input_output_aliases={4: 0},
        scratch_shapes=[
            shorts((rows, behind)),
            floats((16, 128)),
            pltpu.SemaphoreType.DMA((2,)),
        ],
        compiler_params=params(),
        cost_estimate=cost(1),
        name="last",
    )(last_code, last_base, last_right, ahead_mixed, mixed)


def turn_table(outer_ids, inner_ids, modulus):
    product_grid = outer_ids[:, None] * inner_ids[None, :] % modulus
    angles = product_grid.astype(jnp.float32) * (2.0 * math.pi / modulus)
    return (jnp.cos(angles), jnp.sin(angles))


def section_outer(table, data):
    return jnp.einsum(
        "ka,cab->ckb", table, data, precision=HIGHEST, preferred_element_type=jnp.float32
    )


def section_inner(table, data):
    return jnp.einsum(
        "ckb,bj->ckj", data, table, precision=HIGHEST, preferred_element_type=jnp.float32
    )


def padded_spectrum(signal, outer_count, inner_count, tables):
    cos_half, sin_half, cos_twist, sin_twist, cos_inner, sin_inner = tables
    shaped = signal.reshape(signal.shape[0], outer_count // 2, inner_count)
    real_one = section_outer(cos_half, shaped)
    imag_one = -section_outer(sin_half, shaped)
    real_two = real_one * cos_twist + imag_one * sin_twist
    imag_two = imag_one * cos_twist - real_one * sin_twist
    spec_real = section_inner(cos_inner, real_two) + section_inner(sin_inner, imag_two)
    spec_imag = section_inner(cos_inner, imag_two) - section_inner(sin_inner, real_two)
    return (spec_real, spec_imag)


def causal_local(driven_cols, normed_cols, total_len):
    full_len = 2 * total_len
    inner_count = math.gcd(total_len, 128)
    outer_count = full_len // inner_count
    outer_full = jnp.arange(outer_count, dtype=jnp.int32)
    outer_half = jnp.arange(outer_count // 2, dtype=jnp.int32)
    inner_ids = jnp.arange(inner_count, dtype=jnp.int32)
    cos_half, sin_half = turn_table(outer_full, outer_half, outer_count)
    cos_twist, sin_twist = turn_table(outer_full, inner_ids, full_len)
    cos_inner, sin_inner = turn_table(inner_ids, inner_ids, inner_count)
    tables = (cos_half, sin_half, cos_twist, sin_twist, cos_inner, sin_inner)
    sig_real, sig_imag = padded_spectrum(driven_cols, outer_count, inner_count, tables)
    fil_real, fil_imag = padded_spectrum(normed_cols, outer_count, inner_count, tables)
    prod_real = sig_real * fil_real - sig_imag * fil_imag
    prod_imag = sig_real * fil_imag + sig_imag * fil_real
    back_real = section_inner(cos_inner, prod_real) - section_inner(sin_inner, prod_imag)
    back_imag = section_inner(sin_inner, prod_real) + section_inner(cos_inner, prod_imag)
    turned_real = back_real * cos_twist - back_imag * sin_twist
    turned_imag = back_real * sin_twist + back_imag * cos_twist
    cos_last, sin_last = turn_table(outer_half, outer_full, outer_count)
    result = (
        section_outer(cos_last, turned_real) - section_outer(sin_last, turned_imag)
    ) / full_len
    return result.reshape(driven_cols.shape[0], total_len)


def exchanged(
    projected, short_weight, pos_in, pos_bias, sine_freq, pos_mid, pos_out, decay_rate, skip_gain
):
    ctx_count = lax.axis_size("ctx")
    ctx_place = lax.axis_index("ctx")
    block_rows = projected.shape[1]
    total_len = block_rows * ctx_count
    rim_rows = shifted(projected[:, block_rows - (TAPS - 1) :, :], "ctx", 1)
    extended = jnp.concatenate([rim_rows, projected], axis=1)
    short_out = jnp.zeros(projected.shape, jnp.float32)
    for tap_index in range(TAPS):
        offset = TAPS - 1 - tap_index
        short_out = short_out + short_weight[tap_index][:, None, :] * extended[
            :, offset : offset + block_rows, :
        ].astype(jnp.float32)
    left_gate, right_gate, value_stream = (short_out[0], short_out[1], short_out[2])
    driven = left_gate * value_stream
    own_width = driven.shape[1] // ctx_count
    driven_cols = lax.all_to_all(driven.T, "ctx", split_axis=0, concat_axis=1, tiled=True)
    own_out = lax.dynamic_slice_in_dim(pos_out, ctx_place * own_width, own_width, 1)
    own_decay = lax.dynamic_slice_in_dim(decay_rate, ctx_place * own_width, own_width, 0)
    positions = jnp.arange(total_len, dtype=jnp.int32).astype(jnp.float32)
    long_filter = filter_rows(
        positions, total_len, pos_in, pos_bias, sine_freq, pos_mid, own_out, own_decay
    )
    normed = long_filter / jnp.sqrt(jnp.sum(long_filter * long_filter, axis=0) + 1e-05)
    conv_cols = causal_local(driven_cols, normed.T, total_len)
    long_conv = lax.all_to_all(conv_cols, "ctx", split_axis=1, concat_axis=0, tiled=True).T
    return (right_gate * (long_conv + skip_gain[None, :] * driven)).astype(jnp.bfloat16)


def body(projected, *others):
    _, rows, width = projected.shape
    laid_out = rows % 32 == 0 and 64 <= rows <= 128 and width in (1024, 2048)
    if lax.axis_size("ctx") == 2 and laid_out:
        return one_way(projected, *others)
    return exchanged(projected, *others)


def solution(mesh):
    placed = (
        P(None, ("dp", "ctx"), "chan"),
        P(None, None, "chan"),
        P(),
        P(),
        P(),
        P(),
        P(None, "chan"),
        P("chan"),
        P("chan"),
    )
    return jax.shard_map(
        body, mesh=mesh, in_specs=placed, out_specs=P(("dp", "ctx"), "chan"), check_vma=False
    )
```

```python
import functools
import math

import jax
import jax.numpy as jnp
import numpy as np
from jax import lax
from jax.experimental import pallas as pl
from jax.experimental.pallas import tpu as pltpu
from jax.sharding import PartitionSpec as P

BANDS = 16
TAPS = 7
SPAN = 250.0
TINY = 1e-30

HIGHEST = lax.Precision.HIGHEST


def shifted(x, axis, by):
    size = lax.axis_size(axis)
    pairs = [(i, i + by) for i in range(size) if 0 <= i + by < size]
    return lax.ppermute(x, axis, pairs)


def features(positions, total_len):
    band_ids = jnp.arange(1, BANDS + 1, dtype=jnp.float32)
    angles = positions[:, None] * band_ids[None, :] * (2.0 * math.pi / total_len)
    return jnp.concatenate(
        [positions[:, None] / total_len, jnp.cos(angles), jnp.sin(angles)], axis=1
    )


def second_rows(positions, total_len, pos_in, pos_bias, sine_freq, pos_mid):
    inputs = features(positions, total_len)
    first_layer = jnp.sin(
        sine_freq
        * (
            jnp.dot(inputs, pos_in, precision=HIGHEST, preferred_element_type=jnp.float32)
            + pos_bias
        )
    )
    return jnp.sin(
        sine_freq
        * jnp.dot(first_layer, pos_mid, precision=HIGHEST, preferred_element_type=jnp.float32)
    )


def filter_rows(positions, total_len, pos_in, pos_bias, sine_freq, pos_mid, pos_out, decay_rate):
    second_layer = second_rows(positions, total_len, pos_in, pos_bias, sine_freq, pos_mid)
    raw_filter = jnp.dot(
        second_layer, pos_out, precision=HIGHEST, preferred_element_type=jnp.float32
    )
    return raw_filter * jnp.exp(-decay_rate[None, :] * positions[:, None])


def halves(x):
    high = x.astype(jnp.bfloat16)
    low = (x - high.astype(jnp.float32)).astype(jnp.bfloat16)
    return high, low


def feature_table(places, total_len):
    bands = np.arange(1, BANDS + 1, dtype=np.float32)
    angles = places[:, None] * bands[None, :] * np.float32(2.0 * math.pi / total_len)
    first = places[:, None] / np.float32(total_len)
    table = np.concatenate([first, np.cos(angles), np.sin(angles), np.ones_like(first)], axis=1)
    spare = np.zeros((places.shape[0], -table.shape[1] % 8))
    return np.concatenate([table, spare], axis=1).astype(np.float32).T.copy()


def parity_order(rows):
    place = np.arange(rows)
    parity, inner = place // (rows // 2), place % (rows // 2)
    return rows // 8 * (inner % 8) + inner // 8 * 2 + parity


def table_columns(table):
    high = table.astype(jnp.bfloat16)
    low = (table - high.astype(np.float32)).astype(jnp.bfloat16)
    return np.concatenate([high, high, low], axis=1)


def odd_tables(rows):
    half = rows // 2
    order = np.concatenate([np.arange(0, half, 2), np.arange(1, half, 2)])
    turns = (2 * order[:, None] + 1) * parity_order(rows)[None, :] % (4 * rows)
    angles = turns * (np.pi / (2 * rows))
    forward = np.concatenate([np.cos(angles), -np.sin(angles)], axis=0).astype(np.float32)
    pieces = [forward[:, :half], forward[:, half:]]
    return (
        np.concatenate([table_columns(piece) for piece in pieces], axis=0),
        np.concatenate([table_columns(piece.T / np.float32(rows)) for piece in pieces], axis=0),
    )


def each_tile(tiles, unroll, action):
    count = math.gcd(tiles, unroll)

    def step(at, _):
        for number in range(count):
            action(at * count + number, number)
        return 0

    if tiles == count:
        step(0, 0)
    else:
        lax.fori_loop(0, tiles // count, step, 0)


def put_halves(ref, parity, row, cols, value):
    size = ref.shape[1] // 2
    high, low = halves(value)
    count = value.shape[0]
    ref[parity, row : row + count, cols] = high
    ref[parity, size + row : size + row + count, cols] = low


def three_pass(table, ref, parity):
    size = ref.shape[1] // 2
    both = jnp.concatenate([ref[parity], ref[parity, :size]], axis=0)
    return jnp.dot(table, both, preferred_element_type=jnp.float32)


def forward_dots(forward_ref, parts_ref, spec_ref):
    rows = spec_ref.shape[1]
    for parity in range(2):
        spec_ref[parity] = three_pass(forward_ref[parity * rows : (parity + 1) * rows], parts_ref, parity)


def backward_dots(backward_ref, bins_ref, conv_ref):
    half = conv_ref.shape[0] // 2
    for parity in range(2):
        rows = slice(parity * half, (parity + 1) * half)
        conv_ref[rows] = three_pass(backward_ref[rows], bins_ref, parity)


def unfolded(spec_ref, row, cols):
    half = spec_ref.shape[1] // 2
    even_cos, odd_cos = spec_ref[0, row : row + 16, cols], spec_ref[1, row : row + 16, cols]
    sine = slice(half + row, half + row + 16)
    even_sin, odd_sin = spec_ref[0, sine, cols], spec_ref[1, sine, cols]
    return even_cos + odd_cos, even_sin + odd_sin, even_cos - odd_cos, odd_sin - even_sin


def folded_products(spec_ref, filter_ref, row, cols, filter_cols):
    half = spec_ref.shape[1] // 2
    real, imag, real_far, imag_far = unfolded(spec_ref, row, cols)
    taps = [filter_ref[at * half + row : at * half + row + 16, filter_cols] for at in range(4)]
    out_real, out_imag = real * taps[0] - imag * taps[1], real * taps[1] + imag * taps[0]
    far_real = real_far * taps[2] - imag_far * taps[3]
    far_imag = real_far * taps[3] + imag_far * taps[2]
    return out_real + far_real, out_imag - far_imag, out_real - far_real, out_imag + far_imag


def put_bins(bins_ref, row, cols, products):
    half = bins_ref.shape[1] // 4
    for at, value in enumerate(products):
        put_halves(bins_ref, at // 2, at % 2 * half + row, cols, value)


def filtered(spec_ref, filter_ref, bins_ref, cols, filter_cols):
    for row in range(0, spec_ref.shape[1] // 2, 16):
        put_bins(bins_ref, row, cols, folded_products(spec_ref, filter_ref, row, cols, filter_cols))


def strided_rows(values, buf):
    buf[...] = values.astype(jnp.float32)
    count = buf.shape[0] // 8
    return [buf[pl.ds(v, 8, stride=count), :] for v in range(count)]


def short_sum(parts, rim, taps_ref, at, cols):
    top = lax.broadcasted_iota(jnp.int32, (8, 128), 0) == 0
    before = {}
    for back in range(1, TAPS):
        edge = 0.0 if rim is None else rim[8 - back : 9 - back]
        before[-back] = jnp.where(top, edge, pltpu.roll(parts[-back], 1, 0))
    taps = [jnp.broadcast_to(taps_ref[at, k : k + 1, cols], (8, 128)) for k in range(TAPS)]
    sums = []
    for v in range(len(parts)):
        terms = [taps[k] * (parts[v - k] if v >= k else before[v - k]) for k in range(TAPS)]
        sums.append(((terms[0] + terms[1]) + (terms[2] + terms[3])) + ((terms[4] + terms[5]) + terms[6]))
    return sums


def parity_rows(parts):
    ordered = parts[0::2] + parts[1::2]
    return [jnp.concatenate(ordered[i : i + 2], axis=0) for i in range(0, len(ordered), 2)]


def natural_rows(ref_rows, buf):
    count = buf.shape[0] // 8
    for at, value in enumerate(ref_rows):
        for piece in range(2):
            number = 2 * at + piece
            v = number % (count // 2) * 2 + number // (count // 2)
            buf[pl.ds(v, 8, stride=count), :] = value[8 * piece : 8 * piece + 8]
    return buf[...]


def tile_lanes(tile, first=0):
    return pl.ds(pl.multiple_of(first + tile * 128, 128), 128)


def tile_rows(tile, row, count=16):
    return pl.ds(pl.multiple_of(tile * 128 + row, 16), count)


def natural_tile(ref, cols, buf):
    return natural_rows([ref[at : at + 16, cols] for at in range(0, ref.shape[0], 16)], buf)


def place_level(peak, tile, peak_buf, levels_buf, levels_first):
    for step in (1, 2, 4):
        peak = jnp.maximum(peak, pltpu.roll(peak, step, 0))
    level = jnp.maximum(peak, TINY)
    wide = level * 65537.0
    level = wide - (wide - level)
    peak_buf[:, tile_lanes(tile)] = SPAN / level
    levels_buf[pl.ds(levels_first + tile, 1), :] = level[0:1]


def put_coded(coded_ref, tile, row, value, gain):
    coded = jnp.exp2(jnp.abs(value) * gain - SPAN / 2)
    coded_ref[tile_rows(tile, row), :] = jnp.where(value < 0, -coded, coded).astype(jnp.bfloat16)


def decoder(levels_buf, tile):
    level = levels_buf[pl.ds(tile, 1), :]
    slope = jnp.broadcast_to(level * (1.0 / (math.log(2.0) * SPAN)), (16, 128))
    middle = jnp.broadcast_to(level / 2, (16, 128))

    def decode(coded):
        coded = coded.astype(jnp.float32)
        size = jnp.log(jnp.abs(coded)) * slope + middle
        return jnp.where(coded < 0, -size, size)

    return decode


def second_layer(feats_ref, in_ref, bias_ref, freq_ref, mid_ref, scaled_buf):
    dot = functools.partial(
        lax.dot_general,
        dimension_numbers=(((0,), (0,)), ((), ())),
        precision=HIGHEST,
        preferred_element_type=jnp.float32,
    )
    count = in_ref.shape[0]
    freq = freq_ref[...]
    scaled_buf[...] = jnp.zeros_like(scaled_buf)
    scaled_buf[0:count] = in_ref[...] * freq
    scaled_buf[count : count + 1] = bias_ref[...] * freq
    layer = jnp.sin(dot(scaled_buf[...], feats_ref[...]))
    return jnp.sin(dot(mid_ref[...] * freq, layer)).T


def encode_tiles(
    tiles, rows, streams, taps_ref, taps_first, coded_ref, driven_ref, strided_buf, peak_buf, levels_buf, levels_first=0
):
    def drive(tile, number):
        cols = tile_lanes(tile)
        sums = [
            short_sum(
                strided_rows(streams(way, tile), strided_buf.at[number, way]),
                None, taps_ref, 2 * way, tile_lanes(tile, taps_first),
            )
            for way in range(2)
        ]
        driven = [one * two for one, two in zip(*sums)]
        for row, value in enumerate(parity_rows(driven)):
            driven_ref[16 * row : 16 * row + 16, cols] = value
        peak_buf[:, cols] = functools.reduce(jnp.maximum, [jnp.abs(value) for value in driven])

    each_tile(tiles, strided_buf.shape[0], drive)
    code_tiles(tiles, rows, coded_ref, driven_ref, peak_buf, levels_buf, levels_first)


def code_tiles(tiles, rows, coded_ref, values_ref, peak_buf, levels_buf, levels_first=0):
    each_tile(
        tiles, 4,
        lambda tile, _: place_level(peak_buf[:, tile_lanes(tile)], tile, peak_buf, levels_buf, levels_first),
    )
    if levels_first == 0:
        coded_ref[tiles * rows : tiles * rows + 16] = levels_buf[...].astype(jnp.bfloat16)

    def code(tile, _):
        cols = tile_lanes(tile)
        gain = peak_buf[:, cols]
        gain = jnp.concatenate([gain, gain], axis=0)
        for row in range(0, rows, 16):
            put_coded(coded_ref, tile, row, values_ref[row : row + 16, cols], gain)

    each_tile(tiles, 4, code)


def first_kernel(
    projected_ref, taps_ref, coded_ref, driven_ref, levels_ref, rows_buf, rim_buf, taps_buf, strided_buf, peak_buf, sems
):
    rows, size = rows_buf.shape[1:]
    tiles = size // 128

    @pl.when(lax.axis_index("ctx") == 0)
    def _():
        span = pl.ds(0, size)
        copies = [
            pltpu.make_async_copy(taps_ref.at[:, :, span], taps_buf, sems.at[0]),
            pltpu.make_async_copy(projected_ref.at[0, :, span], rows_buf.at[0], sems.at[1]),
            pltpu.make_async_copy(projected_ref.at[2, :, span], rows_buf.at[1], sems.at[2]),
            pltpu.make_async_copy(projected_ref.at[:, pl.ds(rows - 16, 16)], rim_buf, sems.at[3]),
        ]
        for copy in copies:
            copy.start()
        for copy in copies[:3]:
            copy.wait()
        levels_ref[...] = jnp.zeros_like(levels_ref)
        encode_tiles(
            tiles, rows, lambda way, tile: rows_buf[way, :, tile_lanes(tile)], taps_buf, 0, coded_ref, driven_ref,
            strided_buf, peak_buf, levels_ref, 16 - tiles,
        )
        copies[3].wait()
        for at in range(3):
            for group in range(rim_buf.shape[2] // 1024):
                there = tiles * rows + (3 * group + at) * 48
                values = [
                    rim_buf[at, :, (8 * group + way) * 128 : (8 * group + way + 1) * 128].astype(jnp.float32)[8:]
                    for way in range(8)
                ]
                values = pack_rims(values)
                for pair in range(3):
                    both = jnp.concatenate(values[2 * pair : 2 * pair + 2], axis=0)
                    coded_ref[there + 16 * pair : there + 16 * pair + 16] = both.astype(jnp.bfloat16)


def pack_rims(values):
    top = lax.broadcasted_iota(jnp.int32, (8, 128), 0) < 2
    return [
        jnp.where(top, pltpu.roll(values[6 + at // 3], 6 - 2 * (at % 3), 0), values[at]) for at in range(6)
    ]


def unpack_rims(values):
    place = lax.broadcasted_iota(jnp.int32, (8, 128), 0)
    rest = []
    for at in range(2):
        turned = [pltpu.roll(values[3 * at + way], 2 + 2 * way, 0) for way in range(3)]
        rest.append(jnp.where(place < 4, turned[0], jnp.where(place < 6, turned[1], turned[2])))
    return values + rest


def read_rims(coded_ref, rims_buf):
    groups = rims_buf.shape[2] // 1024
    start = coded_ref.shape[0] - groups * 144
    for at in range(3):
        for group in range(groups):
            there = start + (3 * group + at) * 48
            packed = coded_ref[there : there + 48].astype(jnp.float32)
            values = unpack_rims([packed[8 * way : 8 * way + 8] for way in range(6)])
            for way, value in enumerate(values):
                rims_buf[at, :, (8 * group + way) * 128 : (8 * group + way + 1) * 128] = value


def encode_kernel(
    first, projected_ref, taps_ref, one_levels_ref, coded_ref, driven_ref, strided_buf, peak_buf, levels_buf
):
    rows, size = driven_ref.shape

    @pl.when(lax.axis_index("ctx") == 0)
    def _():
        levels_buf[...] = one_levels_ref[...]
        encode_tiles(
            size // 128, rows, lambda way, tile: projected_ref[2 * way, :, tile_lanes(tile, first)], taps_ref, first,
            coded_ref, driven_ref, strided_buf, peak_buf, levels_buf,
        )


def network_halves(layer_refs, halves_ref, scaled_buf):
    second_high, second_low = halves(second_layer(*layer_refs, scaled_buf))
    halves_ref[...] = jnp.concatenate([second_high, second_high, second_low], axis=1)


def network_filter_kernel(first, *refs):
    weight_refs, layer_refs, (near_ref, far_ref, halves_ref), bufs = refs[:5], refs[5:10], refs[10:13], refs[13:]
    network_halves(layer_refs, halves_ref, bufs[-1])
    filter_spectra(first, *weight_refs, halves_ref, near_ref, far_ref, *bufs[:-1])


def filter_spectra(
    first, out_ref, decay_ref, skip_ref, places_ref, forward_ref, halves_ref, near_ref, far_ref,
    raw_buf, parts_buf, spec_buf, scale_buf,
):
    rows, width = near_ref.shape[0] // 2, near_ref.shape[1]
    half = rows // 2
    out_high, out_low = halves(out_ref[:, first : first + width])
    raw_buf[...] = jnp.dot(
        halves_ref[...], jnp.concatenate([out_high, out_low, out_high], axis=0), preferred_element_type=jnp.float32
    )

    def decay(tile, _):
        cols = tile_lanes(tile)
        fall = -decay_ref[:, tile_lanes(tile, first)]
        total = jnp.zeros((8, 128), jnp.float32)
        for row in range(0, 2 * rows, 16):
            taps = raw_buf[row : row + 16, cols] * jnp.exp(fall * places_ref[row : row + 16])
            total = total + (taps[:8] * taps[:8] + taps[8:] * taps[8:])
            parity = row % rows // half
            put_halves(parts_buf, parity, row % half, tile_lanes(tile, row // rows * width), taps)
        for step in (1, 2, 4):
            total = total + pltpu.roll(total, step, 0)
        scale_buf[:, cols] = 1.0 / jnp.sqrt(total + 1e-05)

    each_tile(width // 128, 12, decay)
    forward_dots(forward_ref, parts_buf, spec_buf)

    def shape(tile, _):
        cols = tile_lanes(tile)
        scale = scale_buf[:, cols]
        scale = jnp.concatenate([scale, scale], axis=0)
        skip = skip_ref[:, tile_lanes(tile, first)]
        for row in range(0, half, 16):
            low = [value * scale for value in unfolded(spec_buf, row, cols)]
            high = [value * scale for value in unfolded(spec_buf, row, tile_lanes(tile, width))]
            sign = 1 if row < half // 2 else -1
            turned = [-sign * low[1], sign * low[0], sign * low[3], -sign * low[2]]
            low = [low[0] + skip, low[1], low[2] + skip, low[3]]
            for at in range(4):
                near_ref[at * half + row : at * half + row + 16, cols] = low[at]
                far_ref[at * half + row : at * half + row + 16, cols] = high[at] + turned[at]

    each_tile(width // 128, 12, shape)


def driven_parts(driven, parts_buf, cols):
    half = parts_buf.shape[1] // 2
    for at, value in enumerate(parity_rows(driven)):
        put_halves(parts_buf, 16 * at // half, 16 * at % half, cols, value)


def put_rows(ref, cols, values):
    for at, value in enumerate(parity_rows(values)):
        ref[16 * at : 16 * at + 16, cols] = value


def send_kernel(
    first, projected_ref, taps_ref, near_ref, far_ref, forward_ref, backward_ref, ahead_near_ref, one_ref, two_ref,
    coded_ref, mixed_ref, gates_ref, ahead_bins_ref,
    strided_buf, parts_buf, spec_buf, bins_buf, right_buf, conv_buf, peak_buf, levels_buf, ahead_parts_buf,
    ahead_spec_buf,
):
    rows, width = right_buf.shape
    half = rows // 2
    tiles = width // 128

    @pl.when(lax.axis_index("ctx") == 0)
    def _():
        def drive(tile, number):
            cols = tile_lanes(tile, first)
            sums = [
                short_sum(
                    strided_rows(projected_ref[at, :, cols], strided_buf.at[number, at]), None, taps_ref, at, cols
                )
                for at in range(3)
            ]
            put_rows(right_buf, tile_lanes(tile), sums[1])
            driven_parts([one * two for one, two in zip(sums[0], sums[2])], parts_buf, tile_lanes(tile))

        each_tile(tiles, strided_buf.shape[0], drive)
        forward_dots(forward_ref, parts_buf, spec_buf)
        each_tile(
            tiles, 4, lambda tile, _: filtered(spec_buf, far_ref, bins_buf, tile_lanes(tile), tile_lanes(tile))
        )
        backward_dots(backward_ref, bins_buf, conv_buf)

        def peaks(tile, number):
            cols = tile_lanes(tile)
            conv_buf[:, cols] = natural_tile(conv_buf, cols, strided_buf.at[number, 0])
            peak_buf[:, cols] = functools.reduce(
                jnp.maximum, [jnp.abs(conv_buf[row : row + 8, cols]) for row in range(0, rows, 8)]
            )

        each_tile(tiles, strided_buf.shape[0], peaks)
        code_tiles(tiles, rows, coded_ref, conv_buf, peak_buf, levels_buf)
        each_tile(
            tiles, 4, lambda tile, _: filtered(spec_buf, near_ref, bins_buf, tile_lanes(tile), tile_lanes(tile))
        )
        backward_dots(backward_ref, bins_buf, conv_buf)

        def mix(tile):
            cols = tile_lanes(tile)
            return [right_buf[at : at + 16, cols] * conv_buf[at : at + 16, cols] for at in range(0, rows, 16)]

        def gate(tile, number):
            cols = tile_lanes(tile)
            parts = strided_rows(projected_ref[1, :, cols], strided_buf.at[number, 1])
            put_rows(gates_ref, cols, short_sum(parts, None, taps_ref, 1, cols))

        each_tile(first // 128, strided_buf.shape[0], gate)
        start = 0
        for ref in (one_ref, two_ref):

            def recall(tile, _, ref=ref, start=start):
                for row in range(0, rows, 16):
                    value = ref[row : row + 16, tile_lanes(tile)]
                    put_halves(ahead_parts_buf, row // half, row % half, tile_lanes(tile, start), value)

            each_tile(ref.shape[1] // 128, 4, recall)
            start += ref.shape[1]
        forward_dots(forward_ref, ahead_parts_buf, ahead_spec_buf)
        each_tile(
            first // 128, 4,
            lambda tile, _: filtered(
                ahead_spec_buf, ahead_near_ref, ahead_bins_ref, tile_lanes(tile), tile_lanes(tile)
            ),
        )
        mix_tiles(mix, tiles, mixed_ref, strided_buf.at[:, 0])


def own_kernel(
    projected_ref, rims_ref, taps_ref, near_ref, last_near_ref, forward_ref, backward_ref, gates_ref, ahead_bins_ref,
    behind_ref, right_ref, bins_ref, base_ref, last_right_ref, mixed_ref,
    rims_buf, strided_buf, parts_buf, spec_buf, bins_buf, conv_buf, mixed_buf, sems,
):
    rows, width = right_ref.shape
    half = rows // 2
    middle = near_ref.shape[1]
    place = lax.axis_index("ctx")

    @pl.when(place == 0)
    def _():
        tiles = middle // 128
        behind = pltpu.make_async_copy(behind_ref, mixed_ref.at[:, pl.ds(middle, width - middle)], sems.at[0])
        behind.start()
        backward_dots(backward_ref, ahead_bins_ref, conv_buf)

        def mix(tile):
            cols = tile_lanes(tile)
            return [gates_ref[at : at + 16, cols] * conv_buf[at : at + 16, cols] for at in range(0, rows, 16)]

        mix_tiles(mix, tiles, mixed_buf, strided_buf.at[:, 0])
        ahead = pltpu.make_async_copy(mixed_buf, mixed_ref.at[:, pl.ds(0, middle)], sems.at[1])
        ahead.start()
        ahead.wait()
        behind.wait()

    @pl.when(place != 0)
    def _():
        read_rims(rims_ref, rims_buf)

        def drive(tile, number):
            cols = tile_lanes(tile)
            sums = [
                short_sum(
                    strided_rows(projected_ref[at, :, cols], strided_buf.at[number, at]),
                    rims_buf[at, :, cols], taps_ref, at, cols,
                )
                for at in range(3)
            ]
            put_rows(right_ref, cols, sums[1])
            driven_parts([one * two for one, two in zip(sums[0], sums[2])], parts_buf, cols)

        each_tile(width // 128, strided_buf.shape[0], drive)
        forward_dots(forward_ref, parts_buf, spec_buf)

        def keep(tile, _):
            cols = tile_lanes(tile)
            for row in range(0, half, 16):
                for at, value in enumerate(folded_products(spec_buf, near_ref, row, cols, cols)):
                    bins_ref[at * half + row : at * half + row + 16, cols] = value

        each_tile(middle // 128, 12, keep)
        behind = width - middle

        def finish(tile, _):
            there, cols = tile_lanes(tile, middle), tile_lanes(tile)
            for row in range(0, half, 16):
                put_bins(bins_buf, row, cols, folded_products(spec_buf, last_near_ref, row, there, cols))

        each_tile(behind // 128, 4, finish)
        backward_dots(backward_ref, bins_buf, base_ref)

        def reorder(tile, number):
            cols = tile_lanes(tile)
            base_ref[:, cols] = natural_tile(base_ref, cols, strided_buf.at[number, 0])
            last_right_ref[:, cols] = natural_tile(right_ref, tile_lanes(tile, middle), strided_buf.at[number, 1])

        each_tile(behind // 128, strided_buf.shape[0], reorder)


def mix_tiles(mix, tiles, mixed_ref, strided_buf):
    def one(tile, number):
        mixed_ref[:, tile_lanes(tile)] = natural_rows(mix(tile), strided_buf.at[number]).astype(jnp.bfloat16)

    each_tile(tiles, strided_buf.shape[0], one)


def read_levels(coded_ref, levels_buf, tiles, rows):
    levels_buf[...] = coded_ref[tiles * rows : tiles * rows + 16].astype(jnp.float32)


def join_kernel(
    coded_refs, far_ref, own_bins_ref, right_ref, forward_ref, backward_ref, mixed_ref,
    parts_buf, spec_buf, bins_buf, conv_buf, strided_buf, levels_buf,
):
    rows, width = conv_buf.shape
    half = rows // 2
    tiles = width // 128

    @pl.when(lax.axis_index("ctx") != 0)
    def _():
        counts = [coded_refs[0].shape[0] // rows, coded_refs[1].shape[0] // rows]
        counts[0] = tiles - counts[1]
        read_levels(coded_refs[1], levels_buf, counts[1], rows)
        for at, ref in enumerate(coded_refs):
            start = counts[0] * 128 * at
            levels_first = 0 if at else 16 - counts[0]

            def spread_out(tile, _, ref=ref, start=start, levels_first=levels_first):
                decode = decoder(levels_buf, levels_first + tile)
                for row in range(0, rows, 16):
                    value = decode(ref[tile_rows(tile, row), :])
                    put_halves(parts_buf, row // half, row % half, tile_lanes(tile, start), value)

            each_tile(counts[at], 4, spread_out)
        forward_dots(forward_ref, parts_buf, spec_buf)

        def add(tile, _):
            cols = tile_lanes(tile)
            for row in range(0, half, 16):
                products = [
                    value + own_bins_ref[at * half + row : at * half + row + 16, cols]
                    for at, value in enumerate(folded_products(spec_buf, far_ref, row, cols, cols))
                ]
                put_bins(bins_buf, row, cols, products)

        each_tile(tiles, 12, add)
        backward_dots(backward_ref, bins_buf, conv_buf)

        def mix(tile):
            cols = tile_lanes(tile)
            return [right_ref[at : at + 16, cols] * conv_buf[at : at + 16, cols] for at in range(0, rows, 16)]

        mix_tiles(mix, tiles, mixed_ref, strided_buf)


def last_kernel(
    first, coded_ref, base_ref, right_ref, ahead_ref, _, mixed_ref, buf, levels_buf, sems
):
    rows, width = base_ref.shape
    tiles = width // 128

    @pl.when(lax.axis_index("ctx") != 0)
    def _():
        ahead = pltpu.make_async_copy(ahead_ref, mixed_ref.at[:, pl.ds(0, first)], sems.at[0])
        ahead.start()
        read_levels(coded_ref, levels_buf, tiles, rows)

        def mix(tile, _):
            cols = tile_lanes(tile)
            decode = decoder(levels_buf, tile)
            for at in range(0, rows, 16):
                conv = decode(coded_ref[tile_rows(tile, at), :]) + base_ref[at : at + 16, cols]
                buf[at : at + 16, cols] = (right_ref[at : at + 16, cols] * conv).astype(jnp.bfloat16)

        each_tile(tiles, 4, mix)
        behind = pltpu.make_async_copy(buf, mixed_ref.at[:, pl.ds(first, width)], sems.at[1])
        behind.start()
        behind.wait()
        ahead.wait()


def params(mib=40):
    return pltpu.CompilerParams(vmem_limit_bytes=mib * 1024 * 1024)


def cost(us):
    return pl.CostEstimate(flops=int(us * 1e9), bytes_accessed=int(us * 3e6), transcendentals=0)


def one_way(
    projected, short_weight, pos_in, pos_bias, sine_freq, pos_mid, pos_out, decay_rate, skip_gain
):
    _, rows, width = projected.shape
    half = rows // 2
    total_len = 2 * rows
    ahead = [width // 16, width * 11 // 16]
    middle = sum(ahead)
    behind = width - middle
    forward, backward = odd_tables(rows)
    taps = jnp.transpose(short_weight, (1, 0, 2))
    in_vmem = pl.BlockSpec(memory_space=pltpu.VMEM)
    in_hbm = pl.BlockSpec(memory_space=pltpu.HBM)
    floats, shorts = functools.partial(pltpu.VMEM, dtype=jnp.float32), functools.partial(pltpu.VMEM, dtype=jnp.bfloat16)
    pairs = [(0, 1)]

    def arrays(*shapes, dtype=jnp.float32):
        return [jax.ShapeDtypeStruct(shape, dtype) for shape in shapes]

    def message(size, more=0):
        return arrays((size // 128 * rows + 16 + more, 128), dtype=jnp.bfloat16)

    order = parity_order(rows)
    places = np.concatenate([order, order + rows]).astype(np.float32)
    feats = feature_table(places, total_len)
    places = np.repeat(places[:, None], 128, 1)
    layers = (feats, pos_in, pos_bias[None, :], sine_freq[None, :], pos_mid)
    tile_bufs = [floats((2, 2, rows, 128)), floats((8, width)), floats((16, 128))]
    one, two = ahead
    one_code, one_driven, one_levels = pl.pallas_call(
        first_kernel,
        in_specs=[in_hbm] * 2,
        out_specs=[in_vmem] * 3,
        out_shape=arrays((one // 128 * rows + width // 128 * 18, 128), dtype=jnp.bfloat16)
        + arrays((rows, one), (16, 128)),
        scratch_shapes=[shorts((2, rows, one)), shorts((3, 16, width)), floats((3, TAPS, one))]
        + tile_bufs[:2]
        + [pltpu.SemaphoreType.DMA((4,))],
        compiler_params=params(),
        cost_estimate=cost(1),
        name="first",
    )(*[pltpu.with_memory_space_constraint(array, pltpu.HBM) for array in (projected, taps)])
    one_code = lax.ppermute(one_code, "ctx", [(0, 1), (1, 0)])
    weights = (pos_out, decay_rate[None, :], skip_gain[None, :], places, forward)
    hidden = pos_mid.shape[1]

    def spectra_bufs(size):
        return [floats((total_len, size)), shorts((2, rows, 2 * size)), floats((2, rows, 2 * size)), floats((8, size))]

    spectra = arrays((total_len, behind), (total_len, behind)) + arrays((total_len, 3 * hidden), dtype=jnp.bfloat16)
    two_code, two_driven = pl.pallas_call(
        functools.partial(encode_kernel, one),
        in_specs=[in_vmem] * 3,
        out_specs=[in_vmem] * 2,
        out_shape=message(two) + arrays((rows, two)),
        scratch_shapes=tile_bufs,
        compiler_params=params(),
        cost_estimate=cost(1),
        name="encode",
    )(projected, taps, one_levels)
    two_code = lax.ppermute(two_code, "ctx", [(0, 1), (1, 0)])
    last_near, last_far, second_halves = pl.pallas_call(
        functools.partial(network_filter_kernel, middle),
        in_specs=[in_vmem] * 10,
        out_specs=[in_vmem] * 3,
        out_shape=spectra,
        scratch_shapes=spectra_bufs(behind) + [floats((feats.shape[0], hidden))],
        compiler_params=params(),
        cost_estimate=cost(2),
        name="filter",
    )(*weights, *layers)
    near, far = pl.pallas_call(
        functools.partial(filter_spectra, 0),
        in_specs=[in_vmem] * 6,
        out_specs=[in_vmem] * 2,
        out_shape=arrays((total_len, middle), (total_len, middle)),
        scratch_shapes=spectra_bufs(middle),
        compiler_params=params(),
        cost_estimate=cost(2),
        name="filter",
    )(*weights, second_halves)
    last_near, near = lax.optimization_barrier((last_near, near))
    last_code, behind_mixed, gates, ahead_bins = pl.pallas_call(
        functools.partial(send_kernel, middle),
        in_specs=[in_vmem] * 9,
        out_specs=[in_vmem] * 4,
        out_shape=message(behind)
        + arrays((rows, behind), dtype=jnp.bfloat16)
        + arrays((rows, middle))
        + arrays((2, 2 * rows, middle), dtype=jnp.bfloat16),
        scratch_shapes=[
            floats((2, 3, rows, 128)),
            shorts((2, rows, behind)),
            floats((2, rows, behind)),
            shorts((2, 2 * rows, behind)),
            floats((rows, behind)),
            floats((rows, behind)),
            floats((8, behind)),
            floats((16, 128)),
            shorts((2, rows, middle)),
            floats((2, rows, middle)),
        ],
        compiler_params=params(),
        cost_estimate=cost(2),
        name="send",
    )(projected, taps, last_near, last_far, forward, backward, near, one_driven, two_driven)
    last_code = lax.ppermute(last_code, "ctx", pairs)
    right, own_bins, last_base, last_right, mixed = pl.pallas_call(
        own_kernel,
        in_specs=[in_vmem] * 10,
        out_specs=[in_vmem] * 4 + [in_hbm],
        out_shape=arrays((rows, width), (total_len, middle), (rows, behind), (rows, behind))
        + arrays((rows, width), dtype=jnp.bfloat16),
        scratch_shapes=[
            floats((3, 8, width)),
            floats((2, 3, rows, 128)),
            shorts((2, rows, width)),
            floats((2, rows, width)),
            shorts((2, 2 * rows, behind)),
            floats((rows, middle)),
            shorts((rows, middle)),
            pltpu.SemaphoreType.DMA((2,)),
        ],
        compiler_params=params(),
        cost_estimate=cost(4),
        name="own",
    )(projected, one_code, taps, near, last_near, forward, backward, gates, ahead_bins, behind_mixed)
    ahead_mixed = pl.pallas_call(
        lambda one_ref, two_ref, *refs: join_kernel((one_ref, two_ref), *refs),
        in_specs=[in_vmem] * 7,
        out_specs=in_vmem,
        out_shape=jax.ShapeDtypeStruct((rows, middle), jnp.bfloat16),
        scratch_shapes=[
            shorts((2, rows, middle)),
            floats((2, rows, middle)),
            shorts((2, 2 * rows, middle)),
            floats((rows, middle)),
            floats((4, rows, 128)),
            floats((16, 128)),
        ],
        compiler_params=params(),
        cost_estimate=cost(2),
        name="join",
    )(one_code, two_code, far, own_bins, right, forward, backward)
    return pl.pallas_call(
        functools.partial(last_kernel, middle),
        in_specs=[in_vmem] * 4 + [in_hbm],
        out_specs=in_hbm,
        out_shape=jax.ShapeDtypeStruct((rows, width), jnp.bfloat16),
        input_output_aliases={4: 0},
        scratch_shapes=[
            shorts((rows, behind)),
            floats((16, 128)),
            pltpu.SemaphoreType.DMA((2,)),
        ],
        compiler_params=params(),
        cost_estimate=cost(1),
        name="last",
    )(last_code, last_base, last_right, ahead_mixed, mixed)


def turn_table(outer_ids, inner_ids, modulus):
    product_grid = outer_ids[:, None] * inner_ids[None, :] % modulus
    angles = product_grid.astype(jnp.float32) * (2.0 * math.pi / modulus)
    return (jnp.cos(angles), jnp.sin(angles))


def section_outer(table, data):
    return jnp.einsum(
        "ka,cab->ckb", table, data, precision=HIGHEST, preferred_element_type=jnp.float32
    )


def section_inner(table, data):
    return jnp.einsum(
        "ckb,bj->ckj", data, table, precision=HIGHEST, preferred_element_type=jnp.float32
    )


def padded_spectrum(signal, outer_count, inner_count, tables):
    cos_half, sin_half, cos_twist, sin_twist, cos_inner, sin_inner = tables
    shaped = signal.reshape(signal.shape[0], outer_count // 2, inner_count)
    real_one = section_outer(cos_half, shaped)
    imag_one = -section_outer(sin_half, shaped)
    real_two = real_one * cos_twist + imag_one * sin_twist
    imag_two = imag_one * cos_twist - real_one * sin_twist
    spec_real = section_inner(cos_inner, real_two) + section_inner(sin_inner, imag_two)
    spec_imag = section_inner(cos_inner, imag_two) - section_inner(sin_inner, real_two)
    return (spec_real, spec_imag)


def causal_local(driven_cols, normed_cols, total_len):
    full_len = 2 * total_len
    inner_count = math.gcd(total_len, 128)
    outer_count = full_len // inner_count
    outer_full = jnp.arange(outer_count, dtype=jnp.int32)
    outer_half = jnp.arange(outer_count // 2, dtype=jnp.int32)
    inner_ids = jnp.arange(inner_count, dtype=jnp.int32)
    cos_half, sin_half = turn_table(outer_full, outer_half, outer_count)
    cos_twist, sin_twist = turn_table(outer_full, inner_ids, full_len)
    cos_inner, sin_inner = turn_table(inner_ids, inner_ids, inner_count)
    tables = (cos_half, sin_half, cos_twist, sin_twist, cos_inner, sin_inner)
    sig_real, sig_imag = padded_spectrum(driven_cols, outer_count, inner_count, tables)
    fil_real, fil_imag = padded_spectrum(normed_cols, outer_count, inner_count, tables)
    prod_real = sig_real * fil_real - sig_imag * fil_imag
    prod_imag = sig_real * fil_imag + sig_imag * fil_real
    back_real = section_inner(cos_inner, prod_real) - section_inner(sin_inner, prod_imag)
    back_imag = section_inner(sin_inner, prod_real) + section_inner(cos_inner, prod_imag)
    turned_real = back_real * cos_twist - back_imag * sin_twist
    turned_imag = back_real * sin_twist + back_imag * cos_twist
    cos_last, sin_last = turn_table(outer_half, outer_full, outer_count)
    result = (
        section_outer(cos_last, turned_real) - section_outer(sin_last, turned_imag)
    ) / full_len
    return result.reshape(driven_cols.shape[0], total_len)


def exchanged(
    projected, short_weight, pos_in, pos_bias, sine_freq, pos_mid, pos_out, decay_rate, skip_gain
):
    ctx_count = lax.axis_size("ctx")
    ctx_place = lax.axis_index("ctx")
    block_rows = projected.shape[1]
    total_len = block_rows * ctx_count
    rim_rows = shifted(projected[:, block_rows - (TAPS - 1) :, :], "ctx", 1)
    extended = jnp.concatenate([rim_rows, projected], axis=1)
    short_out = jnp.zeros(projected.shape, jnp.float32)
    for tap_index in range(TAPS):
        offset = TAPS - 1 - tap_index
        short_out = short_out + short_weight[tap_index][:, None, :] * extended[
            :, offset : offset + block_rows, :
        ].astype(jnp.float32)
    left_gate, right_gate, value_stream = (short_out[0], short_out[1], short_out[2])
    driven = left_gate * value_stream
    own_width = driven.shape[1] // ctx_count
    driven_cols = lax.all_to_all(driven.T, "ctx", split_axis=0, concat_axis=1, tiled=True)
    own_out = lax.dynamic_slice_in_dim(pos_out, ctx_place * own_width, own_width, 1)
    own_decay = lax.dynamic_slice_in_dim(decay_rate, ctx_place * own_width, own_width, 0)
    positions = jnp.arange(total_len, dtype=jnp.int32).astype(jnp.float32)
    long_filter = filter_rows(
        positions, total_len, pos_in, pos_bias, sine_freq, pos_mid, own_out, own_decay
    )
    normed = long_filter / jnp.sqrt(jnp.sum(long_filter * long_filter, axis=0) + 1e-05)
    conv_cols = causal_local(driven_cols, normed.T, total_len)
    long_conv = lax.all_to_all(conv_cols, "ctx", split_axis=1, concat_axis=0, tiled=True).T
    return (right_gate * (long_conv + skip_gain[None, :] * driven)).astype(jnp.bfloat16)


def body(projected, *others):
    _, rows, width = projected.shape
    laid_out = rows % 32 == 0 and 64 <= rows <= 128 and width == 2048
    if lax.axis_size("ctx") == 2 and laid_out:
        return one_way(projected, *others)
    return exchanged(projected, *others)


def solution(mesh):
    placed = (
        P(None, ("dp", "ctx"), "chan"),
        P(None, None, "chan"),
        P(),
        P(),
        P(),
        P(),
        P(None, "chan"),
        P("chan"),
        P("chan"),
    )
    return jax.shard_map(
        body, mesh=mesh, in_specs=placed, out_specs=P(("dp", "ctx"), "chan"), check_vma=False
    )
```

```python
import functools
import math

import jax
import jax.numpy as jnp
import numpy as np
from jax import lax
from jax.experimental import pallas as pl
from jax.experimental.pallas import tpu as pltpu
from jax.sharding import PartitionSpec as P

BANDS = 16
TAPS = 7
SPAN = 250.0
TINY = 1e-30

HIGHEST = lax.Precision.HIGHEST


def shifted(x, axis, by):
    size = lax.axis_size(axis)
    pairs = [(i, i + by) for i in range(size) if 0 <= i + by < size]
    return lax.ppermute(x, axis, pairs)


def features(positions, total_len):
    band_ids = jnp.arange(1, BANDS + 1, dtype=jnp.float32)
    angles = positions[:, None] * band_ids[None, :] * (2.0 * math.pi / total_len)
    return jnp.concatenate(
        [positions[:, None] / total_len, jnp.cos(angles), jnp.sin(angles)], axis=1
    )


def second_rows(positions, total_len, pos_in, pos_bias, sine_freq, pos_mid):
    inputs = features(positions, total_len)
    first_layer = jnp.sin(
        sine_freq
        * (
            jnp.dot(inputs, pos_in, precision=HIGHEST, preferred_element_type=jnp.float32)
            + pos_bias
        )
    )
    return jnp.sin(
        sine_freq
        * jnp.dot(first_layer, pos_mid, precision=HIGHEST, preferred_element_type=jnp.float32)
    )


def filter_rows(positions, total_len, pos_in, pos_bias, sine_freq, pos_mid, pos_out, decay_rate):
    second_layer = second_rows(positions, total_len, pos_in, pos_bias, sine_freq, pos_mid)
    raw_filter = jnp.dot(
        second_layer, pos_out, precision=HIGHEST, preferred_element_type=jnp.float32
    )
    return raw_filter * jnp.exp(-decay_rate[None, :] * positions[:, None])


def halves(x):
    high = x.astype(jnp.bfloat16)
    low = (x - high.astype(jnp.float32)).astype(jnp.bfloat16)
    return high, low


def feature_table(places, total_len):
    bands = np.arange(1, BANDS + 1, dtype=np.float32)
    angles = places[:, None] * bands[None, :] * np.float32(2.0 * math.pi / total_len)
    first = places[:, None] / np.float32(total_len)
    table = np.concatenate([first, np.cos(angles), np.sin(angles), np.ones_like(first)], axis=1)
    spare = np.zeros((places.shape[0], -table.shape[1] % 8))
    return np.concatenate([table, spare], axis=1).astype(np.float32).T.copy()


def parity_order(rows):
    place = np.arange(rows)
    parity, inner = place // (rows // 2), place % (rows // 2)
    return rows // 8 * (inner % 8) + inner // 8 * 2 + parity


def table_columns(table):
    high = table.astype(jnp.bfloat16)
    low = (table - high.astype(np.float32)).astype(jnp.bfloat16)
    return np.concatenate([high, high, low], axis=1)


def odd_tables(rows):
    half = rows // 2
    order = np.concatenate([np.arange(0, half, 2), np.arange(1, half, 2)])
    turns = (2 * order[:, None] + 1) * parity_order(rows)[None, :] % (4 * rows)
    angles = turns * (np.pi / (2 * rows))
    forward = np.concatenate([np.cos(angles), -np.sin(angles)], axis=0).astype(np.float32)
    pieces = [forward[:, :half], forward[:, half:]]
    return (
        np.concatenate([table_columns(piece) for piece in pieces], axis=0),
        np.concatenate([table_columns(piece.T / np.float32(rows)) for piece in pieces], axis=0),
    )


def each_tile(tiles, unroll, action):
    count = math.gcd(tiles, unroll)

    def step(at, _):
        for number in range(count):
            action(at * count + number, number)
        return 0

    if tiles == count:
        step(0, 0)
    else:
        lax.fori_loop(0, tiles // count, step, 0)


def put_halves(ref, parity, row, cols, value):
    size = ref.shape[1] // 2
    high, low = halves(value)
    count = value.shape[0]
    ref[parity, row : row + count, cols] = high
    ref[parity, size + row : size + row + count, cols] = low


def three_pass(table, ref, parity):
    size = ref.shape[1] // 2
    both = jnp.concatenate([ref[parity], ref[parity, :size]], axis=0)
    return jnp.dot(table, both, preferred_element_type=jnp.float32)


def forward_dots(forward_ref, parts_ref, spec_ref):
    rows = spec_ref.shape[1]
    for parity in range(2):
        spec_ref[parity] = three_pass(forward_ref[parity * rows : (parity + 1) * rows], parts_ref, parity)


def backward_dots(backward_ref, bins_ref, conv_ref):
    half = conv_ref.shape[0] // 2
    for parity in range(2):
        rows = slice(parity * half, (parity + 1) * half)
        conv_ref[rows] = three_pass(backward_ref[rows], bins_ref, parity)


def unfolded(spec_ref, row, cols):
    half = spec_ref.shape[1] // 2
    even_cos, odd_cos = spec_ref[0, row : row + 16, cols], spec_ref[1, row : row + 16, cols]
    sine = slice(half + row, half + row + 16)
    even_sin, odd_sin = spec_ref[0, sine, cols], spec_ref[1, sine, cols]
    return even_cos + odd_cos, even_sin + odd_sin, even_cos - odd_cos, odd_sin - even_sin


def folded_products(spec_ref, filter_ref, row, cols, filter_cols):
    half = spec_ref.shape[1] // 2
    real, imag, real_far, imag_far = unfolded(spec_ref, row, cols)
    taps = [filter_ref[at * half + row : at * half + row + 16, filter_cols] for at in range(4)]
    out_real, out_imag = real * taps[0] - imag * taps[1], real * taps[1] + imag * taps[0]
    far_real = real_far * taps[2] - imag_far * taps[3]
    far_imag = real_far * taps[3] + imag_far * taps[2]
    return out_real + far_real, out_imag - far_imag, out_real - far_real, out_imag + far_imag


def put_bins(bins_ref, row, cols, products):
    half = bins_ref.shape[1] // 4
    for at, value in enumerate(products):
        put_halves(bins_ref, at // 2, at % 2 * half + row, cols, value)


def filtered(spec_ref, filter_ref, bins_ref, cols, filter_cols):
    for row in range(0, spec_ref.shape[1] // 2, 16):
        put_bins(bins_ref, row, cols, folded_products(spec_ref, filter_ref, row, cols, filter_cols))


def strided_rows(values, buf):
    buf[...] = values.astype(jnp.float32)
    count = buf.shape[0] // 8
    return [buf[pl.ds(v, 8, stride=count), :] for v in range(count)]


def short_sum(parts, rim, taps_ref, at, cols):
    top = lax.broadcasted_iota(jnp.int32, (8, 128), 0) == 0
    before = {}
    for back in range(1, TAPS):
        edge = 0.0 if rim is None else rim[8 - back : 9 - back]
        before[-back] = jnp.where(top, edge, pltpu.roll(parts[-back], 1, 0))
    taps = [jnp.broadcast_to(taps_ref[at, k : k + 1, cols], (8, 128)) for k in range(TAPS)]
    sums = []
    for v in range(len(parts)):
        terms = [taps[k] * (parts[v - k] if v >= k else before[v - k]) for k in range(TAPS)]
        sums.append(((terms[0] + terms[1]) + (terms[2] + terms[3])) + ((terms[4] + terms[5]) + terms[6]))
    return sums


def parity_rows(parts):
    ordered = parts[0::2] + parts[1::2]
    return [jnp.concatenate(ordered[i : i + 2], axis=0) for i in range(0, len(ordered), 2)]


def natural_rows(ref_rows, buf):
    count = buf.shape[0] // 8
    for at, value in enumerate(ref_rows):
        for piece in range(2):
            number = 2 * at + piece
            v = number % (count // 2) * 2 + number // (count // 2)
            buf[pl.ds(v, 8, stride=count), :] = value[8 * piece : 8 * piece + 8]
    return buf[...]


def tile_lanes(tile, first=0):
    return pl.ds(pl.multiple_of(first + tile * 128, 128), 128)


def tile_rows(tile, row, count=16):
    return pl.ds(pl.multiple_of(tile * 128 + row, 16), count)


def natural_tile(ref, cols, buf):
    return natural_rows([ref[at : at + 16, cols] for at in range(0, ref.shape[0], 16)], buf)


def place_level(peak, tile, peak_buf, levels_buf, levels_first):
    for step in (1, 2, 4):
        peak = jnp.maximum(peak, pltpu.roll(peak, step, 0))
    level = jnp.maximum(peak, TINY)
    wide = level * 65537.0
    level = wide - (wide - level)
    peak_buf[:, tile_lanes(tile)] = SPAN / level
    levels_buf[pl.ds(levels_first + tile, 1), :] = level[0:1]


def put_coded(coded_ref, tile, row, value, gain):
    coded = jnp.exp2(jnp.abs(value) * gain - SPAN / 2)
    coded_ref[tile_rows(tile, row), :] = jnp.where(value < 0, -coded, coded).astype(jnp.bfloat16)


def decoder(levels_buf, tile):
    level = levels_buf[pl.ds(tile, 1), :]
    slope = jnp.broadcast_to(level * (1.0 / (math.log(2.0) * SPAN)), (16, 128))
    middle = jnp.broadcast_to(level / 2, (16, 128))

    def decode(coded):
        coded = coded.astype(jnp.float32)
        size = jnp.log(jnp.abs(coded)) * slope + middle
        return jnp.where(coded < 0, -size, size)

    return decode


def second_layer(feats_ref, in_ref, bias_ref, freq_ref, mid_ref, scaled_buf):
    dot = functools.partial(
        lax.dot_general,
        dimension_numbers=(((0,), (0,)), ((), ())),
        precision=HIGHEST,
        preferred_element_type=jnp.float32,
    )
    count = in_ref.shape[0]
    freq = freq_ref[...]
    scaled_buf[...] = jnp.zeros_like(scaled_buf)
    scaled_buf[0:count] = in_ref[...] * freq
    scaled_buf[count : count + 1] = bias_ref[...] * freq
    layer = jnp.sin(dot(scaled_buf[...], feats_ref[...]))
    return jnp.sin(dot(mid_ref[...] * freq, layer)).T


def encode_tiles(
    tiles, rows, streams, taps_ref, taps_first, coded_ref, driven_ref, strided_buf, peak_buf, levels_buf, levels_first=0
):
    def drive(tile, number):
        cols = tile_lanes(tile)
        sums = [
            short_sum(
                strided_rows(streams(way, tile), strided_buf.at[number, way]),
                None, taps_ref, 2 * way, tile_lanes(tile, taps_first),
            )
            for way in range(2)
        ]
        driven = [one * two for one, two in zip(*sums)]
        for row, value in enumerate(parity_rows(driven)):
            driven_ref[16 * row : 16 * row + 16, cols] = value
        peak_buf[:, cols] = functools.reduce(jnp.maximum, [jnp.abs(value) for value in driven])

    each_tile(tiles, strided_buf.shape[0], drive)
    code_tiles(tiles, rows, coded_ref, driven_ref, peak_buf, levels_buf, levels_first)


def code_tiles(tiles, rows, coded_ref, values_ref, peak_buf, levels_buf, levels_first=0):
    each_tile(
        tiles, 4,
        lambda tile, _: place_level(peak_buf[:, tile_lanes(tile)], tile, peak_buf, levels_buf, levels_first),
    )
    if levels_first == 0:
        coded_ref[tiles * rows : tiles * rows + 16] = levels_buf[...].astype(jnp.bfloat16)

    def code(tile, _):
        cols = tile_lanes(tile)
        gain = peak_buf[:, cols]
        gain = jnp.concatenate([gain, gain], axis=0)
        for row in range(0, rows, 16):
            put_coded(coded_ref, tile, row, values_ref[row : row + 16, cols], gain)

    each_tile(tiles, 4, code)


def first_kernel(
    projected_ref, taps_ref, coded_ref, driven_ref, levels_ref, rows_buf, rim_buf, taps_buf, strided_buf, peak_buf, sems
):
    rows, size = rows_buf.shape[1:]
    tiles = size // 128

    @pl.when(lax.axis_index("ctx") == 0)
    def _():
        span = pl.ds(0, size)
        copies = [
            pltpu.make_async_copy(taps_ref.at[:, :, span], taps_buf, sems.at[0]),
            pltpu.make_async_copy(projected_ref.at[0, :, span], rows_buf.at[0], sems.at[1]),
            pltpu.make_async_copy(projected_ref.at[2, :, span], rows_buf.at[1], sems.at[2]),
            pltpu.make_async_copy(projected_ref.at[:, pl.ds(rows - 16, 16)], rim_buf, sems.at[3]),
        ]
        for copy in copies:
            copy.start()
        for copy in copies[:3]:
            copy.wait()
        levels_ref[...] = jnp.zeros_like(levels_ref)
        encode_tiles(
            tiles, rows, lambda way, tile: rows_buf[way, :, tile_lanes(tile)], taps_buf, 0, coded_ref, driven_ref,
            strided_buf, peak_buf, levels_ref, 16 - tiles,
        )
        copies[3].wait()
        for at in range(3):
            for group in range(rim_buf.shape[2] // 1024):
                there = tiles * rows + (3 * group + at) * 48
                values = [
                    rim_buf[at, :, (8 * group + way) * 128 : (8 * group + way + 1) * 128].astype(jnp.float32)[8:]
                    for way in range(8)
                ]
                values = pack_rims(values)
                for pair in range(3):
                    both = jnp.concatenate(values[2 * pair : 2 * pair + 2], axis=0)
                    coded_ref[there + 16 * pair : there + 16 * pair + 16] = both.astype(jnp.bfloat16)


def pack_rims(values):
    top = lax.broadcasted_iota(jnp.int32, (8, 128), 0) < 2
    return [
        jnp.where(top, pltpu.roll(values[6 + at // 3], 6 - 2 * (at % 3), 0), values[at]) for at in range(6)
    ]


def unpack_rims(values):
    place = lax.broadcasted_iota(jnp.int32, (8, 128), 0)
    rest = []
    for at in range(2):
        turned = [pltpu.roll(values[3 * at + way], 2 + 2 * way, 0) for way in range(3)]
        rest.append(jnp.where(place < 4, turned[0], jnp.where(place < 6, turned[1], turned[2])))
    return values + rest


def read_rims(coded_ref, rims_buf):
    groups = rims_buf.shape[2] // 1024
    start = coded_ref.shape[0] - groups * 144
    for at in range(3):
        for group in range(groups):
            there = start + (3 * group + at) * 48
            packed = coded_ref[there : there + 48].astype(jnp.float32)
            values = unpack_rims([packed[8 * way : 8 * way + 8] for way in range(6)])
            for way, value in enumerate(values):
                rims_buf[at, :, (8 * group + way) * 128 : (8 * group + way + 1) * 128] = value


def encode_kernel(
    first, projected_ref, taps_ref, one_levels_ref, coded_ref, driven_ref, strided_buf, peak_buf, levels_buf
):
    rows, size = driven_ref.shape

    @pl.when(lax.axis_index("ctx") == 0)
    def _():
        levels_buf[...] = one_levels_ref[...]
        encode_tiles(
            size // 128, rows, lambda way, tile: projected_ref[2 * way, :, tile_lanes(tile, first)], taps_ref, first,
            coded_ref, driven_ref, strided_buf, peak_buf, levels_buf,
        )


def network_halves(layer_refs, halves_ref, scaled_buf):
    second_high, second_low = halves(second_layer(*layer_refs, scaled_buf))
    halves_ref[...] = jnp.concatenate([second_high, second_high, second_low], axis=1)


def network_filter_kernel(first, *refs):
    weight_refs, layer_refs, (near_ref, far_ref, halves_ref), bufs = refs[:5], refs[5:10], refs[10:13], refs[13:]
    network_halves(layer_refs, halves_ref, bufs[-1])
    filter_spectra(first, *weight_refs, halves_ref, near_ref, far_ref, *bufs[:-1])


def filter_spectra(
    first, out_ref, decay_ref, skip_ref, places_ref, forward_ref, halves_ref, near_ref, far_ref,
    raw_buf, parts_buf, spec_buf, scale_buf,
):
    rows, width = near_ref.shape[0] // 2, near_ref.shape[1]
    half = rows // 2
    out_high, out_low = halves(out_ref[:, first : first + width])
    raw_buf[...] = jnp.dot(
        halves_ref[...], jnp.concatenate([out_high, out_low, out_high], axis=0), preferred_element_type=jnp.float32
    )

    def decay(tile, _):
        cols = tile_lanes(tile)
        fall = -decay_ref[:, tile_lanes(tile, first)]
        total = jnp.zeros((8, 128), jnp.float32)
        for row in range(0, 2 * rows, 16):
            taps = raw_buf[row : row + 16, cols] * jnp.exp(fall * places_ref[row : row + 16])
            total = total + (taps[:8] * taps[:8] + taps[8:] * taps[8:])
            parity = row % rows // half
            put_halves(parts_buf, parity, row % half, tile_lanes(tile, row // rows * width), taps)
        for step in (1, 2, 4):
            total = total + pltpu.roll(total, step, 0)
        scale_buf[:, cols] = 1.0 / jnp.sqrt(total + 1e-05)

    each_tile(width // 128, 12, decay)
    forward_dots(forward_ref, parts_buf, spec_buf)

    def shape(tile, _):
        cols = tile_lanes(tile)
        scale = scale_buf[:, cols]
        scale = jnp.concatenate([scale, scale], axis=0)
        skip = skip_ref[:, tile_lanes(tile, first)]
        for row in range(0, half, 16):
            low = [value * scale for value in unfolded(spec_buf, row, cols)]
            high = [value * scale for value in unfolded(spec_buf, row, tile_lanes(tile, width))]
            sign = 1 if row < half // 2 else -1
            turned = [-sign * low[1], sign * low[0], sign * low[3], -sign * low[2]]
            low = [low[0] + skip, low[1], low[2] + skip, low[3]]
            for at in range(4):
                near_ref[at * half + row : at * half + row + 16, cols] = low[at]
                far_ref[at * half + row : at * half + row + 16, cols] = high[at] + turned[at]

    each_tile(width // 128, 12, shape)


def driven_parts(driven, parts_buf, cols):
    half = parts_buf.shape[1] // 2
    for at, value in enumerate(parity_rows(driven)):
        put_halves(parts_buf, 16 * at // half, 16 * at % half, cols, value)


def put_rows(ref, cols, values):
    for at, value in enumerate(parity_rows(values)):
        ref[16 * at : 16 * at + 16, cols] = value


def send_kernel(
    first, projected_ref, taps_ref, near_ref, far_ref, forward_ref, backward_ref, one_ref, two_ref,
    coded_ref, mixed_ref, gates_ref, ahead_spec_ref,
    strided_buf, parts_buf, spec_buf, bins_buf, right_buf, conv_buf, peak_buf, levels_buf, ahead_parts_buf,
):
    rows, width = right_buf.shape
    half = rows // 2
    tiles = width // 128

    @pl.when(lax.axis_index("ctx") == 0)
    def _():
        def drive(tile, number):
            cols = tile_lanes(tile, first)
            sums = [
                short_sum(
                    strided_rows(projected_ref[at, :, cols], strided_buf.at[number, at]), None, taps_ref, at, cols
                )
                for at in range(3)
            ]
            put_rows(right_buf, tile_lanes(tile), sums[1])
            driven_parts([one * two for one, two in zip(sums[0], sums[2])], parts_buf, tile_lanes(tile))

        each_tile(tiles, strided_buf.shape[0], drive)
        forward_dots(forward_ref, parts_buf, spec_buf)
        each_tile(
            tiles, 4, lambda tile, _: filtered(spec_buf, far_ref, bins_buf, tile_lanes(tile), tile_lanes(tile))
        )
        backward_dots(backward_ref, bins_buf, conv_buf)

        def peaks(tile, number):
            cols = tile_lanes(tile)
            conv_buf[:, cols] = natural_tile(conv_buf, cols, strided_buf.at[number, 0])
            peak_buf[:, cols] = functools.reduce(
                jnp.maximum, [jnp.abs(conv_buf[row : row + 8, cols]) for row in range(0, rows, 8)]
            )

        each_tile(tiles, strided_buf.shape[0], peaks)
        code_tiles(tiles, rows, coded_ref, conv_buf, peak_buf, levels_buf)
        each_tile(
            tiles, 4, lambda tile, _: filtered(spec_buf, near_ref, bins_buf, tile_lanes(tile), tile_lanes(tile))
        )
        backward_dots(backward_ref, bins_buf, conv_buf)

        def mix(tile):
            cols = tile_lanes(tile)
            return [right_buf[at : at + 16, cols] * conv_buf[at : at + 16, cols] for at in range(0, rows, 16)]

        def gate(tile, number):
            cols = tile_lanes(tile)
            parts = strided_rows(projected_ref[1, :, cols], strided_buf.at[number, 1])
            put_rows(gates_ref, cols, short_sum(parts, None, taps_ref, 1, cols))

        each_tile(first // 128, strided_buf.shape[0], gate)
        start = 0
        for ref in (one_ref, two_ref):

            def recall(tile, _, ref=ref, start=start):
                for row in range(0, rows, 16):
                    value = ref[row : row + 16, tile_lanes(tile)]
                    put_halves(ahead_parts_buf, row // half, row % half, tile_lanes(tile, start), value)

            each_tile(ref.shape[1] // 128, 4, recall)
            start += ref.shape[1]
        forward_dots(forward_ref, ahead_parts_buf, ahead_spec_ref)
        mix_tiles(mix, tiles, mixed_ref, strided_buf.at[:, 0])


def own_kernel(
    projected_ref, rims_ref, taps_ref, near_ref, last_near_ref, forward_ref, backward_ref, gates_ref, ahead_spec_ref,
    behind_ref, right_ref, bins_ref, base_ref, last_right_ref, mixed_ref,
    rims_buf, strided_buf, parts_buf, spec_buf, bins_buf, conv_buf, mixed_buf, ahead_bins_buf, sems,
):
    rows, width = right_ref.shape
    half = rows // 2
    middle = near_ref.shape[1]
    place = lax.axis_index("ctx")

    @pl.when(place == 0)
    def _():
        tiles = middle // 128
        behind = pltpu.make_async_copy(behind_ref, mixed_ref.at[:, pl.ds(middle, width - middle)], sems.at[0])
        behind.start()
        each_tile(
            tiles, 4,
            lambda tile, _: filtered(ahead_spec_ref, near_ref, ahead_bins_buf, tile_lanes(tile), tile_lanes(tile)),
        )
        backward_dots(backward_ref, ahead_bins_buf, conv_buf)

        def mix(tile):
            cols = tile_lanes(tile)
            return [gates_ref[at : at + 16, cols] * conv_buf[at : at + 16, cols] for at in range(0, rows, 16)]

        mix_tiles(mix, tiles, mixed_buf, strided_buf.at[:, 0])
        ahead = pltpu.make_async_copy(mixed_buf, mixed_ref.at[:, pl.ds(0, middle)], sems.at[1])
        ahead.start()
        ahead.wait()
        behind.wait()

    @pl.when(place != 0)
    def _():
        read_rims(rims_ref, rims_buf)

        def drive(tile, number):
            cols = tile_lanes(tile)
            sums = [
                short_sum(
                    strided_rows(projected_ref[at, :, cols], strided_buf.at[number, at]),
                    rims_buf[at, :, cols], taps_ref, at, cols,
                )
                for at in range(3)
            ]
            put_rows(right_ref, cols, sums[1])
            driven_parts([one * two for one, two in zip(sums[0], sums[2])], parts_buf, cols)

        each_tile(width // 128, strided_buf.shape[0], drive)
        forward_dots(forward_ref, parts_buf, spec_buf)

        def keep(tile, _):
            cols = tile_lanes(tile)
            for row in range(0, half, 16):
                for at, value in enumerate(folded_products(spec_buf, near_ref, row, cols, cols)):
                    bins_ref[at * half + row : at * half + row + 16, cols] = value

        each_tile(middle // 128, 12, keep)
        behind = width - middle

        def finish(tile, _):
            there, cols = tile_lanes(tile, middle), tile_lanes(tile)
            for row in range(0, half, 16):
                put_bins(bins_buf, row, cols, folded_products(spec_buf, last_near_ref, row, there, cols))

        each_tile(behind // 128, 4, finish)
        backward_dots(backward_ref, bins_buf, base_ref)

        def reorder(tile, number):
            cols = tile_lanes(tile)
            base_ref[:, cols] = natural_tile(base_ref, cols, strided_buf.at[number, 0])
            last_right_ref[:, cols] = natural_tile(right_ref, tile_lanes(tile, middle), strided_buf.at[number, 1])

        each_tile(behind // 128, strided_buf.shape[0], reorder)


def mix_tiles(mix, tiles, mixed_ref, strided_buf):
    def one(tile, number):
        mixed_ref[:, tile_lanes(tile)] = natural_rows(mix(tile), strided_buf.at[number]).astype(jnp.bfloat16)

    each_tile(tiles, strided_buf.shape[0], one)


def read_levels(coded_ref, levels_buf, tiles, rows):
    levels_buf[...] = coded_ref[tiles * rows : tiles * rows + 16].astype(jnp.float32)


def join_kernel(
    coded_refs, far_ref, own_bins_ref, right_ref, forward_ref, backward_ref, mixed_ref,
    parts_buf, spec_buf, bins_buf, conv_buf, strided_buf, levels_buf,
):
    rows, width = conv_buf.shape
    half = rows // 2
    tiles = width // 128

    @pl.when(lax.axis_index("ctx") != 0)
    def _():
        counts = [coded_refs[0].shape[0] // rows, coded_refs[1].shape[0] // rows]
        counts[0] = tiles - counts[1]
        read_levels(coded_refs[1], levels_buf, counts[1], rows)
        for at, ref in enumerate(coded_refs):
            start = counts[0] * 128 * at
            levels_first = 0 if at else 16 - counts[0]

            def spread_out(tile, _, ref=ref, start=start, levels_first=levels_first):
                decode = decoder(levels_buf, levels_first + tile)
                for row in range(0, rows, 16):
                    value = decode(ref[tile_rows(tile, row), :])
                    put_halves(parts_buf, row // half, row % half, tile_lanes(tile, start), value)

            each_tile(counts[at], 4, spread_out)
        forward_dots(forward_ref, parts_buf, spec_buf)

        def add(tile, _):
            cols = tile_lanes(tile)
            for row in range(0, half, 16):
                products = [
                    value + own_bins_ref[at * half + row : at * half + row + 16, cols]
                    for at, value in enumerate(folded_products(spec_buf, far_ref, row, cols, cols))
                ]
                put_bins(bins_buf, row, cols, products)

        each_tile(tiles, 12, add)
        backward_dots(backward_ref, bins_buf, conv_buf)

        def mix(tile):
            cols = tile_lanes(tile)
            return [right_ref[at : at + 16, cols] * conv_buf[at : at + 16, cols] for at in range(0, rows, 16)]

        mix_tiles(mix, tiles, mixed_ref, strided_buf)


def last_kernel(
    first, coded_ref, base_ref, right_ref, ahead_ref, _, mixed_ref, buf, levels_buf, sems
):
    rows, width = base_ref.shape
    tiles = width // 128

    @pl.when(lax.axis_index("ctx") != 0)
    def _():
        ahead = pltpu.make_async_copy(ahead_ref, mixed_ref.at[:, pl.ds(0, first)], sems.at[0])
        ahead.start()
        read_levels(coded_ref, levels_buf, tiles, rows)

        def mix(tile, _):
            cols = tile_lanes(tile)
            decode = decoder(levels_buf, tile)
            for at in range(0, rows, 16):
                conv = decode(coded_ref[tile_rows(tile, at), :]) + base_ref[at : at + 16, cols]
                buf[at : at + 16, cols] = (right_ref[at : at + 16, cols] * conv).astype(jnp.bfloat16)

        each_tile(tiles, 4, mix)
        behind = pltpu.make_async_copy(buf, mixed_ref.at[:, pl.ds(first, width)], sems.at[1])
        behind.start()
        behind.wait()
        ahead.wait()


def params(mib=40):
    return pltpu.CompilerParams(vmem_limit_bytes=mib * 1024 * 1024)


def cost(us):
    return pl.CostEstimate(flops=int(us * 1e9), bytes_accessed=int(us * 3e6), transcendentals=0)


def one_way(
    projected, short_weight, pos_in, pos_bias, sine_freq, pos_mid, pos_out, decay_rate, skip_gain
):
    _, rows, width = projected.shape
    half = rows // 2
    total_len = 2 * rows
    ahead = [width // 8, width * 5 // 8]
    middle = sum(ahead)
    behind = width - middle
    forward, backward = odd_tables(rows)
    taps = jnp.transpose(short_weight, (1, 0, 2))
    in_vmem = pl.BlockSpec(memory_space=pltpu.VMEM)
    in_hbm = pl.BlockSpec(memory_space=pltpu.HBM)
    floats, shorts = functools.partial(pltpu.VMEM, dtype=jnp.float32), functools.partial(pltpu.VMEM, dtype=jnp.bfloat16)
    pairs = [(0, 1)]

    def arrays(*shapes, dtype=jnp.float32):
        return [jax.ShapeDtypeStruct(shape, dtype) for shape in shapes]

    def message(size, more=0):
        return arrays((size // 128 * rows + 16 + more, 128), dtype=jnp.bfloat16)

    order = parity_order(rows)
    places = np.concatenate([order, order + rows]).astype(np.float32)
    feats = feature_table(places, total_len)
    places = np.repeat(places[:, None], 128, 1)
    layers = (feats, pos_in, pos_bias[None, :], sine_freq[None, :], pos_mid)
    tile_bufs = [floats((2, 2, rows, 128)), floats((8, width)), floats((16, 128))]
    one, two = ahead
    one_code, one_driven, one_levels = pl.pallas_call(
        first_kernel,
        in_specs=[in_hbm] * 2,
        out_specs=[in_vmem] * 3,
        out_shape=arrays((one // 128 * rows + width // 128 * 18, 128), dtype=jnp.bfloat16)
        + arrays((rows, one), (16, 128)),
        scratch_shapes=[shorts((2, rows, one)), shorts((3, 16, width)), floats((3, TAPS, one))]
        + tile_bufs[:2]
        + [pltpu.SemaphoreType.DMA((4,))],
        compiler_params=params(),
        cost_estimate=cost(1),
        name="first",
    )(*[pltpu.with_memory_space_constraint(array, pltpu.HBM) for array in (projected, taps)])
    one_code = lax.ppermute(one_code, "ctx", [(0, 1), (1, 0)])
    weights = (pos_out, decay_rate[None, :], skip_gain[None, :], places, forward)
    hidden = pos_mid.shape[1]

    def spectra_bufs(size):
        return [floats((total_len, size)), shorts((2, rows, 2 * size)), floats((2, rows, 2 * size)), floats((8, size))]

    spectra = arrays((total_len, behind), (total_len, behind)) + arrays((total_len, 3 * hidden), dtype=jnp.bfloat16)
    two_code, two_driven = pl.pallas_call(
        functools.partial(encode_kernel, one),
        in_specs=[in_vmem] * 3,
        out_specs=[in_vmem] * 2,
        out_shape=message(two) + arrays((rows, two)),
        scratch_shapes=tile_bufs,
        compiler_params=params(),
        cost_estimate=cost(1),
        name="encode",
    )(projected, taps, one_levels)
    two_code = lax.ppermute(two_code, "ctx", [(0, 1), (1, 0)])
    last_near, last_far, second_halves = pl.pallas_call(
        functools.partial(network_filter_kernel, middle),
        in_specs=[in_vmem] * 10,
        out_specs=[in_vmem] * 3,
        out_shape=spectra,
        scratch_shapes=spectra_bufs(behind) + [floats((feats.shape[0], hidden))],
        compiler_params=params(),
        cost_estimate=cost(2),
        name="filter",
    )(*weights, *layers)
    near, far = pl.pallas_call(
        functools.partial(filter_spectra, 0),
        in_specs=[in_vmem] * 6,
        out_specs=[in_vmem] * 2,
        out_shape=arrays((total_len, middle), (total_len, middle)),
        scratch_shapes=spectra_bufs(middle),
        compiler_params=params(),
        cost_estimate=cost(2),
        name="filter",
    )(*weights, second_halves)
    last_near, near = lax.optimization_barrier((last_near, near))
    last_code, behind_mixed, gates, ahead_spec = pl.pallas_call(
        functools.partial(send_kernel, middle),
        in_specs=[in_vmem] * 8,
        out_specs=[in_vmem] * 4,
        out_shape=message(behind)
        + arrays((rows, behind), dtype=jnp.bfloat16)
        + arrays((rows, middle), (2, rows, middle)),
        scratch_shapes=[
            floats((2, 3, rows, 128)),
            shorts((2, rows, behind)),
            floats((2, rows, behind)),
            shorts((2, 2 * rows, behind)),
            floats((rows, behind)),
            floats((rows, behind)),
            floats((8, behind)),
            floats((16, 128)),
            shorts((2, rows, middle)),
        ],
        compiler_params=params(),
        cost_estimate=cost(2),
        name="send",
    )(projected, taps, last_near, last_far, forward, backward, one_driven, two_driven)
    last_code = lax.ppermute(last_code, "ctx", pairs)
    right, own_bins, last_base, last_right, mixed = pl.pallas_call(
        own_kernel,
        in_specs=[in_vmem] * 10,
        out_specs=[in_vmem] * 4 + [in_hbm],
        out_shape=arrays((rows, width), (total_len, middle), (rows, behind), (rows, behind))
        + arrays((rows, width), dtype=jnp.bfloat16),
        scratch_shapes=[
            floats((3, 8, width)),
            floats((2, 3, rows, 128)),
            shorts((2, rows, width)),
            floats((2, rows, width)),
            shorts((2, 2 * rows, behind)),
            floats((rows, middle)),
            shorts((rows, middle)),
            shorts((2, 2 * rows, middle)),
            pltpu.SemaphoreType.DMA((2,)),
        ],
        compiler_params=params(),
        cost_estimate=cost(4),
        name="own",
    )(projected, one_code, taps, near, last_near, forward, backward, gates, ahead_spec, behind_mixed)
    ahead_mixed = pl.pallas_call(
        lambda one_ref, two_ref, *refs: join_kernel((one_ref, two_ref), *refs),
        in_specs=[in_vmem] * 7,
        out_specs=in_vmem,
        out_shape=jax.ShapeDtypeStruct((rows, middle), jnp.bfloat16),
        scratch_shapes=[
            shorts((2, rows, middle)),
            floats((2, rows, middle)),
            shorts((2, 2 * rows, middle)),
            floats((rows, middle)),
            floats((4, rows, 128)),
            floats((16, 128)),
        ],
        compiler_params=params(),
        cost_estimate=cost(2),
        name="join",
    )(one_code, two_code, far, own_bins, right, forward, backward)
    return pl.pallas_call(
        functools.partial(last_kernel, middle),
        in_specs=[in_vmem] * 4 + [in_hbm],
        out_specs=in_hbm,
        out_shape=jax.ShapeDtypeStruct((rows, width), jnp.bfloat16),
        input_output_aliases={4: 0},
        scratch_shapes=[
            shorts((rows, behind)),
            floats((16, 128)),
            pltpu.SemaphoreType.DMA((2,)),
        ],
        compiler_params=params(),
        cost_estimate=cost(1),
        name="last",
    )(last_code, last_base, last_right, ahead_mixed, mixed)


def turn_table(outer_ids, inner_ids, modulus):
    product_grid = outer_ids[:, None] * inner_ids[None, :] % modulus
    angles = product_grid.astype(jnp.float32) * (2.0 * math.pi / modulus)
    return (jnp.cos(angles), jnp.sin(angles))


def section_outer(table, data):
    return jnp.einsum(
        "ka,cab->ckb", table, data, precision=HIGHEST, preferred_element_type=jnp.float32
    )


def section_inner(table, data):
    return jnp.einsum(
        "ckb,bj->ckj", data, table, precision=HIGHEST, preferred_element_type=jnp.float32
    )


def padded_spectrum(signal, outer_count, inner_count, tables):
    cos_half, sin_half, cos_twist, sin_twist, cos_inner, sin_inner = tables
    shaped = signal.reshape(signal.shape[0], outer_count // 2, inner_count)
    real_one = section_outer(cos_half, shaped)
    imag_one = -section_outer(sin_half, shaped)
    real_two = real_one * cos_twist + imag_one * sin_twist
    imag_two = imag_one * cos_twist - real_one * sin_twist
    spec_real = section_inner(cos_inner, real_two) + section_inner(sin_inner, imag_two)
    spec_imag = section_inner(cos_inner, imag_two) - section_inner(sin_inner, real_two)
    return (spec_real, spec_imag)


def causal_local(driven_cols, normed_cols, total_len):
    full_len = 2 * total_len
    inner_count = math.gcd(total_len, 128)
    outer_count = full_len // inner_count
    outer_full = jnp.arange(outer_count, dtype=jnp.int32)
    outer_half = jnp.arange(outer_count // 2, dtype=jnp.int32)
    inner_ids = jnp.arange(inner_count, dtype=jnp.int32)
    cos_half, sin_half = turn_table(outer_full, outer_half, outer_count)
    cos_twist, sin_twist = turn_table(outer_full, inner_ids, full_len)
    cos_inner, sin_inner = turn_table(inner_ids, inner_ids, inner_count)
    tables = (cos_half, sin_half, cos_twist, sin_twist, cos_inner, sin_inner)
    sig_real, sig_imag = padded_spectrum(driven_cols, outer_count, inner_count, tables)
    fil_real, fil_imag = padded_spectrum(normed_cols, outer_count, inner_count, tables)
    prod_real = sig_real * fil_real - sig_imag * fil_imag
    prod_imag = sig_real * fil_imag + sig_imag * fil_real
    back_real = section_inner(cos_inner, prod_real) - section_inner(sin_inner, prod_imag)
    back_imag = section_inner(sin_inner, prod_real) + section_inner(cos_inner, prod_imag)
    turned_real = back_real * cos_twist - back_imag * sin_twist
    turned_imag = back_real * sin_twist + back_imag * cos_twist
    cos_last, sin_last = turn_table(outer_half, outer_full, outer_count)
    result = (
        section_outer(cos_last, turned_real) - section_outer(sin_last, turned_imag)
    ) / full_len
    return result.reshape(driven_cols.shape[0], total_len)


def exchanged(
    projected, short_weight, pos_in, pos_bias, sine_freq, pos_mid, pos_out, decay_rate, skip_gain
):
    ctx_count = lax.axis_size("ctx")
    ctx_place = lax.axis_index("ctx")
    block_rows = projected.shape[1]
    total_len = block_rows * ctx_count
    rim_rows = shifted(projected[:, block_rows - (TAPS - 1) :, :], "ctx", 1)
    extended = jnp.concatenate([rim_rows, projected], axis=1)
    short_out = jnp.zeros(projected.shape, jnp.float32)
    for tap_index in range(TAPS):
        offset = TAPS - 1 - tap_index
        short_out = short_out + short_weight[tap_index][:, None, :] * extended[
            :, offset : offset + block_rows, :
        ].astype(jnp.float32)
    left_gate, right_gate, value_stream = (short_out[0], short_out[1], short_out[2])
    driven = left_gate * value_stream
    own_width = driven.shape[1] // ctx_count
    driven_cols = lax.all_to_all(driven.T, "ctx", split_axis=0, concat_axis=1, tiled=True)
    own_out = lax.dynamic_slice_in_dim(pos_out, ctx_place * own_width, own_width, 1)
    own_decay = lax.dynamic_slice_in_dim(decay_rate, ctx_place * own_width, own_width, 0)
    positions = jnp.arange(total_len, dtype=jnp.int32).astype(jnp.float32)
    long_filter = filter_rows(
        positions, total_len, pos_in, pos_bias, sine_freq, pos_mid, own_out, own_decay
    )
    normed = long_filter / jnp.sqrt(jnp.sum(long_filter * long_filter, axis=0) + 1e-05)
    conv_cols = causal_local(driven_cols, normed.T, total_len)
    long_conv = lax.all_to_all(conv_cols, "ctx", split_axis=1, concat_axis=0, tiled=True).T
    return (right_gate * (long_conv + skip_gain[None, :] * driven)).astype(jnp.bfloat16)


def body(projected, *others):
    _, rows, width = projected.shape
    laid_out = rows % 32 == 0 and 64 <= rows <= 128 and width in (1024, 2048)
    if lax.axis_size("ctx") == 2 and laid_out:
        return one_way(projected, *others)
    return exchanged(projected, *others)


def solution(mesh):
    placed = (
        P(None, ("dp", "ctx"), "chan"),
        P(None, None, "chan"),
        P(),
        P(),
        P(),
        P(),
        P(None, "chan"),
        P("chan"),
        P("chan"),
    )
    return jax.shard_map(
        body, mesh=mesh, in_specs=placed, out_specs=P(("dp", "ctx"), "chan"), check_vma=False
    )
```
